512 devices in a mesh: region: 16 (over y, core), tile: 32 (over x, z).
Axes of the slice: x: 4, y: 8, z: 8, core: 2. Of those that a mesh axis runs over, the one named last changes fastest.
Arguments:
- tokens: bfloat16 [256, 512, 384], P('region', 'tile'), may hold values from -6 to 6
- grad_out: bfloat16 [256, 512, 384], P('region', 'tile'), may hold values from -6 to 6
- ocean_mask: int32 [32, 64], P('region', 'tile'), may hold values from 0 to 1, as said below
- w_qkv: bfloat16 [384, 1152], replicated, may hold values from -3 to 3
- w_out: bfloat16 [384, 384], replicated, may hold values from -0.3125 to 0.3125
Outputs:
- grad_tokens: bfloat16 [256, 512, 384], P('region', 'tile')
- grad_w_qkv: float32 [384, 1152], P('tile')
- grad_w_out: float32 [384, 384], P('tile')
The draws below stay inside these ranges and needn't reach their ends.
Inputs may be any that keep to these rules, and one draw needn't show every extreme that they name: `ocean_mask`: the windows of one tile column (one index of tile over all regions) hold exactly 48 ocean windows; how they split over the regions varies strongly from column to column.
All inputs are finite; a program needn't handle non-finite values.
Results may differ from the reference program's by a relative error of at most 0.029.
Values may be sent and summed in bfloat16 or wider, within the bound.
A program may use at most 64 MiB of HBM per device.

```python
import math
import jax
import jax.numpy as jnp
from jax import lax

D = 384
HEADS = 12
WT = 64
WR = 2
WC = 2
CAP = 3
WROWS = 32
WCOLS = 64
LAT = 256
LON = 512
N_REGION = 16
N_TILE = 32


def draw_ocean_mask(key, part):
    key = jax.random.fold_in(key, 11)
    key_bias, key_noise, key_order = jax.random.split(key, 3)
    total = N_REGION * WR * N_TILE * WC
    band_bias = jax.random.randint(key_bias, (N_REGION, 1, N_TILE, 1), 0, 4) * 4096
    noise = jax.random.randint(key_noise, (N_REGION, WR, N_TILE, WC), 0, 4096)
    order = jax.random.permutation(key_order, total).astype(jnp.int32).reshape(N_REGION, WR, N_TILE, WC)
    score = (band_bias + noise) * total + order
    column = jnp.transpose(score, (2, 0, 1, 3)).reshape(N_TILE, N_REGION * WR * WC)
    ranking = jnp.argsort(jnp.argsort(-column, axis=1), axis=1)
    chosen = (ranking < CAP * N_REGION).astype(jnp.int32)
    chosen = jnp.transpose(chosen.reshape(N_TILE, N_REGION, WR, WC), (1, 2, 0, 3))
    return chosen.reshape(N_REGION * WR, N_TILE * WC)


def draw_w_qkv(key, part):
    key = jax.random.fold_in(key, 5)
    key_base = jax.random.fold_in(key, 0)
    weights = jax.random.normal(key_base, (D, 3 * D), jnp.float32) / math.sqrt(D)
    return jnp.clip(weights, -3.0, 3.0).astype(jnp.bfloat16)


def level_of(own_key, dims, cuts, low, largest):
    level = 1.0
    for axis_at, blocks in cuts:
        draws = jax.random.uniform(jax.random.fold_in(jax.random.fold_in(own_key, 6), axis_at), (blocks,), jnp.float32, low / len(cuts), largest / len(cuts))
        level = level * jnp.repeat(jnp.exp(draws), dims[axis_at] // blocks).reshape((-1,) + (1,) * (len(dims) - 1 - axis_at))
    return level


def bell_draw(own_key, dims, width, reach, shards=(), dtype=jnp.bfloat16):
    array = width * jax.random.normal(own_key, dims, jnp.float32)
    if shards:
        array = array * level_of(own_key, dims, shards, -0.22, 0.18)
    return jnp.clip(array, -reach, reach).astype(dtype)


def setup_inputs(seed: int = 0) -> dict:
    streams_of = jax.random.split(jax.random.key(seed), 6)
    tokens = bell_draw(streams_of[0], (LAT, LON, D), 1.0, 6.0, ((0, 16), (1, 32)))
    grad_out = bell_draw(streams_of[1], (LAT, LON, D), 1.0, 6.0, ((0, 16), (1, 32)))
    ocean_mask = draw_ocean_mask(jax.random.fold_in(streams_of[5], 71), 0)
    w_qkv = draw_w_qkv(jax.random.fold_in(streams_of[5], 71), 0)
    w_out = bell_draw(streams_of[4], (D, D), D ** -0.5, 0.3125)
    return dict(tokens=tokens, grad_out=grad_out, ocean_mask=ocean_mask, w_qkv=w_qkv, w_out=w_out)


def to_windows(field, row_blocks, col_blocks):
    model_width = field.shape[-1]
    shaped = field.reshape(row_blocks, 8, col_blocks, 8, model_width)
    return jnp.transpose(shaped, (0, 2, 1, 3, 4)).reshape(row_blocks * col_blocks, 64, model_width)

def from_windows(windows, row_blocks, col_blocks):
    model_width = windows.shape[-1]
    shaped = windows.reshape(row_blocks, col_blocks, 8, 8, model_width)
    return jnp.transpose(shaped, (0, 2, 1, 3, 4)).reshape(row_blocks * 8, col_blocks * 8, model_width)

def layer_grads(windows_x, windows_dy, w_qkv, w_out):
    batch_size, window_len, model_width = windows_x.shape
    head_dim = model_width // HEADS
    inv_root = head_dim ** (-0.5)
    features = windows_x.astype(jnp.float32)
    center = lax.optimization_barrier(jnp.mean(features, axis=-1, keepdims=True))
    deviation = features - center
    inverse_std = lax.rsqrt(lax.optimization_barrier(jnp.mean(deviation * deviation, axis=-1, keepdims=True)) + 1e-05)
    x_hat = deviation * inverse_std
    normed = x_hat.astype(jnp.bfloat16)
    projected = jnp.einsum('btd,de->bte', normed.astype(jnp.float32), w_qkv.astype(jnp.float32)).astype(jnp.bfloat16)
    head_shape = (batch_size, window_len, HEADS, head_dim)
    query_heads = projected[..., :model_width].reshape(head_shape).astype(jnp.float32)
    key_heads = projected[..., model_width:2 * model_width].reshape(head_shape).astype(jnp.float32)
    value_heads = projected[..., 2 * model_width:].reshape(head_shape).astype(jnp.float32)
    scores = jnp.einsum('bqhd,bkhd->bhqk', query_heads, key_heads) * inv_root
    scores = scores - lax.optimization_barrier(jnp.max(scores, axis=-1, keepdims=True))
    expd = jnp.exp(scores)
    probs = expd / lax.optimization_barrier(jnp.sum(expd, axis=-1, keepdims=True))
    probs_b = probs.astype(jnp.bfloat16).astype(jnp.float32)
    attended = jnp.einsum('bhqk,bkhd->bqhd', probs_b, value_heads).reshape(batch_size, window_len, model_width).astype(jnp.bfloat16)
    dy_float = windows_dy.astype(jnp.float32)
    grad_att = jnp.einsum('bte,de->btd', dy_float, w_out.astype(jnp.float32)).astype(jnp.bfloat16)
    grad_out_w = jnp.einsum('btd,bte->de', attended.astype(jnp.float32), dy_float)
    grad_heads = grad_att.reshape(head_shape).astype(jnp.float32)
    grad_probs = jnp.einsum('bqhd,bkhd->bhqk', grad_heads, value_heads)
    row_terms = lax.optimization_barrier(jnp.sum(grad_probs * probs, axis=-1, keepdims=True))
    grad_scores = (probs * (grad_probs - row_terms) * inv_root).astype(jnp.bfloat16).astype(jnp.float32)
    d_query = jnp.einsum('bhqk,bkhd->bqhd', grad_scores, key_heads)
    d_key = jnp.einsum('bhqk,bqhd->bkhd', grad_scores, query_heads)
    d_value = jnp.einsum('bhqk,bqhd->bkhd', probs_b, grad_heads)
    flat_shape = (batch_size, window_len, model_width)
    grad_proj = jnp.concatenate([d_query.reshape(flat_shape), d_key.reshape(flat_shape), d_value.reshape(flat_shape)], axis=-1).astype(jnp.bfloat16)
    grad_qkv_w = jnp.einsum('btd,bte->de', normed.astype(jnp.float32), grad_proj.astype(jnp.float32))
    grad_normed = jnp.einsum('bte,de->btd', grad_proj.astype(jnp.float32), w_qkv.astype(jnp.float32))
    branch = inverse_std * (grad_normed - lax.optimization_barrier(jnp.mean(grad_normed, axis=-1, keepdims=True)) - x_hat * lax.optimization_barrier(jnp.mean(grad_normed * x_hat, axis=-1, keepdims=True)))
    return (branch.astype(jnp.bfloat16), grad_qkv_w, grad_out_w)

def reference(tokens, grad_out, ocean_mask, w_qkv, w_out):
    total_windows = WROWS * WCOLS
    block_count = total_windows // 64
    shifted_x = jnp.roll(tokens, -4, axis=1)
    shifted_dy = jnp.roll(grad_out, -4, axis=1)
    windows_x = to_windows(shifted_x, WROWS, WCOLS)
    windows_dy = to_windows(shifted_dy, WROWS, WCOLS)
    flags = ocean_mask.reshape(total_windows).astype(jnp.bfloat16)
    masked = windows_dy * flags[:, None, None]
    blocks_x = windows_x.reshape(block_count, 64, 64, D)
    blocks_dy = masked.reshape(block_count, 64, 64, D)

    def block_step(totals, pair):
        branch, grad_qkv_w, grad_out_w = layer_grads(pair[0], pair[1], w_qkv, w_out)
        return ((totals[0] + grad_qkv_w, totals[1] + grad_out_w), branch)
    start = (jnp.zeros((D, 3 * D), jnp.float32), jnp.zeros((D, D), jnp.float32))
    (sum_qkv, sum_out), branches = lax.scan(block_step, start, (blocks_x, blocks_dy))
    placed = from_windows(branches.reshape(total_windows, 64, D), WROWS, WCOLS)
    placed = jnp.roll(placed, 4, axis=1)
    grad_tokens = (grad_out.astype(jnp.float32) + placed.astype(jnp.float32)).astype(jnp.bfloat16)
    grad_scale = 1.0 / math.sqrt(CAP * WT * N_REGION * N_TILE)
    return (grad_tokens, sum_qkv * grad_scale, sum_out * grad_scale)
```

```python
import math

import jax
import jax.numpy as jnp
from jax import lax
from jax.experimental import pallas as pl
from jax.experimental.pallas import tpu as pltpu
from jax.sharding import PartitionSpec as P

MESH = pl.DeviceIdType.MESH
F32 = jnp.float32
BF16 = jnp.bfloat16
D = 384
HD = 32
GROUPS = 3
NX, NZ, NY = 4, 8, 8
NT = (((1,), (1,)), ((), ()))
TN = (((0,), (0,)), ((), ()))


def dot(a, b, dims=(((1,), (0,)), ((), ()))):
    return lax.dot_general(a, b, dims, preferred_element_type=F32)


def roll4(a):
    n, _, width = a.shape
    return pltpu.roll(a.reshape(n * 8, width).reshape(n, 8, width), 4, 1)


def low4(shape):
    return lax.broadcasted_iota(jnp.int32, shape, len(shape) - 2) % 8 < 4


def kernel(
    x_hbm, dy_hbm, mask_ref, wq_hbm, wo_hbm,
    out_hbm, gq_ref, go_ref,
    xv, dyv, wq, wo, outv,
    rim_out, rim_in, back_out, back_in,
    normed, masked, att, gp, xhat, istd, branch,
    grads, r0x, r0z, hx, hz, r1x, r1z, jx, jz, r2x, r2z, r3x, r3z, fx, fz,
    in_sem, out_sem, rim_sem, back_sem,
    s0, q0, s1x, q1x, s1z, q1z, s2x, q2x, s2z, q2z, s3x, q3x, s3z, q3z, s4, q4,
):
    region, tile = lax.axis_index("region"), lax.axis_index("tile")
    y, core = region // 2, region % 2
    x, z = tile // NZ, tile % NZ
    tiles = NX * NZ

    def at(ax, ay, az, ac):
        return {"region": ay * 2 + ac, "tile": ax * NZ + az}

    other = at(x, y, z, 1 - core)
    west = {"region": region, "tile": (tile + tiles - 1) % tiles}
    east = {"region": region, "tile": (tile + 1) % tiles}
    by_x = [at((x + k) % NX, y, z, core) for k in range(1, NX)]
    by_z = [at(x, y, (z + k) % NZ, core) for k in range(1, NZ)]
    by_y = [at(x, (y + k) % NY, z, core) for k in range(1, NY)]

    def send(src, dst, ss, rs, dev):
        return pltpu.make_async_remote_copy(
            src_ref=src, dst_ref=dst, send_sem=ss, recv_sem=rs,
            device_id=dev, device_id_type=MESH,
        )

    barrier = pltpu.get_barrier_semaphore()
    partners = [west, east, other] + by_x + by_z + by_y
    for dev in partners:
        pl.semaphore_signal(barrier, inc=1, device_id=dev, device_id_type=MESH)

    loads = [
        pltpu.make_async_copy(src, dst, in_sem.at[i])
        for i, (src, dst) in enumerate(
            ((x_hbm, xv), (dy_hbm, dyv), (wq_hbm, wq), (wo_hbm, wo))
        )
    ]
    for c in loads:
        c.start()
    loads[0].wait()
    loads[1].wait()

    sub = low4((1, 8, D))

    def halves(ref):
        v = ref[...].astype(F32)
        return v[:, :8, :], v[:, 8:, :]

    def pairs(v):
        v = v.reshape(8, 2, 8, D)
        return v[:, 0], v[:, 1]

    def rim_of(lo):
        even, odd = pairs(lo)
        return jnp.where(sub, even, roll4(odd)).reshape(64, D)

    x_lo, x_hi = halves(xv)
    rim_out[0] = rim_of(x_lo).astype(BF16)
    dy_lo, dy_hi = halves(dyv)
    rim_out[1] = rim_of(dy_lo).astype(BF16)

    pl.semaphore_wait(barrier, len(partners))
    rim = send(rim_out, rim_in, rim_sem.at[0], rim_sem.at[1], west)
    rim.start()

    lane_head = lax.broadcasted_iota(jnp.int32, (1, 128), 1) // HD
    head_masks = [(lane_head == h).astype(F32).astype(BF16) for h in range(4)]
    inv_root = HD ** -0.5

    def flags(b):
        return [mask_ref[a, b].astype(F32) for a in range(2)]

    def layer(b, feats, dys):
        rows = pl.ds(128 * b, 128)
        center = jnp.mean(feats, axis=-1, keepdims=True)
        dev = feats - center
        inv = lax.rsqrt(jnp.mean(dev * dev, axis=-1, keepdims=True) + 1e-05)
        hat = dev * inv
        xhat[rows, :] = hat
        istd[rows, :] = jnp.broadcast_to(inv, (128, 128))
        nb = hat.astype(BF16)
        normed[rows, :] = nb
        proj = dot(nb, wq[...]).astype(BF16)
        f = flags(b)
        mk = jnp.concatenate([dys[:64] * f[0], dys[64:] * f[1]], axis=0).astype(BF16)
        masked[rows, :] = mk
        ga = dot(mk, wo[...], NT).astype(BF16)
        for g in range(GROUPS):
            lanes = slice(128 * g, 128 * g + 128)
            for a in range(2):
                r = slice(64 * a, 64 * a + 64)
                q = proj[r, 128 * g:128 * g + 128]
                k = proj[r, D + 128 * g:D + 128 * g + 128]
                v = proj[r, 2 * D + 128 * g:2 * D + 128 * g + 128]
                o = ga[r, lanes]
                qbd = jnp.concatenate([q * m for m in head_masks], axis=0)
                obd = jnp.concatenate([o * m for m in head_masks], axis=0)
                s = dot(k, qbd, NT) * inv_root
                dp = dot(v, obd, NT)
                e = jnp.exp(s - jnp.max(s, axis=0, keepdims=True))
                p = e * (1.0 / jnp.sum(e, axis=0, keepdims=True))
                pb = p.astype(BF16)
                row = jnp.sum(dp * p, axis=0, keepdims=True)
                ds = (p * (dp - row) * inv_root).astype(BF16)
                full_o = dot(pb, v, TN)
                full_q = dot(ds, k, TN)

                def own(full):
                    t = full[192:]
                    for h in (2, 1, 0):
                        t = jnp.where(lane_head == h, full[64 * h:64 * h + 64], t)
                    return t.astype(BF16)

                base = 128 * b + 64 * a
                att[base:base + 64, lanes] = own(full_o)
                gp[base:base + 64, 128 * g:128 * g + 128] = own(full_q)
                gp[base:base + 64, D + 128 * g:D + 128 * g + 128] = dot(ds, qbd).astype(BF16)
                gp[base:base + 64, 2 * D + 128 * g:2 * D + 128 * g + 128] = dot(pb, obd).astype(BF16)

    loads[2].wait()
    loads[3].wait()
    layer(
        0,
        jnp.where(sub, x_hi, x_lo).reshape(128, D),
        jnp.where(sub, dy_hi, dy_lo).reshape(128, D),
    )

    def local_of(hi):
        even, odd = pairs(hi)
        return jnp.where(sub, roll4(even), odd).reshape(64, D)

    x_loc, dy_loc = local_of(x_hi), local_of(dy_hi)
    rim.wait()

    def joined(loc, far):
        far = far.astype(F32)
        return jnp.concatenate([loc[:32], far[:32], loc[32:], far[32:]], axis=0)

    layer(1, joined(x_loc, rim_in[0]), joined(dy_loc, rim_in[1]))

    normed_t = normed[...].T
    ga_full = dot(att[...].T, masked[...]).reshape(16, 3, 8, D)
    w0, w1, w2 = ga_full[:, 0], ga_full[:, 1], ga_full[:, 2]
    spare = [
        roll4(jnp.where(sub, w0, w1)),
        jnp.where(sub, w2, w0),
        roll4(jnp.where(sub, w1, w2)),
    ]
    sends = []

    def start(c):
        c.start()
        sends.append(c)
        return c

    core0 = []
    for g in range(GROUPS):
        cols = jnp.concatenate(
            [gp[:, s * D + 128 * g:s * D + 128 * g + 128] for s in range(3)], axis=1
        )
        gn = dot(normed_t, cols).reshape(16, 3, 8, D)
        v0, v1, v2 = gn[:, 0], gn[:, 1], gn[:, 2]
        packed = jnp.stack(
            [v0, jnp.where(sub, v1, spare[g]), v2, jnp.where(sub, spare[g], v1)], axis=1
        )
        grads[g] = packed.reshape(NX, NZ, 16, D).astype(BF16)
        if g < 2:
            c = send(grads.at[g, :, pl.ds((1 - core) * 4, 4)], r0x.at[g], s0.at[g], q0.at[g], other)
        else:
            c = send(grads.at[g, pl.ds((1 - core) * 2, 2)], r0z, s0.at[g], q0.at[g], other)
        core0.append(start(c))

    p1x = []
    for g in range(2):
        core0[g].wait_recv()
        mine = grads[g, :, pl.ds(core * 4, 4)].astype(F32) + r0x[g].astype(F32)
        hx[g] = mine.astype(BF16)
        for k in range(1, NX):
            p1x.append(start(send(
                hx.at[g, (x + k) % NX], r1x.at[g, k - 1],
                s1x.at[g, k - 1], q1x.at[g, k - 1], by_x[k - 1],
            )))
    core0[2].wait_recv()
    mine = grads[2, pl.ds(core * 2, 2)].astype(F32) + r0z[...].astype(F32)
    hz[...] = mine.astype(BF16)
    p1z = []
    for k in range(1, NZ):
        p1z.append(start(send(
            hz.at[:, (z + k) % NZ], r1z.at[k - 1], s1z.at[k - 1], q1z.at[k - 1], by_z[k - 1],
        )))

    def branch_of(b):
        rows = pl.ds(128 * b, 128)
        gn = dot(gp[rows, :], wq[...], NT)
        hat = xhat[rows, :]
        inv = istd[rows, :][:, :1]
        m0 = jnp.mean(gn, axis=-1, keepdims=True)
        m1 = jnp.mean(gn * hat, axis=-1, keepdims=True)
        return (inv * (gn - m0 - hat * m1)).astype(BF16)

    br = branch_of(1)
    back_out[0:32, :] = br[32:64]
    back_out[32:64, :] = br[96:128]
    back = start(send(back_out, back_in, back_sem.at[0], back_sem.at[1], east))
    loc = jnp.concatenate([br[0:32], br[64:96]], axis=0).astype(F32).reshape(8, 8, D)
    branch[...] = branch_of(0).astype(F32)

    for c in p1x:
        c.wait_recv()
    for g in range(2):
        t = hx[g, x].astype(F32)
        for k in range(NX - 1):
            t = t + r1x[g, k].astype(F32)
        jx[g] = t.astype(BF16)
    for k in range(1, NZ):
        to = (z + k) % NZ
        c = send(jx.at[:, to % 4], r2x.at[k - 1], s2x.at[k - 1], q2x.at[k - 1], by_z[k - 1])

        @pl.when(to // 4 == core)
        def _():
            c.start()

    for c in p1z:
        c.wait_recv()
    t = hz[:, z].astype(F32)
    for k in range(NZ - 1):
        t = t + r1z[k].astype(F32)
    jz[...] = t.astype(BF16)
    for k in range(1, NX):
        to = (x + k) % NX
        c = send(jz.at[to % 2], r2z.at[k - 1], s2z.at[k - 1], q2z.at[k - 1], by_x[k - 1])

        @pl.when(to // 2 == core)
        def _():
            c.start()

    has_x = z // 4 == core
    has_z = x // 2 == core

    def y_copies(buf, ss, qs):
        return [
            send(buf.at[y], buf.at[y], ss.at[k - 1], qs.at[y], by_y[k - 1])
            for k in range(1, NY)
        ]

    def y_arrivals(buf, ss, qs):
        return [
            send(buf.at[y], buf.at[(y + k) % NY], ss.at[k - 1], qs.at[(y + k) % NY], by_y[k - 1])
            for k in range(1, NY)
        ]

    @pl.when(has_x)
    def _():
        t = jx[:, z % 4].astype(F32)
        for k in range(1, NZ):
            send(jx.at[:, z % 4], r2x.at[k - 1], s2x.at[k - 1], q2x.at[k - 1], by_z[k - 1]).wait_recv()
        for k in range(NZ - 1):
            t = t + r2x[k].astype(F32)
        r3x[y] = t.astype(BF16)
        for c in y_copies(r3x, s3x, q3x):
            c.start()

    @pl.when(has_z)
    def _():
        t = jz[x % 2].astype(F32)
        for k in range(1, NX):
            send(jz.at[x % 2], r2z.at[k - 1], s2z.at[k - 1], q2z.at[k - 1], by_x[k - 1]).wait_recv()
        for k in range(NX - 1):
            t = t + r2z[k].astype(F32)
        r3z[y] = t.astype(BF16)
        for c in y_copies(r3z, s3z, q3z):
            c.start()

    back.wait_recv()
    far = back_in[...].astype(F32).reshape(8, 8, D)
    br0 = branch[...].reshape(16, 8, D)

    def unpaired(even, odd):
        return jnp.stack([even, odd], axis=1).reshape(16, 8, D)

    new_lo = dyv[:, :8, :].astype(F32) + jnp.where(sub, unpaired(far, roll4(far)), br0)
    new_hi = dyv[:, 8:, :].astype(F32) + jnp.where(sub, br0, unpaired(roll4(loc), loc))
    outv[...] = jnp.concatenate([new_lo, new_hi], axis=1).astype(BF16)
    store = pltpu.make_async_copy(outv, out_hbm, out_sem)
    store.start()

    last_x = send(fx, fx, s4.at[0], q4.at[0], other)
    last_z = send(fz, fz, s4.at[1], q4.at[1], other)

    @pl.when(has_x)
    def _():
        for c in y_arrivals(r3x, s3x, q3x):
            c.wait_recv()
        t = r3x[0].astype(F32)
        for k in range(1, NY):
            t = t + r3x[k].astype(F32)
        fx[...] = t.astype(BF16)
        last_x.start()

    @pl.when(has_z)
    def _():
        for c in y_arrivals(r3z, s3z, q3z):
            c.wait_recv()
        t = r3z[0].astype(F32)
        for k in range(1, NY):
            t = t + r3z[k].astype(F32)
        fz[...] = t.astype(BF16)
        last_z.start()

    @pl.when(jnp.logical_not(has_x))
    def _():
        last_x.wait_recv()

    @pl.when(jnp.logical_not(has_z))
    def _():
        last_z.wait_recv()

    scale = 1.0 / math.sqrt(3 * 64 * 2 * NY * tiles)
    odd = (z % 2) == 1
    for g in range(GROUPS):
        f = (fx[g] if g < 2 else fz[...]).astype(F32) * scale
        top, bot = f[0:8], f[8:16]
        top_r, bot_r = pltpu.roll(top, 4, 0), pltpu.roll(bot, 4, 0)
        low = low4((8, D))
        first = jnp.where(odd, jnp.where(low, bot_r, top_r), top)
        rest = jnp.where(odd, top_r, bot)
        extra = jnp.where(odd, bot, bot_r)
        for s in range(3):
            lanes = slice(s * D + 128 * g, s * D + 128 * g + 128)
            gq_ref[0:8, lanes] = first[:, 128 * s:128 * s + 128]
            gq_ref[8:12, lanes] = rest[0:4, 128 * s:128 * s + 128]
        go_ref[4 * g:4 * g + 4, :] = extra[0:4]

    for c in sends:
        c.wait_send()
    rim_done = store
    for k in range(1, NZ):
        to = (z + k) % NZ
        c = send(jx.at[:, to % 4], r2x.at[k - 1], s2x.at[k - 1], q2x.at[k - 1], by_z[k - 1])

        @pl.when(to // 4 == core)
        def _():
            c.wait_send()

    for k in range(1, NX):
        to = (x + k) % NX
        c = send(jz.at[to % 2], r2z.at[k - 1], s2z.at[k - 1], q2z.at[k - 1], by_x[k - 1])

        @pl.when(to // 2 == core)
        def _():
            c.wait_send()

    @pl.when(has_x)
    def _():
        for c in y_copies(r3x, s3x, q3x):
            c.wait_send()
        last_x.wait_send()

    @pl.when(has_z)
    def _():
        for c in y_copies(r3z, s3z, q3z):
            c.wait_send()
        last_z.wait_send()

    rim_done.wait()


def body(tokens, grad_out, ocean_mask, w_qkv, w_out):
    any_spec = pl.BlockSpec(memory_space=pl.ANY)
    vmem_spec = pl.BlockSpec(memory_space=pltpu.VMEM)

    def buf(*shape, dtype=BF16):
        return pltpu.VMEM(shape, dtype)

    def sem(*shape):
        return pltpu.SemaphoreType.DMA(shape)

    return pl.pallas_call(
        kernel,
        out_shape=(
            jax.ShapeDtypeStruct((16, 16, D), BF16),
            jax.ShapeDtypeStruct((12, 3 * D), F32),
            jax.ShapeDtypeStruct((12, D), F32),
        ),
        in_specs=[any_spec, any_spec, pl.BlockSpec(memory_space=pltpu.SMEM), any_spec, any_spec],
        out_specs=(any_spec, vmem_spec, vmem_spec),
        scratch_shapes=[
            buf(16, 16, D), buf(16, 16, D), buf(D, 3 * D), buf(D, D), buf(16, 16, D),
            buf(2, 64, D), buf(2, 64, D), buf(64, D), buf(64, D),
            buf(256, D), buf(256, D), buf(256, D), buf(256, 3 * D),
            buf(256, D, dtype=F32), buf(256, 128, dtype=F32), buf(128, D, dtype=F32),
            buf(3, NX, NZ, 16, D),
            buf(2, NX, 4, 16, D), buf(2, NZ, 16, D),
            buf(2, NX, 4, 16, D), buf(2, NZ, 16, D),
            buf(2, NX - 1, 4, 16, D), buf(NZ - 1, 2, 16, D),
            buf(2, 4, 16, D), buf(2, 16, D),
            buf(NZ - 1, 2, 16, D), buf(NX - 1, 16, D),
            buf(NY, 2, 16, D), buf(NY, 16, D),
            buf(2, 16, D), buf(16, D),
            sem(4), pltpu.SemaphoreType.DMA, sem(2), sem(2),
            sem(3), sem(3), sem(2, NX - 1), sem(2, NX - 1), sem(NZ - 1), sem(NZ - 1),
            sem(NZ - 1), sem(NZ - 1), sem(NX - 1), sem(NX - 1),
            sem(NY - 1), sem(NY), sem(NY - 1), sem(NY), sem(2), sem(2),
        ],
        compiler_params=pltpu.CompilerParams(
            collective_id=0, has_side_effects=True, vmem_limit_bytes=48 * 1024 * 1024
        ),
        cost_estimate=pl.CostEstimate(
            flops=900_000_000, bytes_accessed=2_000_000, transcendentals=200_000
        ),
        name="window_grads",
    )(tokens, grad_out, ocean_mask, w_qkv, w_out)


def solution(mesh):
    return jax.shard_map(
        body,
        mesh=mesh,
        in_specs=(
            P("region", "tile", None),
            P("region", "tile", None),
            P("region", "tile"),
            P(),
            P(),
        ),
        out_specs=(P("region", "tile", None), P("tile", None), P("tile", None)),
        check_vma=False,
    )
```

```python
import math

import jax
import jax.numpy as jnp
from jax import lax
from jax.experimental import pallas as pl
from jax.experimental.pallas import tpu as pltpu
from jax.sharding import PartitionSpec as P

MESH = pl.DeviceIdType.MESH
F32 = jnp.float32
BF16 = jnp.bfloat16
D = 384
HD = 32
LOG2E = math.log2(math.e)
GROUPS = 3
NX, NZ, NY = 4, 8, 8
WX, WZ = 640, 512
XCUT = (slice(0, 384), slice(384, 640))
NT = (((1,), (1,)), ((), ()))


def dot(a, b, dims=(((1,), (0,)), ((), ()))):
    return lax.dot_general(a, b, dims, preferred_element_type=F32)


def roll4(a):
    n, _, width = a.shape
    return pltpu.roll(a.reshape(n * 8, width).reshape(n, 8, width), 4, 1)


def low4(shape):
    return lax.broadcasted_iota(jnp.int32, shape, len(shape) - 2) % 8 < 4


def kernel(
    x_hbm, dy_hbm, mask_ref, wq_hbm, wo_hbm,
    out_hbm, gq_ref, go_ref,
    xv, dyv, wq, wo, outv,
    rim_out, rim_in, back_out, back_in,
    normed_t, masked, att_t, query_t, gp, xhat, istd, branch,
    gx, gz, r0x, r0z, hx, hz, r1x, r1z, jx, jz, r2x, r2z, r3x, r3z, fx, fz,
    in_sem, out_sem, rim_sem, back_sem,
    s0, q0, s1x, q1x, s1z, q1z, s2x, q2x, s2z, q2z, s3x, q3x, s3z, q3z, s4, q4,
):
    region, tile = lax.axis_index("region"), lax.axis_index("tile")
    y, core = region // 2, region % 2
    x, z = tile // NZ, tile % NZ
    tiles = NX * NZ

    def at(ax, ay, az, ac):
        return {"region": ay * 2 + ac, "tile": ax * NZ + az}

    other = at(x, y, z, 1 - core)
    west = {"region": region, "tile": (tile + tiles - 1) % tiles}
    east = {"region": region, "tile": (tile + 1) % tiles}
    by_x = [at((x + k) % NX, y, z, core) for k in range(1, NX)]
    by_z = [at(x, y, (z + k) % NZ, core) for k in range(1, NZ)]
    by_y = [at(x, (y + k) % NY, z, core) for k in range(1, NY)]

    def send(src, dst, ss, rs, dev):
        return pltpu.make_async_remote_copy(
            src_ref=src, dst_ref=dst, send_sem=ss, recv_sem=rs,
            device_id=dev, device_id_type=MESH,
        )

    barrier = pltpu.get_barrier_semaphore()
    partners = [west, east, other] + by_x + by_z + by_y
    for dev in partners:
        pl.semaphore_signal(barrier, inc=1, device_id=dev, device_id_type=MESH)

    loads = [
        pltpu.make_async_copy(src, dst, in_sem.at[i])
        for i, (src, dst) in enumerate(
            ((x_hbm, xv), (dy_hbm, dyv), (wq_hbm, wq), (wo_hbm, wo))
        )
    ]
    for c in loads:
        c.start()
    loads[0].wait()
    loads[1].wait()

    sub = low4((1, 8, D))

    def halves(ref):
        v = ref[...].astype(F32)
        return v[:, :8, :], v[:, 8:, :]

    def pairs(v):
        v = v.reshape(8, 2, 8, D)
        return v[:, 0], v[:, 1]

    def rim_of(lo):
        even, odd = pairs(lo)
        return jnp.where(sub, even, roll4(odd)).reshape(64, D)

    x_lo, x_hi = halves(xv)
    rim_out[0] = rim_of(x_lo).astype(BF16)
    dy_lo, dy_hi = halves(dyv)
    rim_out[1] = rim_of(dy_lo).astype(BF16)

    pl.semaphore_wait(barrier, len(partners))
    rim = send(rim_out, rim_in, rim_sem.at[0], rim_sem.at[1], west)
    rim.start()

    lane_head = lax.broadcasted_iota(jnp.int32, (1, 128), 1) // HD
    head_masks = [(lane_head == h).astype(F32).astype(BF16) for h in range(4)]
    inv_root = HD ** -0.5

    def flags(b):
        return [mask_ref[a, b].astype(F32) for a in range(2)]

    def layer(b, feats, dys):
        rows = pl.ds(128 * b, 128)
        cols = slice(128 * b, 128 * b + 128)
        center = jnp.mean(feats, axis=-1, keepdims=True)
        dev = feats - center
        inv = lax.rsqrt(jnp.mean(dev * dev, axis=-1, keepdims=True) + 1e-05)
        hat = dev * inv
        xhat[rows, :] = hat
        istd[rows, :] = jnp.broadcast_to(inv, (128, 128))
        nb = hat.astype(BF16)
        proj = dot(nb, wq[...]).astype(BF16)
        f = flags(b)
        mk = jnp.concatenate([dys[:64] * f[0], dys[64:] * f[1]], axis=0).astype(BF16)
        masked[rows, :] = mk
        ga = dot(mk, wo[...], NT).astype(BF16)
        normed_t[:, cols] = nb.T

        units = [(a, g) for g in range(GROUPS) for a in range(2)]

        def part(array, a, first):
            return array[64 * a:64 * a + 64, first:first + 128]

        def spread(array, a):
            order = (1, 0, 3, 2) if a else (0, 1, 2, 3)
            return jnp.concatenate([array * head_masks[h] for h in order], axis=0)

        k = [part(proj, a, D + 128 * g) for a, g in units]
        v = [part(proj, a, 2 * D + 128 * g) for a, g in units]
        qbd = [spread(part(proj, a, 128 * g), a) for a, g in units]
        obd = [spread(part(ga, a, 128 * g), a) for a, g in units]
        s = [dot(m, n, NT) for m, n in zip(k, qbd)]
        dp = [dot(m, n, NT) for m, n in zip(v, obd)]
        kt = [m.T for m in k]
        vt = [m.T for m in v]
        pb, ds = [], []
        for i in range(len(units)):
            e = jnp.exp2((s[i] - jnp.max(s[i], axis=0, keepdims=True)) * (inv_root * LOG2E))
            p = e * (1.0 / jnp.sum(e, axis=0, keepdims=True))
            row = jnp.sum(dp[i] * p, axis=0, keepdims=True)
            pb.append(p.astype(BF16))
            ds.append((p * ((dp[i] - row) * inv_root)).astype(BF16))
        dk = [dot(m, n) for m, n in zip(ds, qbd)]
        dv = [dot(m, n) for m, n in zip(pb, obd)]
        qt = [dot(m, n) for m, n in zip(kt, ds)]
        ot = [dot(m, n) for m, n in zip(vt, pb)]
        for i, (a, g) in enumerate(units):
            at_row = pl.ds(128 * b + 64 * a, 64)
            gp[at_row, D + 128 * g:D + 128 * g + 128] = dk[i].astype(BF16)
            gp[at_row, 2 * D + 128 * g:2 * D + 128 * g + 128] = dv[i].astype(BF16)
        first_half = lax.broadcasted_iota(jnp.int32, (1, 128), 1) < 64

        def own(zero, one):
            blocks = []
            for h in range(4):
                r, c = slice(32 * h, 32 * h + 32), slice(128 * (h // 2), 128 * (h // 2) + 128)
                if h % 2 == 0:
                    blocks.append(jnp.where(first_half, zero[r, c], one[r, c]))
                else:
                    blocks.append(pltpu.roll(jnp.where(first_half, one[r, c], zero[r, c]), 64, 1))
            return jnp.concatenate(blocks, axis=0).astype(BF16)

        for g in range(GROUPS):
            r = slice(128 * g, 128 * g + 128)
            att_t[r, cols] = own(ot[2 * g], ot[2 * g + 1])
            query_t[r, cols] = own(qt[2 * g], qt[2 * g + 1])

    loads[2].wait()
    loads[3].wait()
    layer(
        0,
        jnp.where(sub, x_hi, x_lo).reshape(128, D),
        jnp.where(sub, dy_hi, dy_lo).reshape(128, D),
    )

    def local_of(hi):
        even, odd = pairs(hi)
        return jnp.where(sub, roll4(even), odd).reshape(64, D)

    x_loc, dy_loc = local_of(x_hi), local_of(dy_hi)
    rim.wait()

    def joined(loc, far):
        far = far.astype(F32)
        return jnp.concatenate([loc[:32], far[:32], loc[32:], far[32:]], axis=0)

    layer(1, joined(x_loc, rim_in[0]), joined(dy_loc, rim_in[1]))

    nt = normed_t[...]
    ga_full = dot(att_t[...], masked[...]).reshape(16, 3, 8, D)
    w0, w1, w2 = ga_full[:, 0], ga_full[:, 1], ga_full[:, 2]
    spare = [
        roll4(jnp.where(sub, w0, w1)),
        jnp.where(sub, w2, w0),
        roll4(jnp.where(sub, w1, w2)),
    ]
    sends = []

    def start(c):
        c.start()
        sends.append(c)
        return c

    def swap_x(i):
        return start(send(
            gx.at[:, pl.ds((1 - core) * 4, 4), :, XCUT[i]], r0x.at[:, :, :, XCUT[i]],
            s0.at[i], q0.at[i], other,
        ))

    core0 = []
    for g in range(GROUPS):
        gn = jnp.concatenate([
            dot(nt, query_t[128 * g:128 * g + 128, :], NT),
            dot(nt, gp[:, D + 128 * g:D + 128 * g + 128]),
            dot(nt, gp[:, 2 * D + 128 * g:2 * D + 128 * g + 128]),
        ], axis=1).reshape(16, 3, 8, D)
        v0, v1, v2 = gn[:, 0], gn[:, 1], gn[:, 2]
        packed = jnp.stack(
            [v0, jnp.where(sub, v1, spare[g]), v2, jnp.where(sub, spare[g], v1)], axis=1
        ).reshape(NX, NZ, 16, D).astype(BF16)
        if g == 0:
            gx[:, :, :, 0:384] = packed
            core0.append(swap_x(0))
        elif g == 1:
            gx[:, :, :, 384:640] = packed[..., 0:256]
            gz[:, :, :, 0:128] = packed[..., 256:384]
            core0.append(swap_x(1))
        else:
            gz[:, :, :, 128:512] = packed
            core0.append(start(send(
                gz.at[pl.ds((1 - core) * 2, 2)], r0z, s0.at[g], q0.at[g], other,
            )))

    p1x = []
    for i in range(2):
        core0[i].wait_recv()
        cut = XCUT[i]
        mine = gx[:, pl.ds(core * 4, 4), :, cut].astype(F32) + r0x[:, :, :, cut].astype(F32)
        hx[:, :, :, cut] = mine.astype(BF16)
        for k in (2, 1, 3):
            p1x.append(start(send(
                hx.at[(x + k) % NX, :, :, cut], r1x.at[k - 1, :, :, cut],
                s1x.at[i, k - 1], q1x.at[i, k - 1], by_x[k - 1],
            )))
    core0[2].wait_recv()
    mine = gz[pl.ds(core * 2, 2)].astype(F32) + r0z[...].astype(F32)
    hz[...] = mine.astype(BF16)
    p1z = []
    for k in (4, 3, 5, 2, 6, 1, 7):
        p1z.append(start(send(
            hz.at[:, (z + k) % NZ], r1z.at[k - 1], s1z.at[k - 1], q1z.at[k - 1], by_z[k - 1],
        )))

    for b in range(2):
        gp[128 * b:128 * b + 128, 0:D] = query_t[:, 128 * b:128 * b + 128].T

    def branch_of(b):
        rows = pl.ds(128 * b, 128)
        gn = dot(gp[rows, :], wq[...], NT)
        hat = xhat[rows, :]
        inv = istd[rows, :][:, :1]
        m0 = jnp.mean(gn, axis=-1, keepdims=True)
        m1 = jnp.mean(gn * hat, axis=-1, keepdims=True)
        return (inv * (gn - m0 - hat * m1)).astype(BF16)

    br = branch_of(1)
    back_out[0:32, :] = br[32:64]
    back_out[32:64, :] = br[96:128]
    back = start(send(back_out, back_in, back_sem.at[0], back_sem.at[1], east))
    loc = jnp.concatenate([br[0:32], br[64:96]], axis=0).astype(F32).reshape(8, 8, D)
    branch[...] = branch_of(0).astype(F32)

    for c in p1x:
        c.wait_recv()
    t = hx[x].astype(F32)
    for k in range(NX - 1):
        t = t + r1x[k].astype(F32)
    jx[...] = t.astype(BF16)
    for k in range(1, NZ):
        to = (z + k) % NZ
        c = send(jx.at[to % 4], r2x.at[k - 1], s2x.at[k - 1], q2x.at[k - 1], by_z[k - 1])

        @pl.when(to // 4 == core)
        def _():
            c.start()

    for c in p1z:
        c.wait_recv()
    t = hz[:, z].astype(F32)
    for k in range(NZ - 1):
        t = t + r1z[k].astype(F32)
    jz[...] = t.astype(BF16)
    for k in range(1, NX):
        to = (x + k) % NX
        c = send(jz.at[to % 2], r2z.at[k - 1], s2z.at[k - 1], q2z.at[k - 1], by_x[k - 1])

        @pl.when(to // 2 == core)
        def _():
            c.start()

    has_x = z // 4 == core
    has_z = x // 2 == core

    def y_copies(buf, ss, qs):
        return [
            send(buf.at[y], buf.at[y], ss.at[k - 1], qs.at[y], by_y[k - 1])
            for k in range(1, NY)
        ]

    def y_arrivals(buf, ss, qs):
        return [
            send(buf.at[y], buf.at[(y + k) % NY], ss.at[k - 1], qs.at[(y + k) % NY], by_y[k - 1])
            for k in range(1, NY)
        ]

    @pl.when(has_x)
    def _():
        t = jx[z % 4].astype(F32)
        for k in range(1, NZ):
            send(jx.at[z % 4], r2x.at[k - 1], s2x.at[k - 1], q2x.at[k - 1], by_z[k - 1]).wait_recv()
        for k in range(NZ - 1):
            t = t + r2x[k].astype(F32)
        r3x[y] = t.astype(BF16)
        for c in y_copies(r3x, s3x, q3x):
            c.start()

    @pl.when(has_z)
    def _():
        t = jz[x % 2].astype(F32)
        for k in range(1, NX):
            send(jz.at[x % 2], r2z.at[k - 1], s2z.at[k - 1], q2z.at[k - 1], by_x[k - 1]).wait_recv()
        for k in range(NX - 1):
            t = t + r2z[k].astype(F32)
        r3z[y] = t.astype(BF16)
        for c in y_copies(r3z, s3z, q3z):
            c.start()

    back.wait_recv()
    far = back_in[...].astype(F32).reshape(8, 8, D)
    br0 = branch[...].reshape(16, 8, D)

    def unpaired(even, odd):
        return jnp.stack([even, odd], axis=1).reshape(16, 8, D)

    new_lo = dyv[:, :8, :].astype(F32) + jnp.where(sub, unpaired(far, roll4(far)), br0)
    new_hi = dyv[:, 8:, :].astype(F32) + jnp.where(sub, br0, unpaired(roll4(loc), loc))
    outv[...] = jnp.concatenate([new_lo, new_hi], axis=1).astype(BF16)
    store = pltpu.make_async_copy(outv, out_hbm, out_sem)
    store.start()

    last_x = send(fx, fx, s4.at[0], q4.at[0], other)
    last_z = send(fz, fz, s4.at[1], q4.at[1], other)

    @pl.when(has_x)
    def _():
        for c in y_arrivals(r3x, s3x, q3x):
            c.wait_recv()
        t = r3x[0].astype(F32)
        for k in range(1, NY):
            t = t + r3x[k].astype(F32)
        fx[...] = t.astype(BF16)
        last_x.start()

    @pl.when(has_z)
    def _():
        for c in y_arrivals(r3z, s3z, q3z):
            c.wait_recv()
        t = r3z[0].astype(F32)
        for k in range(1, NY):
            t = t + r3z[k].astype(F32)
        fz[...] = t.astype(BF16)
        last_z.start()

    @pl.when(jnp.logical_not(has_x))
    def _():
        last_x.wait_recv()

    @pl.when(jnp.logical_not(has_z))
    def _():
        last_z.wait_recv()

    scale = 1.0 / math.sqrt(3 * 64 * 2 * NY * tiles)
    odd = (z % 2) == 1
    final = jnp.concatenate([fx[...], fz[...]], axis=1).astype(F32) * scale
    for g in range(GROUPS):
        f = final[:, D * g:D * g + D]
        top, bot = f[0:8], f[8:16]
        top_r, bot_r = pltpu.roll(top, 4, 0), pltpu.roll(bot, 4, 0)
        low = low4((8, D))
        first = jnp.where(odd, jnp.where(low, bot_r, top_r), top)
        rest = jnp.where(odd, top_r, bot)
        extra = jnp.where(odd, bot, bot_r)
        for s in range(3):
            lanes = slice(s * D + 128 * g, s * D + 128 * g + 128)
            gq_ref[0:8, lanes] = first[:, 128 * s:128 * s + 128]
            gq_ref[8:12, lanes] = rest[0:4, 128 * s:128 * s + 128]
        go_ref[4 * g:4 * g + 4, :] = extra[0:4]

    for c in sends:
        c.wait_send()
    rim_done = store
    for k in range(1, NZ):
        to = (z + k) % NZ
        c = send(jx.at[to % 4], r2x.at[k - 1], s2x.at[k - 1], q2x.at[k - 1], by_z[k - 1])

        @pl.when(to // 4 == core)
        def _():
            c.wait_send()

    for k in range(1, NX):
        to = (x + k) % NX
        c = send(jz.at[to % 2], r2z.at[k - 1], s2z.at[k - 1], q2z.at[k - 1], by_x[k - 1])

        @pl.when(to // 2 == core)
        def _():
            c.wait_send()

    @pl.when(has_x)
    def _():
        for c in y_copies(r3x, s3x, q3x):
            c.wait_send()
        last_x.wait_send()

    @pl.when(has_z)
    def _():
        for c in y_copies(r3z, s3z, q3z):
            c.wait_send()
        last_z.wait_send()

    rim_done.wait()


def hand_over(a, b, c, a_out, b_out, c_out, sems):
    copies = [
        pltpu.make_async_copy(src, dst, sems.at[i])
        for i, (src, dst) in enumerate(((a, a_out), (b, b_out), (c, c_out)))
    ]
    for c in copies:
        c.start()
    for c in copies:
        c.wait()


def body(tokens, grad_out, ocean_mask, w_qkv, w_out):
    any_spec = pl.BlockSpec(memory_space=pl.ANY)
    vmem_spec = pl.BlockSpec(memory_space=pltpu.VMEM)

    def buf(*shape, dtype=BF16):
        return pltpu.VMEM(shape, dtype)

    def sem(*shape):
        return pltpu.SemaphoreType.DMA(shape)

    results = pl.pallas_call(
        kernel,
        out_shape=(
            jax.ShapeDtypeStruct((16, 16, D), BF16),
            jax.ShapeDtypeStruct((12, 3 * D), F32),
            jax.ShapeDtypeStruct((12, D), F32),
        ),
        in_specs=[any_spec, any_spec, pl.BlockSpec(memory_space=pltpu.SMEM), any_spec, any_spec],
        out_specs=(any_spec, vmem_spec, vmem_spec),
        scratch_shapes=[
            buf(16, 16, D), buf(16, 16, D), buf(D, 3 * D), buf(D, D), buf(16, 16, D),
            buf(2, 64, D), buf(2, 64, D), buf(64, D), buf(64, D),
            buf(D, 256), buf(256, D), buf(D, 256), buf(D, 256), buf(256, 3 * D),
            buf(256, D, dtype=F32), buf(256, 128, dtype=F32), buf(128, D, dtype=F32),
            buf(NX, NZ, 16, WX), buf(NX, NZ, 16, WZ),
            buf(NX, 4, 16, WX), buf(2, NZ, 16, WZ),
            buf(NX, 4, 16, WX), buf(2, NZ, 16, WZ),
            buf(NX - 1, 4, 16, WX), buf(NZ - 1, 2, 16, WZ),
            buf(4, 16, WX), buf(2, 16, WZ),
            buf(NZ - 1, 16, WX), buf(NX - 1, 16, WZ),
            buf(NY, 16, WX), buf(NY, 16, WZ),
            buf(16, WX), buf(16, WZ),
            sem(4), pltpu.SemaphoreType.DMA, sem(2), sem(2),
            sem(3), sem(3), sem(2, NX - 1), sem(2, NX - 1), sem(NZ - 1), sem(NZ - 1),
            sem(NZ - 1), sem(NZ - 1), sem(NX - 1), sem(NX - 1),
            sem(NY - 1), sem(NY), sem(NY - 1), sem(NY), sem(2), sem(2),
        ],
        compiler_params=pltpu.CompilerParams(
            collective_id=0, has_side_effects=True, vmem_limit_bytes=63 * 1024 * 1024
        ),
        cost_estimate=pl.CostEstimate(
            flops=900_000_000, bytes_accessed=2_000_000, transcendentals=200_000
        ),
        name="window_grads",
    )(tokens, grad_out, ocean_mask, w_qkv, w_out)
    return pl.pallas_call(
        hand_over,
        out_shape=[jax.ShapeDtypeStruct(r.shape, r.dtype) for r in results],
        in_specs=[any_spec] * 3,
        out_specs=[any_spec] * 3,
        scratch_shapes=[sem(3)],
        compiler_params=pltpu.CompilerParams(vmem_limit_bytes=63 * 1024 * 1024),
        cost_estimate=pl.CostEstimate(flops=0, bytes_accessed=600_000, transcendentals=0),
        name="hand_over",
    )(*results)


def solution(mesh):
    return jax.shard_map(
        body,
        mesh=mesh,
        in_specs=(
            P("region", "tile", None),
            P("region", "tile", None),
            P("region", "tile"),
            P(),
            P(),
        ),
        out_specs=(P("region", "tile", None), P("tile", None), P("tile", None)),
        check_vma=False,
    )
```

```python
import math

import jax
import jax.numpy as jnp
from jax import lax
from jax.experimental import pallas as pl
from jax.experimental.pallas import tpu as pltpu
from jax.sharding import PartitionSpec as P

MESH = pl.DeviceIdType.MESH
F32 = jnp.float32
BF16 = jnp.bfloat16
D = 384
HD = 32
LOG2E = math.log2(math.e)
GROUPS = 3
NX, NZ, NY = 4, 8, 8
TX, TZ = 4, 2
WY, WX, WZ = 384, 128 * TX, 128 * TZ
XCUT = (slice(0, 384), slice(384, 512))
NT = (((1,), (1,)), ((), ()))


def dot(a, b, dims=(((1,), (0,)), ((), ()))):
    return lax.dot_general(a, b, dims, preferred_element_type=F32)


def roll4(a):
    n, _, width = a.shape
    return pltpu.roll(a.reshape(n * 8, width).reshape(n, 8, width), 4, 1)


def low4(shape):
    return lax.broadcasted_iota(jnp.int32, shape, len(shape) - 2) % 8 < 4


def kernel(
    x_hbm, dy_hbm, mask_hbm, wq_hbm, wo_hbm,
    out_ref, gq_ref, go_ref,
    xv, dyv, mask_ref, wq, wo,
    rim_out, rim_in, back_out, back_in,
    normed_t, masked, att_t, query_t, gp, xhat, istd, branch,
    gx, gy, gz, r0x, r0y, r0z, hx, hy, hz, r1x, r1y, r1z, jx, jy, jz,
    r2x, r2y, r2z, kx, ky, kz, r3x, r3y, r3z, tiles_in, last_in,
    in_sem, rim_sem, back_sem,
    s0, q0, s1x, q1x, s1y, q1y, s1z, q1z, s2x, q2x, s2y, q2y, s2z, q2z,
    s3x, q3x, s3y, q3y, s3z, q3z, s4x, s4y, s4z, q4, q4y,
):
    loads = [
        pltpu.make_async_copy(src, dst, in_sem.at[i])
        for i, (src, dst) in enumerate(
            ((x_hbm, xv), (dy_hbm, dyv), (wq_hbm, wq), (wo_hbm, wo), (mask_hbm, mask_ref))
        )
    ]
    for c in loads:
        c.start()

    region, tile = lax.axis_index("region"), lax.axis_index("tile")
    y, core = region // 2, region % 2
    x, z = tile // NZ, tile % NZ
    tiles, bands = NX * NZ, 2 * NY

    def at(ax, ay, az, ac):
        return {"region": ay * 2 + ac, "tile": ax * NZ + az}

    other = at(x, y, z, 1 - core)
    west = {"region": region, "tile": (tile + tiles - 1) % tiles}
    east = {"region": region, "tile": (tile + 1) % tiles}
    by_x = [at((x + k) % NX, y, z, core) for k in range(1, NX)]
    by_z = [at(x, y, (z + k) % NZ, core) for k in range(1, NZ)]
    by_y = [at(x, (y + k) % NY, z, core) for k in range(1, NY)]
    by_region = [{"region": (region + k) % bands, "tile": tile} for k in range(1, bands)]

    def send(src, dst, ss, rs, dev):
        return pltpu.make_async_remote_copy(
            src_ref=src, dst_ref=dst, send_sem=ss, recv_sem=rs,
            device_id=dev, device_id_type=MESH,
        )

    barrier = pltpu.get_barrier_semaphore()
    partners = [west, east] + by_x + by_z + by_region
    for dev in partners:
        pl.semaphore_signal(barrier, inc=1, device_id=dev, device_id_type=MESH)
    loads[0].wait()
    loads[1].wait()

    sub = low4((1, 8, D))

    def halves(ref):
        v = ref[...].astype(F32)
        return v[:, :8, :], v[:, 8:, :]

    def pairs(v):
        v = v.reshape(8, 2, 8, D)
        return v[:, 0], v[:, 1]

    def rim_of(lo):
        even, odd = pairs(lo)
        return jnp.where(sub, even, roll4(odd)).reshape(64, D)

    x_lo, x_hi = halves(xv)
    rim_out[0] = rim_of(x_lo).astype(BF16)
    dy_lo, dy_hi = halves(dyv)
    rim_out[1] = rim_of(dy_lo).astype(BF16)

    pl.semaphore_wait(barrier, len(partners))
    rim = send(rim_out, rim_in, rim_sem.at[0], rim_sem.at[1], west)
    rim.start()

    lane_head = lax.broadcasted_iota(jnp.int32, (1, 128), 1) // HD
    head_masks = [(lane_head == h).astype(F32).astype(BF16) for h in range(4)]
    inv_root = HD ** -0.5

    def flags(b):
        return [mask_ref[a, b].astype(F32) for a in range(2)]

    def layer(b, feats, dys):
        rows = pl.ds(128 * b, 128)
        cols = slice(128 * b, 128 * b + 128)
        center = jnp.mean(feats, axis=-1, keepdims=True)
        dev = feats - center
        inv = lax.rsqrt(jnp.mean(dev * dev, axis=-1, keepdims=True) + 1e-05)
        hat = dev * inv
        xhat[rows, :] = hat
        istd[rows, :] = jnp.broadcast_to(inv, (128, 128))
        nb = hat.astype(BF16)
        proj = dot(nb, wq[...]).astype(BF16)
        f = flags(b)
        mk = jnp.concatenate([dys[:64] * f[0], dys[64:] * f[1]], axis=0).astype(BF16)
        masked[rows, :] = mk
        ga = dot(mk, wo[...], NT).astype(BF16)
        normed_t[:, cols] = nb.T

        units = [(a, g) for g in range(GROUPS) for a in range(2)]

        def part(array, a, first):
            return array[64 * a:64 * a + 64, first:first + 128]

        def spread(array, a):
            order = (1, 0, 3, 2) if a else (0, 1, 2, 3)
            return jnp.concatenate([array * head_masks[h] for h in order], axis=0)

        k = [part(proj, a, D + 128 * g) for a, g in units]
        v = [part(proj, a, 2 * D + 128 * g) for a, g in units]
        qbd = [spread(part(proj, a, 128 * g), a) for a, g in units]
        obd = [spread(part(ga, a, 128 * g), a) for a, g in units]
        s = [dot(m, n, NT) for m, n in zip(k, qbd)]
        dp = [dot(m, n, NT) for m, n in zip(v, obd)]
        kt = [m.T for m in k]
        vt = [m.T for m in v]
        p = []
        for t in s:
            e = jnp.exp2((t - jnp.max(t, axis=0, keepdims=True)) * (inv_root * LOG2E))
            p.append(e * (1.0 / jnp.sum(e, axis=0, keepdims=True)))
        pb = [t.astype(BF16) for t in p]
        ot = [dot(m, n) for m, n in zip(vt, pb)]
        first_half = lax.broadcasted_iota(jnp.int32, (1, 128), 1) < 64

        def own(zero, one):
            blocks = []
            for h in range(4):
                r, c = slice(32 * h, 32 * h + 32), slice(128 * (h // 2), 128 * (h // 2) + 128)
                if h % 2 == 0:
                    blocks.append(jnp.where(first_half, zero[r, c], one[r, c]))
                else:
                    blocks.append(pltpu.roll(jnp.where(first_half, one[r, c], zero[r, c]), 64, 1))
            return jnp.concatenate(blocks, axis=0).astype(BF16)

        for g in range(GROUPS):
            att_t[128 * g:128 * g + 128, cols] = own(ot[2 * g], ot[2 * g + 1])

        def backward(g):
            qt = []
            for a in range(2):
                i = 2 * g + a
                row = jnp.sum(dp[i] * p[i], axis=0, keepdims=True)
                ds = (p[i] * ((dp[i] - row) * inv_root)).astype(BF16)
                at_row = pl.ds(128 * b + 64 * a, 64)
                gp[at_row, D + 128 * g:D + 128 * g + 128] = dot(ds, qbd[i]).astype(BF16)
                gp[at_row, 2 * D + 128 * g:2 * D + 128 * g + 128] = dot(pb[i], obd[i]).astype(BF16)
                qt.append(dot(kt[i], ds))
            query_t[128 * g:128 * g + 128, cols] = own(qt[0], qt[1])

        return backward

    for c in loads[2:]:
        c.wait()
    backward = layer(
        0,
        jnp.where(sub, x_hi, x_lo).reshape(128, D),
        jnp.where(sub, dy_hi, dy_lo).reshape(128, D),
    )
    for g in range(GROUPS):
        backward(g)

    def local_of(hi):
        even, odd = pairs(hi)
        return jnp.where(sub, roll4(even), odd).reshape(64, D)

    x_loc, dy_loc = local_of(x_hi), local_of(dy_hi)
    rim.wait()

    def joined(loc, far):
        far = far.astype(F32)
        return jnp.concatenate([loc[:32], far[:32], loc[32:], far[32:]], axis=0)

    backward = layer(1, joined(x_loc, rim_in[0]), joined(dy_loc, rim_in[1]))

    nt = normed_t[...]
    ga_full = dot(att_t[...], masked[...]).reshape(16, 3, 8, D)
    w0, w1, w2 = ga_full[:, 0], ga_full[:, 1], ga_full[:, 2]
    spare = [
        roll4(jnp.where(sub, w0, w1)),
        jnp.where(sub, w2, w0),
        roll4(jnp.where(sub, w1, w2)),
    ]
    sends = []

    def start(c):
        c.start()
        sends.append(c)
        return c

    def swap_x(i):
        return start(send(
            gx.at[:, pl.ds((1 - core) * 4, 4), :, XCUT[i]], r0x.at[:, :, :, XCUT[i]],
            s0.at[i], q0.at[i], other,
        ))

    far_half = pl.ds((1 - core) * 2, 2)
    core0 = []
    for g in range(GROUPS):
        backward(g)
        gn = jnp.concatenate([
            dot(nt, query_t[128 * g:128 * g + 128, :], NT),
            dot(nt, gp[:, D + 128 * g:D + 128 * g + 128]),
            dot(nt, gp[:, 2 * D + 128 * g:2 * D + 128 * g + 128]),
        ], axis=1).reshape(16, 3, 8, D)
        v0, v1, v2 = gn[:, 0], gn[:, 1], gn[:, 2]
        packed = jnp.stack(
            [v0, jnp.where(sub, v1, spare[g]), v2, jnp.where(sub, spare[g], v1)], axis=1
        ).reshape(NX, NZ, 16, D).astype(BF16)
        if g == 0:
            gy[...] = packed
            core0.append(start(send(gy.at[far_half], r0y, s0.at[3], q0.at[3], other)))
        elif g == 1:
            gx[:, :, :, XCUT[0]] = packed
            core0.append(swap_x(0))
        else:
            gx[:, :, :, XCUT[1]] = packed[..., 0:128]
            gz[...] = packed[..., 128:384]
            core0.append(swap_x(1))
            core0.append(start(send(gz.at[far_half], r0z, s0.at[2], q0.at[2], other)))

    my_half = pl.ds(core * 2, 2)
    far_first = (4, 3, 5, 2, 6, 1, 7)
    core0[0].wait_recv()
    hy[...] = (gy[my_half].astype(F32) + r0y[...].astype(F32)).astype(BF16)
    p1y = [
        start(send(
            hy.at[:, (y + k) % NY], r1y.at[k - 1], s1y.at[k - 1], q1y.at[k - 1], by_y[k - 1],
        ))
        for k in far_first
    ]
    p1x = []
    for i in range(2):
        core0[1 + i].wait_recv()
        cut = XCUT[i]
        mine = gx[:, pl.ds(core * 4, 4), :, cut].astype(F32) + r0x[:, :, :, cut].astype(F32)
        hx[:, :, :, cut] = mine.astype(BF16)
        for k in (2, 1, 3):
            p1x.append(start(send(
                hx.at[(x + k) % NX, :, :, cut], r1x.at[k - 1, :, :, cut],
                s1x.at[i, k - 1], q1x.at[i, k - 1], by_x[k - 1],
            )))
    core0[3].wait_recv()
    hz[...] = (gz[my_half].astype(F32) + r0z[...].astype(F32)).astype(BF16)
    p1z = [
        start(send(
            hz.at[:, (z + k) % NZ], r1z.at[k - 1], s1z.at[k - 1], q1z.at[k - 1], by_z[k - 1],
        ))
        for k in far_first
    ]

    for b in range(2):
        gp[128 * b:128 * b + 128, 0:D] = query_t[:, 128 * b:128 * b + 128].T

    def branch_of(b):
        rows = pl.ds(128 * b, 128)
        gn = dot(gp[rows, :], wq[...], NT)
        hat = xhat[rows, :]
        inv = istd[rows, :][:, :1]
        m0 = jnp.mean(gn, axis=-1, keepdims=True)
        m1 = jnp.mean(gn * hat, axis=-1, keepdims=True)
        return (inv * (gn - m0 - hat * m1)).astype(BF16)

    br = branch_of(1)
    back_out[0:32, :] = br[32:64]
    back_out[32:64, :] = br[96:128]
    back = start(send(back_out, back_in, back_sem.at[0], back_sem.at[1], east))
    loc = jnp.concatenate([br[0:32], br[64:96]], axis=0).astype(F32).reshape(8, 8, D)
    branch[...] = branch_of(0).astype(F32)

    has_x = z // 4 == core
    has_z = x // 2 == core

    def total(first, buf, count):
        t = first.astype(F32)
        for i in range(count):
            t = t + buf[i].astype(F32)
        return t.astype(BF16)

    def second(buf, slots, ss, qs, devs, place, count, half):
        out = []
        for k in range(1, count):
            to = (place + k) % count
            c = send(buf.at[to % half], slots.at[k - 1], ss.at[k - 1], qs.at[k - 1], devs[k - 1])
            out.append((c, to // half == core))
        return out

    p2y = second(jy, r2y, s2y, q2y, by_x, x, NX, 2)
    p2x = second(jx, r2x, s2x, q2x, by_z, z, NZ, 4)
    p2z = second(jz, r2z, s2z, q2z, by_x, x, NX, 2)

    def start_if(copies):
        for c, yes in copies:
            pl.when(yes)(c.start)

    for c in p1x:
        c.wait_recv()
    jx[...] = total(hx[x], r1x, NX - 1)
    start_if(p2x)
    for c in p1y:
        c.wait_recv()
    jy[...] = total(hy[:, y], r1y, NY - 1)
    start_if(p2y)
    for c in p1z:
        c.wait_recv()
    jz[...] = total(hz[:, z], r1z, NZ - 1)
    start_if(p2z)

    p3y = [
        send(ky, r3y.at[k - 1], s3y.at[k - 1], q3y.at[k - 1], by_z[k - 1]) for k in range(1, NZ)
    ]

    @pl.when(has_z)
    def _():
        for c, _ in p2y:
            c.wait_recv()
        ky[...] = total(jy[x % 2], r2y, NX - 1)
        for k in range(1, NZ):
            pl.when((z + k) % NZ == y)(p3y[k - 1].start)

    def third(buf, slots, ss, qs, base, count):
        out = []
        for k in range(1, NY):
            to = (y + k) % NY
            yes = jnp.logical_and(to >= base, to < base + count)
            place = jnp.where(yes, to - base, 0)
            c = send(buf.at[place], slots.at[k - 1], ss.at[k - 1], qs.at[k - 1], by_y[k - 1])
            out.append((c, yes))
        return out

    p3x = third(kx, r3x, s3x, q3x, 0, TX)
    p3z = third(kz, r3z, s3z, q3z, TX, TZ)

    @pl.when(has_x)
    def _():
        for c, _ in p2x:
            c.wait_recv()
        t = total(jx[z % 4], r2x, NZ - 1)
        for i in range(TX):
            kx[i] = t[:, 128 * i:128 * i + 128]
        start_if(p3x)

    @pl.when(has_z)
    def _():
        for c, _ in p2z:
            c.wait_recv()
        t = total(jz[x % 2], r2z, NX - 1)
        for i in range(TZ):
            kz[i] = t[:, 128 * i:128 * i + 128]
        start_if(p3z)

    own_y = jnp.logical_and(has_z, y == z)
    own_x = jnp.logical_and(has_x, y < TX)
    own_z = jnp.logical_and(has_z, jnp.logical_and(y >= TX, y < TX + TZ))
    mine_x = jnp.where(own_x, y, 0)
    mine_z = jnp.where(own_z, y, TX)
    p4y = [
        send(last_in, last_in, s4y.at[k], q4y, dev) for k, dev in enumerate(by_region)
    ]
    p4x = [
        send(tiles_in.at[mine_x], tiles_in.at[mine_x], s4x.at[k], q4.at[mine_x], dev)
        for k, dev in enumerate(by_region)
    ]
    p4z = [
        send(tiles_in.at[mine_z], tiles_in.at[mine_z], s4z.at[k], q4.at[mine_z], dev)
        for k, dev in enumerate(by_region)
    ]

    @pl.when(own_y)
    def _():
        for c in p3y:
            c.wait_recv()
        last_in[...] = total(ky[...], r3y, NZ - 1)
        for c in p4y:
            c.start()

    @pl.when(own_x)
    def _():
        for c, _ in p3x:
            c.wait_recv()
        tiles_in[mine_x] = total(kx[mine_x], r3x, NY - 1)
        for c in p4x:
            c.start()

    @pl.when(own_z)
    def _():
        for c, _ in p3z:
            c.wait_recv()
        tiles_in[mine_z] = total(kz[mine_z - TX], r3z, NY - 1)
        for c in p4z:
            c.start()

    back.wait_recv()
    far = back_in[...].astype(F32).reshape(8, 8, D)
    br0 = branch[...].reshape(16, 8, D)

    def unpaired(even, odd):
        return jnp.stack([even, odd], axis=1).reshape(16, 8, D)

    new_lo = dyv[:, :8, :].astype(F32) + jnp.where(sub, unpaired(far, roll4(far)), br0)
    new_hi = dyv[:, 8:, :].astype(F32) + jnp.where(sub, br0, unpaired(roll4(loc), loc))
    out_ref[...] = jnp.concatenate([new_lo, new_hi], axis=1).astype(BF16)

    def arrive(owner, c):
        pl.when(jnp.logical_not(owner))(c.wait_recv)

    arrive(own_y, p4y[0])
    for i in range(TX + TZ):
        mine = jnp.logical_and(own_x if i < TX else own_z, y == i)
        arrive(mine, send(tiles_in.at[i], tiles_in.at[i], s4x.at[0], q4.at[i], other))

    scale = 1.0 / math.sqrt(3 * 64 * 2 * NY * tiles)
    odd = (z % 2) == 1
    final = jnp.concatenate(
        [last_in[...]] + [tiles_in[i] for i in range(TX + TZ)], axis=1
    ).astype(F32) * scale
    for g in range(GROUPS):
        f = final[:, D * g:D * g + D]
        top, bot = f[0:8], f[8:16]
        top_r, bot_r = pltpu.roll(top, 4, 0), pltpu.roll(bot, 4, 0)
        low = low4((8, D))
        first = jnp.where(odd, jnp.where(low, bot_r, top_r), top)
        rest = jnp.where(odd, top_r, bot)
        extra = jnp.where(odd, bot, bot_r)
        for s in range(3):
            lanes = slice(s * D + 128 * g, s * D + 128 * g + 128)
            gq_ref[0:8, lanes] = first[:, 128 * s:128 * s + 128]
            gq_ref[8:12, lanes] = rest[0:4, 128 * s:128 * s + 128]
        go_ref[4 * g:4 * g + 4, :] = extra[0:4]

    for c in sends:
        c.wait_send()
    for c, yes in p2x + p2y + p2z:
        pl.when(yes)(c.wait_send)

    @pl.when(has_x)
    def _():
        for c, yes in p3x:
            pl.when(yes)(c.wait_send)

    @pl.when(has_z)
    def _():
        for k in range(1, NZ):
            pl.when((z + k) % NZ == y)(p3y[k - 1].wait_send)
        for c, yes in p3z:
            pl.when(yes)(c.wait_send)

    for owner, copies in ((own_y, p4y), (own_x, p4x), (own_z, p4z)):
        @pl.when(owner)
        def _():
            for c in copies:
                c.wait_send()


def hand_over(a, b, c, a_out, b_out, c_out, sems):
    copies = [
        pltpu.make_async_copy(src, dst, sems.at[i])
        for i, (src, dst) in enumerate(((a, a_out), (b, b_out), (c, c_out)))
    ]
    for c in copies:
        c.start()
    for c in copies:
        c.wait()


def body(tokens, grad_out, ocean_mask, w_qkv, w_out):
    any_spec = pl.BlockSpec(memory_space=pl.ANY)
    vmem_spec = pl.BlockSpec(memory_space=pltpu.VMEM)
    hbm_spec = pl.BlockSpec(memory_space=pltpu.HBM)

    def buf(*shape, dtype=BF16):
        return pltpu.VMEM(shape, dtype)

    def sem(*shape):
        return pltpu.SemaphoreType.DMA(shape)

    results = pl.pallas_call(
        kernel,
        out_shape=(
            pltpu.VMEM((16, 16, D), BF16),
            pltpu.VMEM((12, 3 * D), F32),
            pltpu.VMEM((12, D), F32),
        ),
        in_specs=[hbm_spec] * 5,
        out_specs=(vmem_spec, vmem_spec, vmem_spec),
        scratch_shapes=[
            buf(16, 16, D), buf(16, 16, D), pltpu.SMEM((2, 2), jnp.int32),
            buf(D, 3 * D), buf(D, D),
            buf(2, 64, D), buf(2, 64, D), buf(64, D), buf(64, D),
            buf(D, 256), buf(256, D), buf(D, 256), buf(D, 256), buf(256, 3 * D),
            buf(256, D, dtype=F32), buf(256, 128, dtype=F32), buf(128, D, dtype=F32),
            buf(NX, NZ, 16, WX), buf(NX, NZ, 16, WY), buf(NX, NZ, 16, WZ),
            buf(NX, 4, 16, WX), buf(2, NZ, 16, WY), buf(2, NZ, 16, WZ),
            buf(NX, 4, 16, WX), buf(2, NZ, 16, WY), buf(2, NZ, 16, WZ),
            buf(NX - 1, 4, 16, WX), buf(NY - 1, 2, 16, WY), buf(NZ - 1, 2, 16, WZ),
            buf(4, 16, WX), buf(2, 16, WY), buf(2, 16, WZ),
            buf(NZ - 1, 16, WX), buf(NX - 1, 16, WY), buf(NX - 1, 16, WZ),
            buf(TX, 16, 128), buf(16, WY), buf(TZ, 16, 128),
            buf(NY - 1, 16, 128), buf(NZ - 1, 16, WY), buf(NY - 1, 16, 128),
            buf(TX + TZ, 16, 128), buf(16, WY),
            sem(5), sem(2), sem(2),
            sem(4), sem(4), sem(2, NX - 1), sem(2, NX - 1),
            sem(NY - 1), sem(NY - 1), sem(NZ - 1), sem(NZ - 1),
            sem(NZ - 1), sem(NZ - 1), sem(NX - 1), sem(NX - 1), sem(NX - 1), sem(NX - 1),
            sem(NY - 1), sem(NY - 1), sem(NZ - 1), sem(NZ - 1), sem(NY - 1), sem(NY - 1),
            sem(2 * NY - 1), sem(2 * NY - 1), sem(2 * NY - 1), sem(TX + TZ), pltpu.SemaphoreType.DMA,
        ],
        compiler_params=pltpu.CompilerParams(
            collective_id=0, has_side_effects=True, vmem_limit_bytes=58 * 1024 * 1024
        ),
        cost_estimate=pl.CostEstimate(
            flops=900_000_000, bytes_accessed=2_000_000, transcendentals=200_000
        ),
        name="window_grads",
    )(tokens, grad_out, ocean_mask, w_qkv, w_out)
    return pl.pallas_call(
        hand_over,
        out_shape=[jax.ShapeDtypeStruct(r.shape, r.dtype) for r in results],
        in_specs=[any_spec] * 3,
        out_specs=[any_spec] * 3,
        scratch_shapes=[sem(3)],
        cost_estimate=pl.CostEstimate(flops=0, bytes_accessed=600_000, transcendentals=0),
        name="hand_over",
    )(*results)


def solution(mesh):
    return jax.shard_map(
        body,
        mesh=mesh,
        in_specs=(
            P("region", "tile", None),
            P("region", "tile", None),
            P("region", "tile"),
            P(),
            P(),
        ),
        out_specs=(P("region", "tile", None), P("tile", None), P("tile", None)),
        check_vma=False,
    )
```

```python
import math

import jax
import jax.numpy as jnp
from jax import lax
from jax.experimental import pallas as pl
from jax.experimental.pallas import tpu as pltpu
from jax.sharding import PartitionSpec as P

MESH = pl.DeviceIdType.MESH
F32 = jnp.float32
BF16 = jnp.bfloat16
D = 384
HD = 32
LOG2E = math.log2(math.e)
GROUPS = 3
NX, NZ, NY = 4, 8, 8
TX, TZ = 4, 2
WY, WX, WZ = 384, 128 * TX, 128 * TZ
XCUT = (slice(0, 384), slice(384, 512))
NT = (((1,), (1,)), ((), ()))


def dot(a, b, dims=(((1,), (0,)), ((), ()))):
    return lax.dot_general(a, b, dims, preferred_element_type=F32)


def roll4(a):
    n, _, width = a.shape
    return pltpu.roll(a.reshape(n * 8, width).reshape(n, 8, width), 4, 1)


def low4(shape):
    return lax.broadcasted_iota(jnp.int32, shape, len(shape) - 2) % 8 < 4


def layer(feats, mk, wq, wo, refs):
    normed_t, masked, att_t, query_t, gp, xhat, istd = refs
    lane_head = lax.broadcasted_iota(jnp.int32, (1, 128), 1) // HD
    head_masks = [(lane_head == h).astype(F32).astype(BF16) for h in range(4)]
    inv_root = HD ** -0.5
    center = jnp.mean(feats, axis=-1, keepdims=True)
    dev = feats - center
    inv = lax.rsqrt(jnp.mean(dev * dev, axis=-1, keepdims=True) + 1e-05)
    hat = dev * inv
    xhat[...] = hat
    istd[...] = jnp.broadcast_to(inv, (128, 128))
    nb = hat.astype(BF16)
    proj = dot(nb, wq[...]).astype(BF16)
    if masked is not None:
        masked[...] = mk
    ga = dot(mk, wo[...], NT).astype(BF16)
    normed_t[...] = nb.T

    units = [(a, g) for g in range(GROUPS) for a in range(2)]

    def part(array, a, first):
        return array[64 * a:64 * a + 64, first:first + 128]

    def spread(array, a):
        order = (1, 0, 3, 2) if a else (0, 1, 2, 3)
        return jnp.concatenate([array * head_masks[h] for h in order], axis=0)

    k = [part(proj, a, D + 128 * g) for a, g in units]
    v = [part(proj, a, 2 * D + 128 * g) for a, g in units]
    qbd = [spread(part(proj, a, 128 * g), a) for a, g in units]
    obd = [spread(part(ga, a, 128 * g), a) for a, g in units]
    s = [dot(m, n, NT) for m, n in zip(k, qbd)]
    dp = [dot(m, n, NT) for m, n in zip(v, obd)]
    kt = [m.T for m in k]
    vt = [m.T for m in v]
    p = []
    for t in s:
        e = jnp.exp2((t - jnp.max(t, axis=0, keepdims=True)) * (inv_root * LOG2E))
        p.append(e * (1.0 / jnp.sum(e, axis=0, keepdims=True)))
    pb = [t.astype(BF16) for t in p]
    ot = [dot(m, n) for m, n in zip(vt, pb)]
    first_half = lax.broadcasted_iota(jnp.int32, (1, 128), 1) < 64

    def own(zero, one):
        blocks = []
        for h in range(4):
            r, c = slice(32 * h, 32 * h + 32), slice(128 * (h // 2), 128 * (h // 2) + 128)
            if h % 2 == 0:
                blocks.append(jnp.where(first_half, zero[r, c], one[r, c]))
            else:
                blocks.append(pltpu.roll(jnp.where(first_half, one[r, c], zero[r, c]), 64, 1))
        return jnp.concatenate(blocks, axis=0).astype(BF16)

    for g in range(GROUPS):
        att_t[128 * g:128 * g + 128, :] = own(ot[2 * g], ot[2 * g + 1])

    def backward(g):
        qt = []
        for a in range(2):
            i = 2 * g + a
            row = jnp.sum(dp[i] * p[i], axis=0, keepdims=True)
            ds = (p[i] * ((dp[i] - row) * inv_root)).astype(BF16)
            at_row = pl.ds(64 * a, 64)
            gp[at_row, 128 * g:128 * g + 128] = dot(ds, qbd[i]).astype(BF16)
            gp[at_row, D + 128 * g:D + 128 * g + 128] = dot(pb[i], obd[i]).astype(BF16)
            qt.append(dot(kt[i], ds))
        query_t[128 * g:128 * g + 128, :] = own(qt[0], qt[1])

    return backward


def device():
    region, tile = lax.axis_index("region"), lax.axis_index("tile")
    tiles = NX * NZ
    west = {"region": region, "tile": (tile + tiles - 1) % tiles}
    east = {"region": region, "tile": (tile + 1) % tiles}
    return region, tile, west, east


def send(src, dst, ss, rs, dev):
    return pltpu.make_async_remote_copy(
        src_ref=src, dst_ref=dst, send_sem=ss, recv_sem=rs, device_id=dev, device_id_type=MESH,
    )


def greet(partners):
    barrier = pltpu.get_barrier_semaphore()
    for dev in partners:
        pl.semaphore_signal(barrier, inc=1, device_id=dev, device_id_type=MESH)
    return lambda: pl.semaphore_wait(barrier, len(partners))


def pairs(v):
    v = v.reshape(8, 2, 8, D)
    return v[:, 0], v[:, 1]


def first_column(
    x_hbm, dy_hbm, mask_hbm, wq_hbm, wo_hbm,
    wq, wo, feats1, masked1, normed_t, masked, att_t, query_t, gp, xhat, istd,
    xv, dyv, mask_ref, rim_out, rim_in, in_sem, rim_sem,
):
    loads = [
        pltpu.make_async_copy(src, dst, in_sem.at[i])
        for i, (src, dst) in enumerate(
            ((x_hbm, xv), (dy_hbm, dyv), (wq_hbm, wq), (wo_hbm, wo), (mask_hbm, mask_ref))
        )
    ]
    for c in loads:
        c.start()
    _, _, west, east = device()
    greeted = greet([west, east])
    loads[0].wait()
    loads[1].wait()
    sub = low4((1, 8, D))

    def halves(ref):
        v = ref[...].astype(F32)
        return v[:, :8, :], v[:, 8:, :]

    def rim_of(lo):
        even, odd = pairs(lo)
        return jnp.where(sub, even, roll4(odd)).reshape(64, D)

    x_lo, x_hi = halves(xv)
    rim_out[0] = rim_of(x_lo).astype(BF16)
    dy_lo, dy_hi = halves(dyv)
    rim_out[1] = rim_of(dy_lo).astype(BF16)
    greeted()
    rim = send(rim_out, rim_in, rim_sem.at[0], rim_sem.at[1], west)
    rim.start()

    for c in loads[2:]:
        c.wait()
    flag = [[mask_ref[a, b].astype(F32) for a in range(2)] for b in range(2)]

    def mask_of(dys, b):
        return jnp.concatenate([dys[:64] * flag[b][0], dys[64:] * flag[b][1]], axis=0).astype(BF16)

    backward = layer(
        jnp.where(sub, x_hi, x_lo).reshape(128, D),
        mask_of(jnp.where(sub, dy_hi, dy_lo).reshape(128, D), 0),
        wq, wo, (normed_t, masked, att_t, query_t, gp, xhat, istd),
    )
    for g in range(GROUPS):
        backward(g)

    def joined(hi, far):
        even, odd = pairs(hi)
        loc = jnp.where(sub, roll4(even), odd).reshape(64, D)
        far = far.astype(F32)
        return jnp.concatenate([loc[:32], far[:32], loc[32:], far[32:]], axis=0)

    rim.wait()
    feats1[...] = joined(x_hi, rim_in[0]).astype(BF16)
    masked1[...] = mask_of(joined(dy_hi, rim_in[1]), 1)


def second_column(
    dy_hbm, wq, wo, feats1, masked1, normed_t0, masked0, att_t0, query_t0, gp0, xhat0, istd0,
    out_ref, gq_ref, go_ref,
    dyv, back_out, back_in,
    normed_t1, att_t1, query_t1, gp1, xhat1, istd1, branch,
    gx, gy, gz, r0x, r0y, r0z, hx, hy, hz, r1x, r1y, r1z, jx, jy, jz,
    r2x, r2y, r2z, kx, ky, kz, r3x, r3y, r3z, tiles_in, last_in,
    in_sem, back_sem,
    s0, q0, s1x, q1x, s1y, q1y, s1z, q1z, s2x, q2x, s2y, q2y, s2z, q2z,
    s3x, q3x, s3y, q3y, s3z, q3z, s4, q4, q4y,
):
    load = pltpu.make_async_copy(dy_hbm, dyv, in_sem)
    load.start()
    region, tile, west, east = device()
    y, core = region // 2, region % 2
    x, z = tile // NZ, tile % NZ
    tiles, bands = NX * NZ, 2 * NY

    def at(ax, ay, az, ac):
        return {"region": ay * 2 + ac, "tile": ax * NZ + az}

    other = at(x, y, z, 1 - core)
    by_x = [at((x + k) % NX, y, z, core) for k in range(1, NX)]
    by_z = [at(x, y, (z + k) % NZ, core) for k in range(1, NZ)]
    by_y = [at(x, (y + k) % NY, z, core) for k in range(1, NY)]
    by_region = [{"region": (region + k) % bands, "tile": tile} for k in range(1, bands)]
    greeted = greet([west, east] + by_x + by_z + by_region)
    sub = low4((1, 8, D))
    backward = layer(
        feats1[...].astype(F32), masked1[...], wq, wo,
        (normed_t1, None, att_t1, query_t1, gp1, xhat1, istd1),
    )

    def both(a, b, axis):
        return jnp.concatenate([a, b], axis=axis)

    nt = both(normed_t0[...], normed_t1[...], 1)
    ga_full = dot(
        both(att_t0[...], att_t1[...], 1), both(masked0[...], masked1[...], 0)
    ).reshape(16, 3, 8, D)
    w0, w1, w2 = ga_full[:, 0], ga_full[:, 1], ga_full[:, 2]
    spare = [
        roll4(jnp.where(sub, w0, w1)),
        jnp.where(sub, w2, w0),
        roll4(jnp.where(sub, w1, w2)),
    ]
    sends = []

    def start(c):
        c.start()
        sends.append(c)
        return c

    def swap_x(i):
        return start(send(
            gx.at[:, pl.ds((1 - core) * 4, 4), :, XCUT[i]], r0x.at[:, :, :, XCUT[i]],
            s0.at[i], q0.at[i], other,
        ))

    far_half = pl.ds((1 - core) * 2, 2)
    core0 = []
    for g in range(GROUPS):
        backward(g)
        at_g = slice(128 * g, 128 * g + 128)
        at_gv = slice(D + 128 * g, D + 128 * g + 128)
        if g == 0:
            greeted()
        gn = jnp.concatenate([
            dot(nt, both(query_t0[at_g, :], query_t1[at_g, :], 1), NT),
            dot(nt, both(gp0[:, at_g], gp1[:, at_g], 0)),
            dot(nt, both(gp0[:, at_gv], gp1[:, at_gv], 0)),
        ], axis=1).reshape(16, 3, 8, D)
        v0, v1, v2 = gn[:, 0], gn[:, 1], gn[:, 2]
        packed = jnp.stack(
            [v0, jnp.where(sub, v1, spare[g]), v2, jnp.where(sub, spare[g], v1)], axis=1
        ).reshape(NX, NZ, 16, D).astype(BF16)
        if g == 0:
            gy[...] = packed
            core0.append(start(send(gy.at[far_half], r0y, s0.at[3], q0.at[3], other)))
        elif g == 1:
            gx[:, :, :, XCUT[0]] = packed
            core0.append(swap_x(0))
        else:
            gx[:, :, :, XCUT[1]] = packed[..., 0:128]
            gz[...] = packed[..., 128:384]
            core0.append(swap_x(1))
            core0.append(start(send(gz.at[far_half], r0z, s0.at[2], q0.at[2], other)))

    my_half = pl.ds(core * 2, 2)
    far_first = (4, 3, 5, 2, 6, 1, 7)
    core0[0].wait_recv()
    hy[...] = (gy[my_half].astype(F32) + r0y[...].astype(F32)).astype(BF16)
    p1y = [
        start(send(
            hy.at[:, (y + k) % NY], r1y.at[k - 1], s1y.at[k - 1], q1y.at[k - 1], by_y[k - 1],
        ))
        for k in far_first
    ]
    p1x = []
    for i in range(2):
        core0[1 + i].wait_recv()
        cut = XCUT[i]
        mine = gx[:, pl.ds(core * 4, 4), :, cut].astype(F32) + r0x[:, :, :, cut].astype(F32)
        hx[:, :, :, cut] = mine.astype(BF16)
        for k in (2, 1, 3):
            p1x.append(start(send(
                hx.at[(x + k) % NX, :, :, cut], r1x.at[k - 1, :, :, cut],
                s1x.at[i, k - 1], q1x.at[i, k - 1], by_x[k - 1],
            )))
    core0[3].wait_recv()
    hz[...] = (gz[my_half].astype(F32) + r0z[...].astype(F32)).astype(BF16)
    p1z = [
        start(send(
            hz.at[:, (z + k) % NZ], r1z.at[k - 1], s1z.at[k - 1], q1z.at[k - 1], by_z[k - 1],
        ))
        for k in far_first
    ]

    def branch_of(query_t, gp, xhat, istd):
        gn = dot(query_t[...].T, wq[:, 0:D], NT) + dot(gp[...], wq[:, D:3 * D], NT)
        hat = xhat[...]
        inv = istd[:, 0:1]
        m0 = jnp.mean(gn, axis=-1, keepdims=True)
        m1 = jnp.mean(gn * hat, axis=-1, keepdims=True)
        return (inv * (gn - m0 - hat * m1)).astype(BF16)

    br = branch_of(query_t1, gp1, xhat1, istd1)
    back_out[0:32, :] = br[32:64]
    back_out[32:64, :] = br[96:128]
    back = start(send(back_out, back_in, back_sem.at[0], back_sem.at[1], east))
    loc = jnp.concatenate([br[0:32], br[64:96]], axis=0).astype(F32).reshape(8, 8, D)
    branch[...] = branch_of(query_t0, gp0, xhat0, istd0).astype(F32)

    has_x = z // 4 == core
    has_z = x // 2 == core

    def total(first, buf, count):
        t = first.astype(F32)
        for i in range(count):
            t = t + buf[i].astype(F32)
        return t.astype(BF16)

    def second(buf, slots, ss, qs, devs, place, count, half):
        out = []
        for k in range(1, count):
            to = (place + k) % count
            c = send(buf.at[to % half], slots.at[k - 1], ss.at[k - 1], qs.at[k - 1], devs[k - 1])
            out.append((c, to // half == core))
        return out

    p2y = second(jy, r2y, s2y, q2y, by_x, x, NX, 2)
    p2x = second(jx, r2x, s2x, q2x, by_z, z, NZ, 4)
    p2z = second(jz, r2z, s2z, q2z, by_x, x, NX, 2)

    def start_if(copies):
        for c, yes in copies:
            pl.when(yes)(c.start)

    for c in p1x:
        c.wait_recv()
    jx[...] = total(hx[x], r1x, NX - 1)
    start_if(p2x)
    for c in p1y:
        c.wait_recv()
    jy[...] = total(hy[:, y], r1y, NY - 1)
    start_if(p2y)
    for c in p1z:
        c.wait_recv()
    jz[...] = total(hz[:, z], r1z, NZ - 1)
    start_if(p2z)

    p3y = [
        send(ky, r3y.at[k - 1], s3y.at[k - 1], q3y.at[k - 1], by_z[k - 1]) for k in range(1, NZ)
    ]

    @pl.when(has_z)
    def _():
        for c, _ in p2y:
            c.wait_recv()
        ky[...] = total(jy[x % 2], r2y, NX - 1)
        for k in range(1, NZ):
            pl.when((z + k) % NZ == y)(p3y[k - 1].start)

    def third(buf, slots, ss, qs, base, count):
        out = []
        for k in range(1, NY):
            place = (y + k - z - 1 - base + 2 * NY) % NY
            yes = place < count
            c = send(
                buf.at[jnp.where(yes, place, 0)], slots.at[k - 1],
                ss.at[k - 1], qs.at[k - 1], by_y[k - 1],
            )
            out.append((c, yes))
        return out

    p3x = third(kx, r3x, s3x, q3x, 0, TX)
    p3z = third(kz, r3z, s3z, q3z, TX, TZ)

    @pl.when(has_x)
    def _():
        for c, _ in p2x:
            c.wait_recv()
        t = total(jx[z % 4], r2x, NZ - 1)
        for i in range(TX):
            kx[i] = t[:, 128 * i:128 * i + 128]
        start_if(p3x)

    @pl.when(has_z)
    def _():
        for c, _ in p2z:
            c.wait_recv()
        t = total(jz[x % 2], r2z, NX - 1)
        for i in range(TZ):
            kz[i] = t[:, 128 * i:128 * i + 128]
        start_if(p3z)

    slot = (y - z - 1 + NY) % NY
    own_y = jnp.logical_and(has_z, slot == NY - 1)
    own_x = jnp.logical_and(has_x, slot < TX)
    own_z = jnp.logical_and(has_z, jnp.logical_and(slot >= TX, slot < TX + TZ))
    mine = jnp.minimum(slot, TX + TZ - 1)
    p4y = [send(last_in, last_in, s4.at[k], q4y, dev) for k, dev in enumerate(by_region)]
    p4 = [
        send(tiles_in.at[mine], tiles_in.at[mine], s4.at[k], q4.at[mine], dev)
        for k, dev in enumerate(by_region)
    ]

    @pl.when(own_y)
    def _():
        for c in p3y:
            c.wait_recv()
        last_in[...] = total(ky[...], r3y, NZ - 1)
        for c in p4y:
            c.start()

    @pl.when(own_x)
    def _():
        for c, _ in p3x:
            c.wait_recv()
        tiles_in[mine] = total(kx[jnp.minimum(slot, TX - 1)], r3x, NY - 1)
        for c in p4:
            c.start()

    @pl.when(own_z)
    def _():
        for c, _ in p3z:
            c.wait_recv()
        tiles_in[mine] = total(kz[jnp.clip(slot - TX, 0, TZ - 1)], r3z, NY - 1)
        for c in p4:
            c.start()

    back.wait_recv()
    load.wait()
    far = back_in[...].astype(F32).reshape(8, 8, D)
    br0 = branch[...].reshape(16, 8, D)

    def unpaired(even, odd):
        return jnp.stack([even, odd], axis=1).reshape(16, 8, D)

    new_lo = dyv[:, :8, :].astype(F32) + jnp.where(sub, unpaired(far, roll4(far)), br0)
    new_hi = dyv[:, 8:, :].astype(F32) + jnp.where(sub, br0, unpaired(roll4(loc), loc))
    out_ref[...] = jnp.concatenate([new_lo, new_hi], axis=1).astype(BF16)

    def arrive(owner, c):
        pl.when(jnp.logical_not(owner))(c.wait_recv)

    arrive(own_y, p4y[0])
    for i in range(TX + TZ):
        here = jnp.logical_and(own_x if i < TX else own_z, slot == i)
        arrive(here, send(tiles_in.at[i], tiles_in.at[i], s4.at[0], q4.at[i], other))

    scale = 1.0 / math.sqrt(3 * 64 * 2 * NY * tiles)
    odd = (z % 2) == 1
    final = jnp.concatenate(
        [last_in[...]] + [tiles_in[i] for i in range(TX + TZ)], axis=1
    ).astype(F32) * scale
    for g in range(GROUPS):
        f = final[:, D * g:D * g + D]
        top, bot = f[0:8], f[8:16]
        top_r, bot_r = pltpu.roll(top, 4, 0), pltpu.roll(bot, 4, 0)
        low = low4((8, D))
        first = jnp.where(odd, jnp.where(low, bot_r, top_r), top)
        rest = jnp.where(odd, top_r, bot)
        extra = jnp.where(odd, bot, bot_r)
        for s in range(3):
            lanes = slice(s * D + 128 * g, s * D + 128 * g + 128)
            gq_ref[0:8, lanes] = first[:, 128 * s:128 * s + 128]
            gq_ref[8:12, lanes] = rest[0:4, 128 * s:128 * s + 128]
        go_ref[4 * g:4 * g + 4, :] = extra[0:4]

    for c in sends:
        c.wait_send()
    for c, yes in p2x + p2y + p2z:
        pl.when(yes)(c.wait_send)

    @pl.when(has_x)
    def _():
        for c, yes in p3x:
            pl.when(yes)(c.wait_send)

    @pl.when(has_z)
    def _():
        for k in range(1, NZ):
            pl.when((z + k) % NZ == y)(p3y[k - 1].wait_send)
        for c, yes in p3z:
            pl.when(yes)(c.wait_send)

    for owner, copies in ((own_y, p4y), (jnp.logical_or(own_x, own_z), p4)):
        @pl.when(owner)
        def _():
            for c in copies:
                c.wait_send()


def hand_over(a, b, c, a_out, b_out, c_out, sems):
    copies = [
        pltpu.make_async_copy(src, dst, sems.at[i])
        for i, (src, dst) in enumerate(((a, a_out), (b, b_out), (c, c_out)))
    ]
    for c in copies:
        c.start()
    for c in copies:
        c.wait()


def body(tokens, grad_out, ocean_mask, w_qkv, w_out):
    any_spec = pl.BlockSpec(memory_space=pl.ANY)
    vmem_spec = pl.BlockSpec(memory_space=pltpu.VMEM)

    def buf(*shape, dtype=BF16):
        return pltpu.VMEM(shape, dtype)

    def sem(*shape):
        return pltpu.SemaphoreType.DMA(shape)

    def params(collective, mib):
        return pltpu.CompilerParams(
            collective_id=collective, has_side_effects=True, vmem_limit_bytes=mib * 1024 * 1024
        )

    column = [
        buf(D, 128), buf(128, D), buf(D, 128), buf(D, 128), buf(128, 2 * D),
        buf(128, D, dtype=F32), buf(128, 128, dtype=F32),
    ]
    handed = [buf(D, 3 * D), buf(D, D), buf(128, D), buf(128, D)] + column
    first = pl.pallas_call(
        first_column,
        out_shape=handed,
        in_specs=[any_spec] * 5,
        out_specs=[vmem_spec] * len(handed),
        scratch_shapes=[
            buf(16, 16, D), buf(16, 16, D), pltpu.SMEM((2, 2), jnp.int32),
            buf(2, 64, D), buf(2, 64, D), sem(5), sem(2),
        ],
        compiler_params=params(0, 56),
        cost_estimate=pl.CostEstimate(
            flops=300_000_000, bytes_accessed=2_000_000, transcendentals=100_000
        ),
        name="first_column",
    )(tokens, grad_out, ocean_mask, w_qkv, w_out)
    results = pl.pallas_call(
        second_column,
        out_shape=(buf(16, 16, D), buf(12, 3 * D, dtype=F32), buf(12, D, dtype=F32)),
        in_specs=[any_spec] + [vmem_spec] * len(handed),
        out_specs=(vmem_spec, vmem_spec, vmem_spec),
        scratch_shapes=[
            buf(16, 16, D), buf(64, D), buf(64, D),
            column[0], column[2], column[3], column[4], column[5], column[6],
            buf(128, D, dtype=F32),
            buf(NX, NZ, 16, WX), buf(NX, NZ, 16, WY), buf(NX, NZ, 16, WZ),
            buf(NX, 4, 16, WX), buf(2, NZ, 16, WY), buf(2, NZ, 16, WZ),
            buf(NX, 4, 16, WX), buf(2, NZ, 16, WY), buf(2, NZ, 16, WZ),
            buf(NX - 1, 4, 16, WX), buf(NY - 1, 2, 16, WY), buf(NZ - 1, 2, 16, WZ),
            buf(4, 16, WX), buf(2, 16, WY), buf(2, 16, WZ),
            buf(NZ - 1, 16, WX), buf(NX - 1, 16, WY), buf(NX - 1, 16, WZ),
            buf(TX, 16, 128), buf(16, WY), buf(TZ, 16, 128),
            buf(NY - 1, 16, 128), buf(NZ - 1, 16, WY), buf(NY - 1, 16, 128),
            buf(TX + TZ, 16, 128), buf(16, WY),
            pltpu.SemaphoreType.DMA, sem(2),
            sem(4), sem(4), sem(2, NX - 1), sem(2, NX - 1),
            sem(NY - 1), sem(NY - 1), sem(NZ - 1), sem(NZ - 1),
            sem(NZ - 1), sem(NZ - 1), sem(NX - 1), sem(NX - 1), sem(NX - 1), sem(NX - 1),
            sem(NY - 1), sem(NY - 1), sem(NZ - 1), sem(NZ - 1), sem(NY - 1), sem(NY - 1),
            sem(2 * NY - 1), sem(TX + TZ), pltpu.SemaphoreType.DMA,
        ],
        compiler_params=params(1, 24),
        cost_estimate=pl.CostEstimate(
            flops=600_000_000, bytes_accessed=1_000_000, transcendentals=100_000
        ),
        name="second_column",
    )(grad_out, *first)
    return pl.pallas_call(
        hand_over,
        out_shape=[jax.ShapeDtypeStruct(r.shape, r.dtype) for r in results],
        in_specs=[any_spec] * 3,
        out_specs=[any_spec] * 3,
        scratch_shapes=[sem(3)],
        compiler_params=pltpu.CompilerParams(vmem_limit_bytes=4 * 1024 * 1024),
        cost_estimate=pl.CostEstimate(flops=0, bytes_accessed=600_000, transcendentals=0),
        name="hand_over",
    )(*results)


def solution(mesh):
    return jax.shard_map(
        body,
        mesh=mesh,
        in_specs=(
            P("region", "tile", None),
            P("region", "tile", None),
            P("region", "tile"),
            P(),
            P(),
        ),
        out_specs=(P("region", "tile", None), P("tile", None), P("tile", None)),
        check_vma=False,
    )
```

```python
import math

import jax
import jax.numpy as jnp
from jax import lax
from jax.experimental import pallas as pl
from jax.experimental.pallas import tpu as pltpu
from jax.sharding import PartitionSpec as P

MESH = pl.DeviceIdType.MESH
F32 = jnp.float32
BF16 = jnp.bfloat16
D = 384
HD = 32
LOG2E = math.log2(math.e)
GROUPS = 3
NX, NZ, NY = 4, 8, 8
WX, WZ = 640, 512
XCUT = (slice(0, 384), slice(384, 640))
NT = (((1,), (1,)), ((), ()))


def dot(a, b, dims=(((1,), (0,)), ((), ()))):
    return lax.dot_general(a, b, dims, preferred_element_type=F32)


def roll4(a):
    n, _, width = a.shape
    return pltpu.roll(a.reshape(n * 8, width).reshape(n, 8, width), 4, 1)


def low4(shape):
    return lax.broadcasted_iota(jnp.int32, shape, len(shape) - 2) % 8 < 4


def part(array, a, first):
    return array[64 * a:64 * a + 64, first:first + 128]


def spread(array, a):
    lane_head = lax.broadcasted_iota(jnp.int32, (1, 128), 1) // HD
    order = (1, 0, 3, 2) if a else (0, 1, 2, 3)
    return jnp.concatenate(
        [array * (lane_head == h).astype(F32).astype(BF16) for h in order], axis=0
    )


def own(zero, one):
    first_half = lax.broadcasted_iota(jnp.int32, (1, 128), 1) < 64
    blocks = []
    for h in range(4):
        r, c = slice(32 * h, 32 * h + 32), slice(128 * (h // 2), 128 * (h // 2) + 128)
        if h % 2 == 0:
            blocks.append(jnp.where(first_half, zero[r, c], one[r, c]))
        else:
            blocks.append(pltpu.roll(jnp.where(first_half, one[r, c], zero[r, c]), 64, 1))
    return jnp.concatenate(blocks, axis=0).astype(BF16)


UNITS = [(a, g) for g in range(GROUPS) for a in range(2)]
ROOT = HD ** -0.5


def forward(feats, wq, normed_t, att_t, xhat, istd):
    center = jnp.mean(feats, axis=-1, keepdims=True)
    dev = feats - center
    inv = lax.rsqrt(jnp.mean(dev * dev, axis=-1, keepdims=True) + 1e-05)
    hat = dev * inv
    xhat[...] = hat
    istd[...] = jnp.broadcast_to(inv, (128, 128))
    nb = hat.astype(BF16)
    proj = dot(nb, wq[...]).astype(BF16)
    normed_t[...] = nb.T
    s = [
        dot(part(proj, a, D + 128 * g), spread(part(proj, a, 128 * g), a), NT) for a, g in UNITS
    ]
    vt = [part(proj, a, 2 * D + 128 * g).T for a, g in UNITS]
    p = []
    for t in s:
        e = jnp.exp2((t - jnp.max(t, axis=0, keepdims=True)) * (ROOT * LOG2E))
        p.append(e * (1.0 / jnp.sum(e, axis=0, keepdims=True)))
    ot = [dot(m, n.astype(BF16)) for m, n in zip(vt, p)]
    for g in range(GROUPS):
        att_t[128 * g:128 * g + 128, :] = own(ot[2 * g], ot[2 * g + 1])
    return proj, p


def backward(g, proj, p, ga, gp, query_t):
    qt = []
    for a in range(2):
        q, k = part(proj, a, 128 * g), part(proj, a, D + 128 * g)
        obd = spread(part(ga, a, 128 * g), a)
        dp = dot(part(proj, a, 2 * D + 128 * g), obd, NT)
        pa = p[2 * g + a]
        row = jnp.sum(dp * pa, axis=0, keepdims=True)
        ds = (pa * ((dp - row) * ROOT)).astype(BF16)
        at_row = pl.ds(64 * a, 64)
        gp[at_row, 128 * g:128 * g + 128] = dot(ds, spread(q, a)).astype(BF16)
        gp[at_row, D + 128 * g:D + 128 * g + 128] = dot(pa.astype(BF16), obd).astype(BF16)
        qt.append(dot(k.T, ds))
    query_t[128 * g:128 * g + 128, :] = own(qt[0], qt[1])


def device():
    region, tile = lax.axis_index("region"), lax.axis_index("tile")
    tiles = NX * NZ
    west = {"region": region, "tile": (tile + tiles - 1) % tiles}
    east = {"region": region, "tile": (tile + 1) % tiles}
    return region, tile, west, east


def send(src, dst, ss, rs, dev):
    return pltpu.make_async_remote_copy(
        src_ref=src, dst_ref=dst, send_sem=ss, recv_sem=rs, device_id=dev, device_id_type=MESH,
    )


def greet(partners):
    barrier = pltpu.get_barrier_semaphore()
    for dev in partners:
        pl.semaphore_signal(barrier, inc=1, device_id=dev, device_id_type=MESH)
    return lambda: pl.semaphore_wait(barrier, len(partners))


def pairs(v):
    v = v.reshape(8, 2, 8, D)
    return v[:, 0], v[:, 1]


def first_column(
    x_hbm, dy_hbm, mask_hbm, wq_hbm, wo_hbm,
    wq, wo, masked1, proj1, p1, normed_t1, att_t1, xhat1, istd1,
    normed_t, masked, att_t, query_t, gp, xhat, istd,
    xv, dyv, mask_ref, rim_out, rim_in, in_sem, rim_send, rim_recv,
):
    loads = [
        pltpu.make_async_copy(src, dst, in_sem.at[i])
        for i, (src, dst) in enumerate(
            ((x_hbm, xv), (dy_hbm, dyv), (wq_hbm, wq), (wo_hbm, wo), (mask_hbm, mask_ref))
        )
    ]
    for c in loads:
        c.start()
    _, _, west, east = device()
    greeted = greet([west, east])
    sub = low4((1, 8, D))

    def halves(ref):
        v = ref[...].astype(F32)
        return v[:, :8, :], v[:, 8:, :]

    def rim_of(lo):
        even, odd = pairs(lo)
        return jnp.where(sub, even, roll4(odd)).reshape(64, D).astype(BF16)

    rims = [
        send(rim_out.at[i], rim_in.at[i], rim_send.at[i], rim_recv.at[i], west) for i in range(2)
    ]
    loads[0].wait()
    x_lo, x_hi = halves(xv)
    rim_out[0] = rim_of(x_lo)
    greeted()
    rims[0].start()
    loads[1].wait()
    dy_lo, dy_hi = halves(dyv)
    rim_out[1] = rim_of(dy_lo)
    rims[1].start()

    for c in loads[2:]:
        c.wait()
    flag = [[mask_ref[a, b].astype(F32) for a in range(2)] for b in range(2)]

    def mask_of(dys, b):
        return jnp.concatenate([dys[:64] * flag[b][0], dys[64:] * flag[b][1]], axis=0).astype(BF16)

    proj, p = forward(
        jnp.where(sub, x_hi, x_lo).reshape(128, D), wq, normed_t, att_t, xhat, istd
    )
    mk = mask_of(jnp.where(sub, dy_hi, dy_lo).reshape(128, D), 0)
    masked[...] = mk
    ga = dot(mk, wo[...], NT).astype(BF16)
    for g in range(GROUPS):
        backward(g, proj, p, ga, gp, query_t)

    def joined(hi, far):
        even, odd = pairs(hi)
        loc = jnp.where(sub, roll4(even), odd).reshape(64, D)
        far = far.astype(F32)
        return jnp.concatenate([loc[:32], far[:32], loc[32:], far[32:]], axis=0)

    rims[0].wait()
    proj, p = forward(joined(x_hi, rim_in[0]), wq, normed_t1, att_t1, xhat1, istd1)
    proj1[...] = proj
    for i in range(2 * GROUPS):
        p1[i] = p[i]
    rims[1].wait()
    masked1[...] = mask_of(joined(dy_hi, rim_in[1]), 1)


def second_column(
    dy_hbm, wq, wo, masked1, proj1, p1, normed_t1, att_t1, xhat1, istd1,
    normed_t0, masked0, att_t0, query_t0, gp0, xhat0, istd0,
    out_ref, gq_ref, go_ref,
    dyv, back_out, back_in, query_t1, gp1, branch,
    gx, gz, r0x, r0z, hx, hz, r1x, r1z, jx, jz, r2x, r2z, r3x, r3z, fx, fz,
    in_sem, back_sem,
    s0, q0, s1x, q1x, s1z, q1z, s2x, q2x, s2z, q2z, s3x, q3x, s3z, q3z, s4, q4,
):
    load = pltpu.make_async_copy(dy_hbm, dyv, in_sem)
    load.start()
    region, tile, west, east = device()
    y, core = region // 2, region % 2
    x, z = tile // NZ, tile % NZ
    tiles = NX * NZ

    def at(ax, ay, az, ac):
        return {"region": ay * 2 + ac, "tile": ax * NZ + az}

    other = at(x, y, z, 1 - core)
    by_x = [at((x + k) % NX, y, z, core) for k in range(1, NX)]
    by_z = [at(x, y, (z + k) % NZ, core) for k in range(1, NZ)]
    by_y = [at(x, (y + k) % NY, z, core) for k in range(1, NY)]
    greeted = greet([west, east, other] + by_x + by_z + by_y)
    sub = low4((1, 8, D))
    ga = dot(masked1[...], wo[...], NT).astype(BF16)
    proj, p = proj1, p1

    def both(a, b, axis):
        return jnp.concatenate([a, b], axis=axis)

    nt = both(normed_t0[...], normed_t1[...], 1)
    ga_full = dot(
        both(att_t0[...], att_t1[...], 1), both(masked0[...], masked1[...], 0)
    ).reshape(16, 3, 8, D)
    w0, w1, w2 = ga_full[:, 0], ga_full[:, 1], ga_full[:, 2]
    spare = [
        roll4(jnp.where(sub, w0, w1)),
        jnp.where(sub, w2, w0),
        roll4(jnp.where(sub, w1, w2)),
    ]
    sends = []

    def start(c):
        c.start()
        sends.append(c)
        return c

    def swap_x(i):
        return start(send(
            gx.at[:, pl.ds((1 - core) * 4, 4), :, XCUT[i]], r0x.at[:, :, :, XCUT[i]],
            s0.at[i], q0.at[i], other,
        ))

    core0 = []
    for g in range(GROUPS):
        backward(g, proj, p, ga, gp1, query_t1)
        at_g = slice(128 * g, 128 * g + 128)
        at_gv = slice(D + 128 * g, D + 128 * g + 128)
        if g == 0:
            greeted()
        gn = jnp.concatenate([
            dot(nt, both(query_t0[at_g, :], query_t1[at_g, :], 1), NT),
            dot(nt, both(gp0[:, at_g], gp1[:, at_g], 0)),
            dot(nt, both(gp0[:, at_gv], gp1[:, at_gv], 0)),
        ], axis=1).reshape(16, 3, 8, D)
        v0, v1, v2 = gn[:, 0], gn[:, 1], gn[:, 2]
        packed = jnp.stack(
            [v0, jnp.where(sub, v1, spare[g]), v2, jnp.where(sub, spare[g], v1)], axis=1
        ).reshape(NX, NZ, 16, D).astype(BF16)
        if g == 0:
            gx[:, :, :, 0:384] = packed
            core0.append(swap_x(0))
        elif g == 1:
            gx[:, :, :, 384:640] = packed[..., 0:256]
            gz[:, :, :, 0:128] = packed[..., 256:384]
            core0.append(swap_x(1))
        else:
            gz[:, :, :, 128:512] = packed
            core0.append(start(send(
                gz.at[pl.ds((1 - core) * 2, 2)], r0z, s0.at[g], q0.at[g], other,
            )))

    p1x = []
    for i in range(2):
        core0[i].wait_recv()
        cut = XCUT[i]
        mine = gx[:, pl.ds(core * 4, 4), :, cut].astype(F32) + r0x[:, :, :, cut].astype(F32)
        hx[:, :, :, cut] = mine.astype(BF16)
        for k in (2, 1, 3):
            p1x.append(start(send(
                hx.at[(x + k) % NX, :, :, cut], r1x.at[k - 1, :, :, cut],
                s1x.at[i, k - 1], q1x.at[i, k - 1], by_x[k - 1],
            )))
    core0[2].wait_recv()
    mine = gz[pl.ds(core * 2, 2)].astype(F32) + r0z[...].astype(F32)
    hz[...] = mine.astype(BF16)
    p1z = []
    for k in (4, 3, 5, 2, 6, 1, 7):
        p1z.append(start(send(
            hz.at[:, (z + k) % NZ], r1z.at[k - 1], s1z.at[k - 1], q1z.at[k - 1], by_z[k - 1],
        )))

    def branch_of(query_t, gp, xhat, istd):
        gn = dot(query_t[...].T, wq[:, 0:D], NT) + dot(gp[...], wq[:, D:3 * D], NT)
        hat = xhat[...]
        inv = istd[:, 0:1]
        m0 = jnp.mean(gn, axis=-1, keepdims=True)
        m1 = jnp.mean(gn * hat, axis=-1, keepdims=True)
        return (inv * (gn - m0 - hat * m1)).astype(BF16)

    br = branch_of(query_t1, gp1, xhat1, istd1)
    back_out[0:32, :] = br[32:64]
    back_out[32:64, :] = br[96:128]
    back = start(send(back_out, back_in, back_sem.at[0], back_sem.at[1], east))
    loc = jnp.concatenate([br[0:32], br[64:96]], axis=0).astype(F32).reshape(8, 8, D)

    for c in p1x:
        c.wait_recv()
    t = hx[x].astype(F32)
    for k in range(NX - 1):
        t = t + r1x[k].astype(F32)
    jx[...] = t.astype(BF16)
    for k in range(1, NZ):
        to = (z + k) % NZ
        c = send(jx.at[to % 4], r2x.at[k - 1], s2x.at[k - 1], q2x.at[k - 1], by_z[k - 1])

        @pl.when(to // 4 == core)
        def _():
            c.start()

    for c in p1z:
        c.wait_recv()
    t = hz[:, z].astype(F32)
    for k in range(NZ - 1):
        t = t + r1z[k].astype(F32)
    jz[...] = t.astype(BF16)
    for k in range(1, NX):
        to = (x + k) % NX
        c = send(jz.at[to % 2], r2z.at[k - 1], s2z.at[k - 1], q2z.at[k - 1], by_x[k - 1])

        @pl.when(to // 2 == core)
        def _():
            c.start()

    branch[...] = branch_of(query_t0, gp0, xhat0, istd0).astype(F32)

    has_x = z // 4 == core
    has_z = x // 2 == core

    def y_copies(buf, ss, qs):
        return [
            send(buf.at[y], buf.at[y], ss.at[k - 1], qs.at[y], by_y[k - 1])
            for k in range(1, NY)
        ]

    def y_arrivals(buf, ss, qs):
        return [
            send(buf.at[y], buf.at[(y + k) % NY], ss.at[k - 1], qs.at[(y + k) % NY], by_y[k - 1])
            for k in range(1, NY)
        ]

    @pl.when(has_x)
    def _():
        t = jx[z % 4].astype(F32)
        for k in range(1, NZ):
            send(jx.at[z % 4], r2x.at[k - 1], s2x.at[k - 1], q2x.at[k - 1], by_z[k - 1]).wait_recv()
        for k in range(NZ - 1):
            t = t + r2x[k].astype(F32)
        r3x[y] = t.astype(BF16)
        for c in y_copies(r3x, s3x, q3x):
            c.start()

    @pl.when(has_z)
    def _():
        t = jz[x % 2].astype(F32)
        for k in range(1, NX):
            send(jz.at[x % 2], r2z.at[k - 1], s2z.at[k - 1], q2z.at[k - 1], by_x[k - 1]).wait_recv()
        for k in range(NX - 1):
            t = t + r2z[k].astype(F32)
        r3z[y] = t.astype(BF16)
        for c in y_copies(r3z, s3z, q3z):
            c.start()

    back.wait_recv()
    load.wait()
    far = back_in[...].astype(F32).reshape(8, 8, D)
    br0 = branch[...].reshape(16, 8, D)

    def unpaired(even, odd):
        return jnp.stack([even, odd], axis=1).reshape(16, 8, D)

    new_lo = dyv[:, :8, :].astype(F32) + jnp.where(sub, unpaired(far, roll4(far)), br0)
    new_hi = dyv[:, 8:, :].astype(F32) + jnp.where(sub, br0, unpaired(roll4(loc), loc))
    out_ref[...] = jnp.concatenate([new_lo, new_hi], axis=1).astype(BF16)

    last_x = send(fx, fx, s4.at[0], q4.at[0], other)
    last_z = send(fz, fz, s4.at[1], q4.at[1], other)

    @pl.when(has_x)
    def _():
        for c in y_arrivals(r3x, s3x, q3x):
            c.wait_recv()
        t = r3x[0].astype(F32)
        for k in range(1, NY):
            t = t + r3x[k].astype(F32)
        fx[...] = t.astype(BF16)
        last_x.start()

    @pl.when(has_z)
    def _():
        for c in y_arrivals(r3z, s3z, q3z):
            c.wait_recv()
        t = r3z[0].astype(F32)
        for k in range(1, NY):
            t = t + r3z[k].astype(F32)
        fz[...] = t.astype(BF16)
        last_z.start()

    @pl.when(jnp.logical_not(has_x))
    def _():
        last_x.wait_recv()

    @pl.when(jnp.logical_not(has_z))
    def _():
        last_z.wait_recv()

    scale = 1.0 / math.sqrt(3 * 64 * 2 * NY * tiles)
    odd = (z % 2) == 1
    final = jnp.concatenate([fx[...], fz[...]], axis=1).astype(F32) * scale
    for g in range(GROUPS):
        f = final[:, D * g:D * g + D]
        top, bot = f[0:8], f[8:16]
        top_r, bot_r = pltpu.roll(top, 4, 0), pltpu.roll(bot, 4, 0)
        low = low4((8, D))
        first = jnp.where(odd, jnp.where(low, bot_r, top_r), top)
        rest = jnp.where(odd, top_r, bot)
        extra = jnp.where(odd, bot, bot_r)
        for s in range(3):
            lanes = slice(s * D + 128 * g, s * D + 128 * g + 128)
            gq_ref[0:8, lanes] = first[:, 128 * s:128 * s + 128]
            gq_ref[8:12, lanes] = rest[0:4, 128 * s:128 * s + 128]
        go_ref[4 * g:4 * g + 4, :] = extra[0:4]

    for c in sends:
        c.wait_send()
    for k in range(1, NZ):
        to = (z + k) % NZ
        c = send(jx.at[to % 4], r2x.at[k - 1], s2x.at[k - 1], q2x.at[k - 1], by_z[k - 1])

        @pl.when(to // 4 == core)
        def _():
            c.wait_send()

    for k in range(1, NX):
        to = (x + k) % NX
        c = send(jz.at[to % 2], r2z.at[k - 1], s2z.at[k - 1], q2z.at[k - 1], by_x[k - 1])

        @pl.when(to // 2 == core)
        def _():
            c.wait_send()

    @pl.when(has_x)
    def _():
        for c in y_copies(r3x, s3x, q3x):
            c.wait_send()
        last_x.wait_send()

    @pl.when(has_z)
    def _():
        for c in y_copies(r3z, s3z, q3z):
            c.wait_send()
        last_z.wait_send()


def hand_over(a, b, c, a_out, b_out, c_out, sems):
    copies = [
        pltpu.make_async_copy(src, dst, sems.at[i])
        for i, (src, dst) in enumerate(((a, a_out), (b, b_out), (c, c_out)))
    ]
    for c in copies:
        c.start()
    for c in copies:
        c.wait()


def body(tokens, grad_out, ocean_mask, w_qkv, w_out):
    any_spec = pl.BlockSpec(memory_space=pl.ANY)
    vmem_spec = pl.BlockSpec(memory_space=pltpu.VMEM)

    def buf(*shape, dtype=BF16):
        return pltpu.VMEM(shape, dtype)

    def sem(*shape):
        return pltpu.SemaphoreType.DMA(shape)

    def params(collective, mib):
        return pltpu.CompilerParams(
            collective_id=collective, has_side_effects=True, vmem_limit_bytes=mib * 1024 * 1024
        )

    column = [
        buf(D, 128), buf(128, D), buf(D, 128), buf(D, 128), buf(128, 2 * D),
        buf(128, D, dtype=F32), buf(128, 128, dtype=F32),
    ]
    handed = [
        buf(D, 3 * D), buf(D, D), buf(128, D), buf(128, 3 * D),
        buf(2 * GROUPS, 64, 256, dtype=F32),
        column[0], column[2], column[5], column[6],
    ] + column
    first = pl.pallas_call(
        first_column,
        out_shape=handed,
        in_specs=[any_spec] * 5,
        out_specs=[vmem_spec] * len(handed),
        scratch_shapes=[
            buf(16, 16, D), buf(16, 16, D), pltpu.SMEM((2, 2), jnp.int32),
            buf(2, 64, D), buf(2, 64, D), sem(5), sem(2), sem(2),
        ],
        compiler_params=params(0, 56),
        cost_estimate=pl.CostEstimate(
            flops=300_000_000, bytes_accessed=2_000_000, transcendentals=100_000
        ),
        name="first_column",
    )(tokens, grad_out, ocean_mask, w_qkv, w_out)
    results = pl.pallas_call(
        second_column,
        out_shape=(buf(16, 16, D), buf(12, 3 * D, dtype=F32), buf(12, D, dtype=F32)),
        in_specs=[any_spec] + [vmem_spec] * len(handed),
        out_specs=(vmem_spec, vmem_spec, vmem_spec),
        scratch_shapes=[
            buf(16, 16, D), buf(64, D), buf(64, D), column[3], column[4],
            buf(128, D, dtype=F32),
            buf(NX, NZ, 16, WX), buf(NX, NZ, 16, WZ),
            buf(NX, 4, 16, WX), buf(2, NZ, 16, WZ),
            buf(NX, 4, 16, WX), buf(2, NZ, 16, WZ),
            buf(NX - 1, 4, 16, WX), buf(NZ - 1, 2, 16, WZ),
            buf(4, 16, WX), buf(2, 16, WZ),
            buf(NZ - 1, 16, WX), buf(NX - 1, 16, WZ),
            buf(NY, 16, WX), buf(NY, 16, WZ),
            buf(16, WX), buf(16, WZ),
            pltpu.SemaphoreType.DMA, sem(2),
            sem(3), sem(3), sem(2, NX - 1), sem(2, NX - 1), sem(NZ - 1), sem(NZ - 1),
            sem(NZ - 1), sem(NZ - 1), sem(NX - 1), sem(NX - 1),
            sem(NY - 1), sem(NY), sem(NY - 1), sem(NY), sem(2), sem(2),
        ],
        compiler_params=params(1, 24),
        cost_estimate=pl.CostEstimate(
            flops=600_000_000, bytes_accessed=1_000_000, transcendentals=100_000
        ),
        name="second_column",
    )(grad_out, *first)
    return pl.pallas_call(
        hand_over,
        out_shape=[jax.ShapeDtypeStruct(r.shape, r.dtype) for r in results],
        in_specs=[any_spec] * 3,
        out_specs=[any_spec] * 3,
        scratch_shapes=[sem(3)],
        compiler_params=pltpu.CompilerParams(vmem_limit_bytes=4 * 1024 * 1024),
        cost_estimate=pl.CostEstimate(flops=0, bytes_accessed=600_000, transcendentals=0),
        name="hand_over",
    )(*results)


def solution(mesh):
    return jax.shard_map(
        body,
        mesh=mesh,
        in_specs=(
            P("region", "tile", None),
            P("region", "tile", None),
            P("region", "tile"),
            P(),
            P(),
        ),
        out_specs=(P("region", "tile", None), P("tile", None), P("tile", None)),
        check_vma=False,
    )
```

```python
import math

import jax
import jax.numpy as jnp
from jax import lax
from jax.experimental import pallas as pl
from jax.experimental.pallas import tpu as pltpu
from jax.sharding import PartitionSpec as P

MESH = pl.DeviceIdType.MESH
F32 = jnp.float32
BF16 = jnp.bfloat16
D = 384
HD = 32
LOG2E = math.log2(math.e)
GROUPS = 3
NX, NZ, NY = 4, 8, 8
WY, WX, WZ = 384, 512, 256
XCUT = (slice(0, 384), slice(384, 512))
NT = (((1,), (1,)), ((), ()))


def dot(a, b, dims=(((1,), (0,)), ((), ()))):
    return lax.dot_general(a, b, dims, preferred_element_type=F32)


def roll4(a):
    n, _, width = a.shape
    return pltpu.roll(a.reshape(n * 8, width).reshape(n, 8, width), 4, 1)


def low4(shape):
    return lax.broadcasted_iota(jnp.int32, shape, len(shape) - 2) % 8 < 4


def part(array, a, first):
    return array[64 * a:64 * a + 64, first:first + 128]


def spread(array, a):
    lane_head = lax.broadcasted_iota(jnp.int32, (1, 128), 1) // HD
    order = (1, 0, 3, 2) if a else (0, 1, 2, 3)
    return jnp.concatenate(
        [array * (lane_head == h).astype(F32).astype(BF16) for h in order], axis=0
    )


def own(zero, one):
    first_half = lax.broadcasted_iota(jnp.int32, (1, 128), 1) < 64
    blocks = []
    for h in range(4):
        r, c = slice(32 * h, 32 * h + 32), slice(128 * (h // 2), 128 * (h // 2) + 128)
        if h % 2 == 0:
            blocks.append(jnp.where(first_half, zero[r, c], one[r, c]))
        else:
            blocks.append(pltpu.roll(jnp.where(first_half, one[r, c], zero[r, c]), 64, 1))
    return jnp.concatenate(blocks, axis=0).astype(BF16)


UNITS = [(a, g) for g in range(GROUPS) for a in range(2)]
ROOT = HD ** -0.5


def forward(feats, wq, normed_t, att_t, xhat, istd):
    center = jnp.mean(feats, axis=-1, keepdims=True)
    dev = feats - center
    inv = lax.rsqrt(jnp.mean(dev * dev, axis=-1, keepdims=True) + 1e-05)
    hat = dev * inv
    xhat[...] = hat
    istd[...] = jnp.broadcast_to(inv, (128, 128))
    nb = hat.astype(BF16)
    proj = dot(nb, wq[...]).astype(BF16)
    normed_t[...] = nb.T
    s = [
        dot(part(proj, a, D + 128 * g), spread(part(proj, a, 128 * g), a), NT) for a, g in UNITS
    ]
    vt = [part(proj, a, 2 * D + 128 * g).T for a, g in UNITS]
    p = []
    for t in s:
        e = jnp.exp2((t - jnp.max(t, axis=0, keepdims=True)) * (ROOT * LOG2E))
        p.append(e * (1.0 / jnp.sum(e, axis=0, keepdims=True)))
    ot = [dot(m, n.astype(BF16)) for m, n in zip(vt, p)]
    for g in range(GROUPS):
        att_t[128 * g:128 * g + 128, :] = own(ot[2 * g], ot[2 * g + 1])
    return proj, p


def backward(g, proj, p, ga, gp, query_t):
    qt = []
    for a in range(2):
        q, k = part(proj, a, 128 * g), part(proj, a, D + 128 * g)
        obd = spread(part(ga, a, 128 * g), a)
        dp = dot(part(proj, a, 2 * D + 128 * g), obd, NT)
        pa = p[2 * g + a]
        row = jnp.sum(dp * pa, axis=0, keepdims=True)
        ds = (pa * ((dp - row) * ROOT)).astype(BF16)
        at_row = pl.ds(64 * a, 64)
        gp[at_row, 128 * g:128 * g + 128] = dot(ds, spread(q, a)).astype(BF16)
        gp[at_row, D + 128 * g:D + 128 * g + 128] = dot(pa.astype(BF16), obd).astype(BF16)
        qt.append(dot(k.T, ds))
    query_t[128 * g:128 * g + 128, :] = own(qt[0], qt[1])


def device():
    region, tile = lax.axis_index("region"), lax.axis_index("tile")
    tiles = NX * NZ
    west = {"region": region, "tile": (tile + tiles - 1) % tiles}
    east = {"region": region, "tile": (tile + 1) % tiles}
    return region, tile, west, east


def send(src, dst, ss, rs, dev):
    return pltpu.make_async_remote_copy(
        src_ref=src, dst_ref=dst, send_sem=ss, recv_sem=rs, device_id=dev, device_id_type=MESH,
    )


def greet(partners):
    barrier = pltpu.get_barrier_semaphore()
    for dev in partners:
        pl.semaphore_signal(barrier, inc=1, device_id=dev, device_id_type=MESH)
    return lambda: pl.semaphore_wait(barrier, len(partners))


def pairs(v):
    v = v.reshape(8, 2, 8, D)
    return v[:, 0], v[:, 1]


def kernel(
    x_hbm, dy_hbm, mask_hbm, wq_hbm, wo_hbm,
    out_ref, gq_ref, go_ref,
    xv, dyv, mask_ref, wq, wo,
    rim_out, rim_in, back_out, back_in,
    normed_t0, att_t0, query_t0, gp0, xhat0, istd0, masked0,
    normed_t1, att_t1, query_t1, gp1, xhat1, istd1, masked1, branch,
    gx, gy, gz, r0x, r0y, r0z, hx, hy, hz, r1x, r1y, r1z, jx, jy, jz,
    r2x, r2y, r2z, r3x, ky, r3y, r3z, fx, fy, fz,
    in_sem, rim_send, rim_recv, back_sem,
    s0, q0, s1x, q1x, s1y, q1y, s1z, q1z, s2x, q2x, s2y, q2y, s2z, q2z,
    s3x, q3x, s3y, q3y, s3z, q3z, s4y, q4y, s5, q5,
):
    loads = [
        pltpu.make_async_copy(src, dst, in_sem.at[i])
        for i, (src, dst) in enumerate(
            ((x_hbm, xv), (dy_hbm, dyv), (wq_hbm, wq), (wo_hbm, wo), (mask_hbm, mask_ref))
        )
    ]
    for c in loads:
        c.start()
    region, tile, west, east = device()
    y, core = region // 2, region % 2
    x, z = tile // NZ, tile % NZ
    tiles = NX * NZ

    def at(ax, ay, az, ac):
        return {"region": ay * 2 + ac, "tile": ax * NZ + az}

    other = at(x, y, z, 1 - core)
    by_x = [at((x + k) % NX, y, z, core) for k in range(1, NX)]
    by_z = [at(x, y, (z + k) % NZ, core) for k in range(1, NZ)]
    by_y = [at(x, (y + k) % NY, z, core) for k in range(1, NY)]
    greeted = greet([west, east, other] + by_x + by_z + by_y)
    sub = low4((1, 8, D))

    def halves(ref):
        v = ref[...].astype(F32)
        return v[:, :8, :], v[:, 8:, :]

    def rim_of(lo):
        even, odd = pairs(lo)
        return jnp.where(sub, even, roll4(odd)).reshape(64, D).astype(BF16)

    rims = [
        send(rim_out.at[i], rim_in.at[i], rim_send.at[i], rim_recv.at[i], west) for i in range(2)
    ]
    loads[0].wait()
    x_lo, x_hi = halves(xv)
    rim_out[0] = rim_of(x_lo)
    greeted()
    rims[0].start()
    loads[1].wait()
    dy_lo, dy_hi = halves(dyv)
    rim_out[1] = rim_of(dy_lo)
    rims[1].start()

    for c in loads[2:]:
        c.wait()
    flag = [[mask_ref[a, b].astype(F32) for a in range(2)] for b in range(2)]

    def mask_of(dys, b):
        return jnp.concatenate([dys[:64] * flag[b][0], dys[64:] * flag[b][1]], axis=0).astype(BF16)

    proj, p = forward(
        jnp.where(sub, x_hi, x_lo).reshape(128, D), wq, normed_t0, att_t0, xhat0, istd0
    )
    mk = mask_of(jnp.where(sub, dy_hi, dy_lo).reshape(128, D), 0)
    masked0[...] = mk
    ga = dot(mk, wo[...], NT).astype(BF16)
    for g in range(GROUPS):
        backward(g, proj, p, ga, gp0, query_t0)

    def joined(hi, far):
        even, odd = pairs(hi)
        loc = jnp.where(sub, roll4(even), odd).reshape(64, D)
        far = far.astype(F32)
        return jnp.concatenate([loc[:32], far[:32], loc[32:], far[32:]], axis=0)

    rims[0].wait()
    proj, p = forward(joined(x_hi, rim_in[0]), wq, normed_t1, att_t1, xhat1, istd1)
    rims[1].wait()
    masked1[...] = mask_of(joined(dy_hi, rim_in[1]), 1)
    ga = dot(masked1[...], wo[...], NT).astype(BF16)

    def both(a, b, axis):
        return jnp.concatenate([a, b], axis=axis)

    nt = both(normed_t0[...], normed_t1[...], 1)
    ga_full = dot(
        both(att_t0[...], att_t1[...], 1), both(masked0[...], masked1[...], 0)
    ).reshape(16, 3, 8, D)
    w0, w1, w2 = ga_full[:, 0], ga_full[:, 1], ga_full[:, 2]
    spare = [
        roll4(jnp.where(sub, w0, w1)),
        jnp.where(sub, w2, w0),
        roll4(jnp.where(sub, w1, w2)),
    ]
    sends = []

    def start(c):
        c.start()
        sends.append(c)
        return c

    def swap_x(i):
        return start(send(
            gx.at[:, pl.ds((1 - core) * 4, 4), :, XCUT[i]], r0x.at[:, :, :, XCUT[i]],
            s0.at[i], q0.at[i], other,
        ))

    far_half = pl.ds((1 - core) * 2, 2)
    core0 = []
    for g in range(GROUPS):
        backward(g, proj, p, ga, gp1, query_t1)
        at_g = slice(128 * g, 128 * g + 128)
        at_gv = slice(D + 128 * g, D + 128 * g + 128)
        gn = jnp.concatenate([
            dot(nt, both(query_t0[at_g, :], query_t1[at_g, :], 1), NT),
            dot(nt, both(gp0[:, at_g], gp1[:, at_g], 0)),
            dot(nt, both(gp0[:, at_gv], gp1[:, at_gv], 0)),
        ], axis=1).reshape(16, 3, 8, D)
        v0, v1, v2 = gn[:, 0], gn[:, 1], gn[:, 2]
        packed = jnp.stack(
            [v0, jnp.where(sub, v1, spare[g]), v2, jnp.where(sub, spare[g], v1)], axis=1
        ).reshape(NX, NZ, 16, D).astype(BF16)
        if g == 0:
            gy[...] = packed
            core0.append(start(send(gy.at[far_half], r0y, s0.at[3], q0.at[3], other)))
        elif g == 1:
            gx[:, :, :, XCUT[0]] = packed
            core0.append(swap_x(0))
        else:
            gx[:, :, :, XCUT[1]] = packed[..., 0:128]
            gz[...] = packed[..., 128:384]
            core0.append(swap_x(1))
            core0.append(start(send(gz.at[far_half], r0z, s0.at[2], q0.at[2], other)))

    my_half = pl.ds(core * 2, 2)
    far_first = (4, 3, 5, 2, 6, 1, 7)
    core0[0].wait_recv()
    hy[...] = (gy[my_half].astype(F32) + r0y[...].astype(F32)).astype(BF16)
    p1y = [
        start(send(
            hy.at[:, (y + k) % NY], r1y.at[k - 1], s1y.at[k - 1], q1y.at[k - 1], by_y[k - 1],
        ))
        for k in far_first
    ]
    p1x = []
    for i in range(2):
        core0[1 + i].wait_recv()
        cut = XCUT[i]
        mine = gx[:, pl.ds(core * 4, 4), :, cut].astype(F32) + r0x[:, :, :, cut].astype(F32)
        hx[:, :, :, cut] = mine.astype(BF16)
        for k in (2, 1, 3):
            p1x.append(start(send(
                hx.at[(x + k) % NX, :, :, cut], r1x.at[k - 1, :, :, cut],
                s1x.at[i, k - 1], q1x.at[i, k - 1], by_x[k - 1],
            )))
    core0[3].wait_recv()
    hz[...] = (gz[my_half].astype(F32) + r0z[...].astype(F32)).astype(BF16)
    p1z = [
        start(send(
            hz.at[:, (z + k) % NZ], r1z.at[k - 1], s1z.at[k - 1], q1z.at[k - 1], by_z[k - 1],
        ))
        for k in far_first
    ]

    def branch_of(query_t, gp, xhat, istd):
        gn = dot(query_t[...].T, wq[:, 0:D], NT) + dot(gp[...], wq[:, D:3 * D], NT)
        hat = xhat[...]
        inv = istd[:, 0:1]
        m0 = jnp.mean(gn, axis=-1, keepdims=True)
        m1 = jnp.mean(gn * hat, axis=-1, keepdims=True)
        return (inv * (gn - m0 - hat * m1)).astype(BF16)

    br = branch_of(query_t1, gp1, xhat1, istd1)
    back_out[0:32, :] = br[32:64]
    back_out[32:64, :] = br[96:128]
    back = start(send(back_out, back_in, back_sem.at[0], back_sem.at[1], east))
    loc = jnp.concatenate([br[0:32], br[64:96]], axis=0).astype(F32).reshape(8, 8, D)

    branch[...] = branch_of(query_t0, gp0, xhat0, istd0).astype(F32)

    has_x = z // 4 == core
    has_z = x // 2 == core

    def total(first, buf, count):
        t = first.astype(F32)
        for i in range(count):
            t = t + buf[i].astype(F32)
        return t.astype(BF16)

    def second(buf, slots, ss, qs, devs, place, count, half):
        out = []
        for k in range(1, count):
            to = (place + k) % count
            c = send(buf.at[to % half], slots.at[k - 1], ss.at[k - 1], qs.at[k - 1], devs[k - 1])
            out.append((c, to // half == core))
        return out

    p2y = second(jy, r2y, s2y, q2y, by_x, x, NX, 2)
    p2x = second(jx, r2x, s2x, q2x, by_z, z, NZ, 4)
    p2z = second(jz, r2z, s2z, q2z, by_x, x, NX, 2)

    def start_if(copies):
        for c, yes in copies:
            pl.when(yes)(c.start)

    for c in p1y:
        c.wait_recv()
    jy[...] = total(hy[:, y], r1y, NY - 1)
    start_if(p2y)
    for c in p1x:
        c.wait_recv()
    jx[...] = total(hx[x], r1x, NX - 1)
    start_if(p2x)
    for c in p1z:
        c.wait_recv()
    jz[...] = total(hz[:, z], r1z, NZ - 1)
    start_if(p2z)

    def y_copies(buf, ss, qs):
        return [
            send(buf.at[y], buf.at[y], ss.at[k - 1], qs.at[y], by_y[k - 1])
            for k in (4, 3, 5, 2, 6, 1, 7)
        ]

    def y_arrivals(buf, ss, qs):
        return [
            send(buf.at[y], buf.at[(y + k) % NY], ss.at[k - 1], qs.at[(y + k) % NY], by_y[k - 1])
            for k in range(1, NY)
        ]

    own_y = jnp.logical_and(has_z, y == z)
    p3y = [
        (send(ky, r3y.at[k - 1], s3y.at[k - 1], q3y.at[k - 1], by_z[k - 1]), (z + k) % NZ == y)
        for k in range(1, NZ)
    ]
    p4y = [send(fy, fy, s4y.at[k], q4y, dev) for k, dev in enumerate(by_y)]

    @pl.when(has_z)
    def _():
        for c, _ in p2y:
            c.wait_recv()
        ky[...] = total(jy[x % 2], r2y, NX - 1)
        start_if(p3y)

    @pl.when(has_x)
    def _():
        for c, _ in p2x:
            c.wait_recv()
        r3x[y] = total(jx[z % 4], r2x, NZ - 1)
        for c in y_copies(r3x, s3x, q3x):
            c.start()

    @pl.when(has_z)
    def _():
        for c, _ in p2z:
            c.wait_recv()
        r3z[y] = total(jz[x % 2], r2z, NX - 1)
        for c in y_copies(r3z, s3z, q3z):
            c.start()

    @pl.when(own_y)
    def _():
        for c, _ in p3y:
            c.wait_recv()
        fy[...] = total(ky[...], r3y, NZ - 1)
        for c in p4y:
            c.start()

    back.wait_recv()
    far = back_in[...].astype(F32).reshape(8, 8, D)
    br0 = branch[...].reshape(16, 8, D)

    def unpaired(even, odd):
        return jnp.stack([even, odd], axis=1).reshape(16, 8, D)

    new_lo = dyv[:, :8, :].astype(F32) + jnp.where(sub, unpaired(far, roll4(far)), br0)
    new_hi = dyv[:, 8:, :].astype(F32) + jnp.where(sub, br0, unpaired(roll4(loc), loc))
    out_ref[...] = jnp.concatenate([new_lo, new_hi], axis=1).astype(BF16)

    last_x = send(fx, fx, s5.at[0], q5.at[0], other)
    last_y = send(fy, fy, s5.at[1], q5.at[1], other)
    last_z = send(fz, fz, s5.at[2], q5.at[2], other)

    def settle(buf, out, ss, qs, last):
        for c in y_arrivals(buf, ss, qs):
            c.wait_recv()
        out[...] = total(buf[0], buf.at[1:], NY - 1)
        last.start()

    @pl.when(has_x)
    def _():
        settle(r3x, fx, s3x, q3x, last_x)

    @pl.when(has_z)
    def _():
        settle(r3z, fz, s3z, q3z, last_z)
        pl.when(y != z)(p4y[0].wait_recv)
        last_y.start()

    @pl.when(jnp.logical_not(has_x))
    def _():
        last_x.wait_recv()

    @pl.when(jnp.logical_not(has_z))
    def _():
        last_z.wait_recv()
        last_y.wait_recv()

    scale = 1.0 / math.sqrt(3 * 64 * 2 * NY * tiles)
    odd = (z % 2) == 1
    final = jnp.concatenate([fy[...], fx[...], fz[...]], axis=1).astype(F32) * scale
    for g in range(GROUPS):
        f = final[:, D * g:D * g + D]
        top, bot = f[0:8], f[8:16]
        top_r, bot_r = pltpu.roll(top, 4, 0), pltpu.roll(bot, 4, 0)
        low = low4((8, D))
        first = jnp.where(odd, jnp.where(low, bot_r, top_r), top)
        rest = jnp.where(odd, top_r, bot)
        extra = jnp.where(odd, bot, bot_r)
        for s in range(3):
            lanes = slice(s * D + 128 * g, s * D + 128 * g + 128)
            gq_ref[0:8, lanes] = first[:, 128 * s:128 * s + 128]
            gq_ref[8:12, lanes] = rest[0:4, 128 * s:128 * s + 128]
        go_ref[4 * g:4 * g + 4, :] = extra[0:4]

    for c in sends:
        c.wait_send()
    for c, yes in p2x + p2y + p2z:
        pl.when(yes)(c.wait_send)

    @pl.when(has_x)
    def _():
        for c in y_copies(r3x, s3x, q3x):
            c.wait_send()
        last_x.wait_send()

    @pl.when(has_z)
    def _():
        for c, yes in p3y:
            pl.when(yes)(c.wait_send)
        for c in y_copies(r3z, s3z, q3z):
            c.wait_send()
        last_z.wait_send()
        last_y.wait_send()

    @pl.when(own_y)
    def _():
        for c in p4y:
            c.wait_send()


def hand_over(a, b, c, a_out, b_out, c_out, sems):
    copies = [
        pltpu.make_async_copy(src, dst, sems.at[i])
        for i, (src, dst) in enumerate(((a, a_out), (b, b_out), (c, c_out)))
    ]
    for c in copies:
        c.start()
    for c in copies:
        c.wait()


def body(tokens, grad_out, ocean_mask, w_qkv, w_out):
    any_spec = pl.BlockSpec(memory_space=pl.ANY)
    vmem_spec = pl.BlockSpec(memory_space=pltpu.VMEM)

    def buf(*shape, dtype=BF16):
        return pltpu.VMEM(shape, dtype)

    def sem(*shape):
        return pltpu.SemaphoreType.DMA(shape)

    column = [
        buf(D, 128), buf(D, 128), buf(D, 128), buf(128, 2 * D),
        buf(128, D, dtype=F32), buf(128, 128, dtype=F32), buf(128, D),
    ]
    results = pl.pallas_call(
        kernel,
        out_shape=(buf(16, 16, D), buf(12, 3 * D, dtype=F32), buf(12, D, dtype=F32)),
        in_specs=[any_spec] * 5,
        out_specs=(vmem_spec, vmem_spec, vmem_spec),
        scratch_shapes=[
            buf(16, 16, D), buf(16, 16, D), pltpu.SMEM((2, 2), jnp.int32),
            buf(D, 3 * D), buf(D, D),
            buf(2, 64, D), buf(2, 64, D), buf(64, D), buf(64, D),
            *column, *column, buf(128, D, dtype=F32),
            buf(NX, NZ, 16, WX), buf(NX, NZ, 16, WY), buf(NX, NZ, 16, WZ),
            buf(NX, 4, 16, WX), buf(2, NZ, 16, WY), buf(2, NZ, 16, WZ),
            buf(NX, 4, 16, WX), buf(2, NZ, 16, WY), buf(2, NZ, 16, WZ),
            buf(NX - 1, 4, 16, WX), buf(NY - 1, 2, 16, WY), buf(NZ - 1, 2, 16, WZ),
            buf(4, 16, WX), buf(2, 16, WY), buf(2, 16, WZ),
            buf(NZ - 1, 16, WX), buf(NX - 1, 16, WY), buf(NX - 1, 16, WZ),
            buf(NY, 16, WX), buf(16, WY), buf(NZ - 1, 16, WY), buf(NY, 16, WZ),
            buf(16, WX), buf(16, WY), buf(16, WZ),
            sem(5), sem(2), sem(2), sem(2),
            sem(4), sem(4), sem(2, NX - 1), sem(2, NX - 1),
            sem(NY - 1), sem(NY - 1), sem(NZ - 1), sem(NZ - 1),
            sem(NZ - 1), sem(NZ - 1), sem(NX - 1), sem(NX - 1), sem(NX - 1), sem(NX - 1),
            sem(NY - 1), sem(NY), sem(NZ - 1), sem(NZ - 1), sem(NY - 1), sem(NY),
            sem(NY - 1), pltpu.SemaphoreType.DMA, sem(3), sem(3),
        ],
        compiler_params=pltpu.CompilerParams(
            collective_id=0, has_side_effects=True, vmem_limit_bytes=56 * 1024 * 1024
        ),
        cost_estimate=pl.CostEstimate(
            flops=900_000_000, bytes_accessed=2_000_000, transcendentals=200_000
        ),
        name="window_grads",
    )(tokens, grad_out, ocean_mask, w_qkv, w_out)
    return pl.pallas_call(
        hand_over,
        out_shape=[jax.ShapeDtypeStruct(r.shape, r.dtype) for r in results],
        in_specs=[any_spec] * 3,
        out_specs=[any_spec] * 3,
        scratch_shapes=[sem(3)],
        compiler_params=pltpu.CompilerParams(vmem_limit_bytes=4 * 1024 * 1024),
        cost_estimate=pl.CostEstimate(flops=0, bytes_accessed=600_000, transcendentals=0),
        name="hand_over",
    )(*results)


def solution(mesh):
    return jax.shard_map(
        body,
        mesh=mesh,
        in_specs=(
            P("region", "tile", None),
            P("region", "tile", None),
            P("region", "tile"),
            P(),
            P(),
        ),
        out_specs=(P("region", "tile", None), P("tile", None), P("tile", None)),
        check_vma=False,
    )
```

```python
import math

import jax
import jax.numpy as jnp
from jax import lax
from jax.experimental import pallas as pl
from jax.experimental.pallas import tpu as pltpu
from jax.sharding import PartitionSpec as P

MESH = pl.DeviceIdType.MESH
F32 = jnp.float32
BF16 = jnp.bfloat16
D = 384
HD = 32
LOG2E = math.log2(math.e)
GROUPS = 3
NX, NZ, NY = 4, 8, 8
PY, PX, PZ = 0, 1, 2
AROUND = (3, 2, 6, 1, 7)
NT = (((1,), (1,)), ((), ()))


def dot(a, b, dims=(((1,), (0,)), ((), ()))):
    return lax.dot_general(a, b, dims, preferred_element_type=F32)


def roll4(a):
    n, _, width = a.shape
    return pltpu.roll(a.reshape(n * 8, width).reshape(n, 8, width), 4, 1)


def low4(shape):
    return lax.broadcasted_iota(jnp.int32, shape, len(shape) - 2) % 8 < 4


def part(array, a, first):
    return array[64 * a:64 * a + 64, first:first + 128]


def spread(array, a):
    lane_head = lax.broadcasted_iota(jnp.int32, (1, 128), 1) // HD
    order = (1, 0, 3, 2) if a else (0, 1, 2, 3)
    return jnp.concatenate(
        [array * (lane_head == h).astype(F32).astype(BF16) for h in order], axis=0
    )


def own(zero, one):
    first_half = lax.broadcasted_iota(jnp.int32, (1, 128), 1) < 64
    blocks = []
    for h in range(4):
        r, c = slice(32 * h, 32 * h + 32), slice(128 * (h // 2), 128 * (h // 2) + 128)
        if h % 2 == 0:
            blocks.append(jnp.where(first_half, zero[r, c], one[r, c]))
        else:
            blocks.append(pltpu.roll(jnp.where(first_half, one[r, c], zero[r, c]), 64, 1))
    return jnp.concatenate(blocks, axis=0).astype(BF16)


UNITS = [(a, g) for g in range(GROUPS) for a in range(2)]
ROOT = HD ** -0.5


def forward(feats, wq, normed_t, att_t, xhat, istd):
    center = jnp.mean(feats, axis=-1, keepdims=True)
    dev = feats - center
    inv = lax.rsqrt(jnp.mean(dev * dev, axis=-1, keepdims=True) + 1e-05)
    hat = dev * inv
    xhat[...] = hat
    istd[...] = jnp.broadcast_to(inv, (128, 128))
    nb = hat.astype(BF16)
    proj = dot(nb, wq[...]).astype(BF16)
    normed_t[...] = nb.T
    s = [
        dot(part(proj, a, D + 128 * g), spread(part(proj, a, 128 * g), a), NT) for a, g in UNITS
    ]
    vt = [part(proj, a, 2 * D + 128 * g).T for a, g in UNITS]
    p = []
    for t in s:
        e = jnp.exp2((t - jnp.max(t, axis=0, keepdims=True)) * (ROOT * LOG2E))
        p.append(e * (1.0 / jnp.sum(e, axis=0, keepdims=True)))
    ot = [dot(m, n.astype(BF16)) for m, n in zip(vt, p)]
    for g in range(GROUPS):
        att_t[128 * g:128 * g + 128, :] = own(ot[2 * g], ot[2 * g + 1])
    return proj, p


def backward(g, proj, p, ga, gp, query_t):
    qt = []
    for a in range(2):
        q, k = part(proj, a, 128 * g), part(proj, a, D + 128 * g)
        obd = spread(part(ga, a, 128 * g), a)
        dp = dot(part(proj, a, 2 * D + 128 * g), obd, NT)
        pa = p[2 * g + a]
        row = jnp.sum(dp * pa, axis=0, keepdims=True)
        ds = (pa * ((dp - row) * ROOT)).astype(BF16)
        at_row = pl.ds(64 * a, 64)
        gp[at_row, 128 * g:128 * g + 128] = dot(ds, spread(q, a)).astype(BF16)
        gp[at_row, D + 128 * g:D + 128 * g + 128] = dot(pa.astype(BF16), obd).astype(BF16)
        qt.append(dot(k.T, ds))
    query_t[128 * g:128 * g + 128, :] = own(qt[0], qt[1])


def device():
    region, tile = lax.axis_index("region"), lax.axis_index("tile")
    tiles = NX * NZ
    west = {"region": region, "tile": (tile + tiles - 1) % tiles}
    east = {"region": region, "tile": (tile + 1) % tiles}
    return region, tile, west, east


def send(src, dst, ss, rs, dev):
    return pltpu.make_async_remote_copy(
        src_ref=src, dst_ref=dst, send_sem=ss, recv_sem=rs, device_id=dev, device_id_type=MESH,
    )


def greet(partners):
    barrier = pltpu.get_barrier_semaphore()
    for dev in partners:
        pl.semaphore_signal(barrier, inc=1, device_id=dev, device_id_type=MESH)
    return lambda: pl.semaphore_wait(barrier, len(partners))


def pairs(v):
    v = v.reshape(8, 2, 8, D)
    return v[:, 0], v[:, 1]


def kernel(
    x_hbm, dy_hbm, mask_hbm, wq_hbm, wo_hbm,
    out_ref, gq_ref, go_ref,
    xv, dyv, mask_ref, wq, wo,
    rim_out, rim_in, back_out, back_in,
    normed_t0, att_t0, query_t0, gp0, xhat0, istd0, masked0,
    normed_t1, att_t1, query_t1, gp1, xhat1, istd1, masked1, branch,
    grads, r0, hx, hy, hz, relay_y, relay_z, r1x, r1y, r1z, jx, jy, jz,
    r2x, r2y, r2z, r3x, ky, r3y, r3z, fx, fy, fz,
    in_sem, rim_send, rim_recv, back_sem,
    s0, q0, s1x, q1x, s1y, q1y, s1z, q1z, s2x, q2x, s2y, q2y, s2z, q2z,
    s3x, q3x, s3y, q3y, s3z, q3z, s4y, q4y, s5, q5,
):
    loads = [
        pltpu.make_async_copy(src, dst, in_sem.at[i])
        for i, (src, dst) in enumerate(
            ((x_hbm, xv), (dy_hbm, dyv), (wq_hbm, wq), (wo_hbm, wo), (mask_hbm, mask_ref))
        )
    ]
    for c in loads:
        c.start()
    region, tile, west, east = device()
    y, core = region // 2, region % 2
    x, z = tile // NZ, tile % NZ
    tiles = NX * NZ

    def at(ax, ay, az, ac):
        return {"region": ay * 2 + ac, "tile": ax * NZ + az}

    other = at(x, y, z, 1 - core)
    by_x = [at((x + k) % NX, y, z, core) for k in range(1, NX)]
    by_z = [at(x, y, (z + k) % NZ, core) for k in range(1, NZ)]
    by_y = [at(x, (y + k) % NY, z, core) for k in range(1, NY)]
    greeted = greet([west, east, other] + by_x + by_z + by_y)
    sub = low4((1, 8, D))

    def halves(ref):
        v = ref[...].astype(F32)
        return v[:, :8, :], v[:, 8:, :]

    def rim_of(lo):
        even, odd = pairs(lo)
        return jnp.where(sub, even, roll4(odd)).reshape(64, D).astype(BF16)

    rims = [
        send(rim_out.at[i], rim_in.at[i], rim_send.at[i], rim_recv.at[i], west) for i in range(2)
    ]
    loads[0].wait()
    x_lo, x_hi = halves(xv)
    rim_out[0] = rim_of(x_lo)
    greeted()
    rims[0].start()
    loads[1].wait()
    dy_lo, dy_hi = halves(dyv)
    rim_out[1] = rim_of(dy_lo)
    rims[1].start()

    for c in loads[2:]:
        c.wait()
    flag = [[mask_ref[a, b].astype(F32) for a in range(2)] for b in range(2)]

    def mask_of(dys, b):
        return jnp.concatenate([dys[:64] * flag[b][0], dys[64:] * flag[b][1]], axis=0).astype(BF16)

    proj, p = forward(
        jnp.where(sub, x_hi, x_lo).reshape(128, D), wq, normed_t0, att_t0, xhat0, istd0
    )
    mk = mask_of(jnp.where(sub, dy_hi, dy_lo).reshape(128, D), 0)
    masked0[...] = mk
    ga = dot(mk, wo[...], NT).astype(BF16)
    for g in range(GROUPS):
        backward(g, proj, p, ga, gp0, query_t0)

    def joined(hi, far):
        even, odd = pairs(hi)
        loc = jnp.where(sub, roll4(even), odd).reshape(64, D)
        far = far.astype(F32)
        return jnp.concatenate([loc[:32], far[:32], loc[32:], far[32:]], axis=0)

    rims[0].wait()
    proj, p = forward(joined(x_hi, rim_in[0]), wq, normed_t1, att_t1, xhat1, istd1)
    rims[1].wait()
    masked1[...] = mask_of(joined(dy_hi, rim_in[1]), 1)
    ga = dot(masked1[...], wo[...], NT).astype(BF16)

    def both(a, b, axis):
        return jnp.concatenate([a, b], axis=axis)

    nt = both(normed_t0[...], normed_t1[...], 1)
    ga_full = dot(
        both(att_t0[...], att_t1[...], 1), both(masked0[...], masked1[...], 0)
    ).reshape(16, 3, 8, D)
    w0, w1, w2 = ga_full[:, 0], ga_full[:, 1], ga_full[:, 2]
    spare = [
        roll4(jnp.where(sub, w0, w1)),
        jnp.where(sub, w2, w0),
        roll4(jnp.where(sub, w1, w2)),
    ]
    sends = []

    def start(c):
        c.start()
        sends.append(c)
        return c

    keep = {PX: core, PY: 1 - core, PZ: 1 - core}
    core0 = []
    for g in range(GROUPS):
        backward(g, proj, p, ga, gp1, query_t1)
        at_g = slice(128 * g, 128 * g + 128)
        at_gv = slice(D + 128 * g, D + 128 * g + 128)
        gn = jnp.concatenate([
            dot(nt, both(query_t0[at_g, :], query_t1[at_g, :], 1), NT),
            dot(nt, both(gp0[:, at_g], gp1[:, at_g], 0)),
            dot(nt, both(gp0[:, at_gv], gp1[:, at_gv], 0)),
        ], axis=1).reshape(16, 3, 8, D)
        v0, v1, v2 = gn[:, 0], gn[:, 1], gn[:, 2]
        packed = jnp.stack(
            [v0, jnp.where(sub, v1, spare[g]), v2, jnp.where(sub, spare[g], v1)], axis=1
        ).reshape(NX, NZ, 16, D).astype(BF16)
        grads[g] = packed
        core0.append(start(send(
            grads.at[g, :, pl.ds((1 - keep[g]) * 4, 4)], r0.at[g], s0.at[g], q0.at[g], other,
        )))

    def start_if(copies):
        for c, yes in copies:
            pl.when(yes)(c.start)

    def combined(part):
        core0[part].wait_recv()
        mine = grads[part, :, pl.ds(keep[part] * 4, 4)].astype(F32)
        return (mine + r0[part].astype(F32)).astype(BF16)

    def around(buf, slots, relay, ss, qs, devs, place, half):
        def copy(k, slot, dev):
            to = (place + k) % 8
            c = send(buf.at[:, to % 4], slot, ss.at[k - 1], qs.at[k - 1], devs[dev - 1])
            return c, to // 4 == half

        return (
            [copy(4, relay, 7)] + [copy(k, slots.at[k - 1], k) for k in AROUND],
            copy(5, slots.at[4], 5),
        )

    def pass_on(buf, relay, first, last, place):
        arrived, (c, yes) = first[0][0], last
        at_chunk = (place + 5) % 4

        @pl.when(yes)
        def _():
            arrived.wait_recv()
            t = buf[:, at_chunk].astype(F32) + relay[...].astype(F32)
            buf[:, at_chunk] = t.astype(BF16)
            c.start()

    p1y, p1y_last = around(hy, r1y, relay_y, s1y, q1y, by_y, y, keep[PY])
    p1z, p1z_last = around(hz, r1z, relay_z, s1z, q1z, by_z, z, keep[PZ])
    hy[...] = combined(PY)
    start_if(p1y)
    hx[...] = combined(PX)
    p1x = [
        start(send(hx.at[(x + k) % NX], r1x.at[k - 1], s1x.at[k - 1], q1x.at[k - 1], by_x[k - 1]))
        for k in (2, 1, 3)
    ]
    hz[...] = combined(PZ)
    start_if(p1z)
    pass_on(hy, relay_y, p1y, p1y_last, y)
    pass_on(hz, relay_z, p1z, p1z_last, z)

    gn = dot(both(query_t0[...].T, query_t1[...].T, 0), wq[:, 0:D], NT)
    gn = gn + dot(both(gp0[...], gp1[...], 0), wq[:, D:3 * D], NT)
    hat = both(xhat0[...], xhat1[...], 0)
    inv = both(istd0[:, 0:1], istd1[:, 0:1], 0)
    m0 = jnp.mean(gn, axis=-1, keepdims=True)
    m1 = jnp.mean(gn * hat, axis=-1, keepdims=True)
    br = (inv * (gn - m0 - hat * m1)).astype(BF16)
    branch[...] = br[0:128].astype(F32)
    back_out[0:32, :] = br[160:192]
    back_out[32:64, :] = br[224:256]
    loc = jnp.concatenate([br[128:160], br[192:224]], axis=0).astype(F32).reshape(8, 8, D)

    has_x = z // 4 == core
    has_z = z // 4 != core
    mid_y = y // 4 != core

    def total(first, buf, slots):
        t = first.astype(F32)
        for i in slots:
            t = t + buf[i].astype(F32)
        return t.astype(BF16)

    def over_x(buf, slots, ss, qs):
        return [
            send(buf.at[(x + k) % NX], slots.at[k - 1], ss.at[k - 1], qs.at[k - 1], by_x[k - 1])
            for k in (2, 1, 3)
        ]

    def over_z(buf, slots, ss, qs):
        out = []
        for k in (4, 3, 5, 2, 6, 1, 7):
            to = (z + k) % NZ
            c = send(buf.at[to % 4], slots.at[k - 1], ss.at[k - 1], qs.at[k - 1], by_z[k - 1])
            out.append((c, to // 4 == core))
        return out

    p2y = over_x(jy, r2y, s2y, q2y)
    p2x = over_z(jx, r2x, s2x, q2x)
    p2z = over_x(jz, r2z, s2z, q2z)
    direct = tuple(k - 1 for k in AROUND)

    def arrived(first, last):
        for c, _ in first[1:]:
            c.wait_recv()
        last[0].wait_recv()

    @pl.when(mid_y)
    def _():
        arrived(p1y, p1y_last)
        jy[...] = total(hy[:, y % 4], r1y, direct + (4,))
        for c in p2y:
            c.start()

    for c in p1x:
        c.wait_recv()
    jx[...] = total(hx[x], r1x, range(NX - 1))
    start_if(p2x)

    @pl.when(has_z)
    def _():
        arrived(p1z, p1z_last)
        jz[...] = total(hz[:, z % 4], r1z, direct + (4,))
        for c in p2z:
            c.start()

    back = start(send(back_out, back_in, back_sem.at[0], back_sem.at[1], east))

    def y_copies(buf, ss, qs):
        return [
            send(buf.at[y], buf.at[y], ss.at[k - 1], qs.at[y], by_y[k - 1])
            for k in (4, 3, 5, 2, 6, 1, 7)
        ]

    def y_arrivals(buf, ss, qs):
        return [
            send(buf.at[y], buf.at[(y + k) % NY], ss.at[k - 1], qs.at[(y + k) % NY], by_y[k - 1])
            for k in range(1, NY)
        ]

    own_y = jnp.logical_and(has_z, y == z)
    p3y = [
        (send(ky, r3y.at[k - 1], s3y.at[k - 1], q3y.at[k - 1], by_z[k - 1]), (z + k) % NZ == y)
        for k in range(1, NZ)
    ]
    p4y = [send(fy, fy, s4y.at[k], q4y, dev) for k, dev in enumerate(by_y)]

    @pl.when(mid_y)
    def _():
        for c in p2y:
            c.wait_recv()
        ky[...] = total(jy[x], r2y, range(NX - 1))
        start_if(p3y)

    @pl.when(has_x)
    def _():
        for c, _ in p2x:
            c.wait_recv()
        r3x[y] = total(jx[z % 4], r2x, range(NZ - 1))
        for c in y_copies(r3x, s3x, q3x):
            c.start()

    @pl.when(has_z)
    def _():
        for c in p2z:
            c.wait_recv()
        r3z[y] = total(jz[x], r2z, range(NX - 1))
        for c in y_copies(r3z, s3z, q3z):
            c.start()

    @pl.when(own_y)
    def _():
        for c, _ in p3y:
            c.wait_recv()
        fy[...] = total(ky[...], r3y, range(NZ - 1))
        for c in p4y:
            c.start()

    back.wait_recv()
    far = back_in[...].astype(F32).reshape(8, 8, D)
    br0 = branch[...].reshape(16, 8, D)

    def unpaired(even, odd):
        return jnp.stack([even, odd], axis=1).reshape(16, 8, D)

    new_lo = dyv[:, :8, :].astype(F32) + jnp.where(sub, unpaired(far, roll4(far)), br0)
    new_hi = dyv[:, 8:, :].astype(F32) + jnp.where(sub, br0, unpaired(roll4(loc), loc))
    out_ref[...] = jnp.concatenate([new_lo, new_hi], axis=1).astype(BF16)

    last_x = send(fx, fx, s5.at[0], q5.at[0], other)
    last_y = send(fy, fy, s5.at[1], q5.at[1], other)
    last_z = send(fz, fz, s5.at[2], q5.at[2], other)

    def settle(buf, out, ss, qs, last):
        for c in y_arrivals(buf, ss, qs):
            c.wait_recv()
        out[...] = total(buf[0], buf, range(1, NY))
        last.start()

    @pl.when(has_x)
    def _():
        settle(r3x, fx, s3x, q3x, last_x)

    @pl.when(has_z)
    def _():
        settle(r3z, fz, s3z, q3z, last_z)
        pl.when(y != z)(p4y[0].wait_recv)
        last_y.start()

    @pl.when(jnp.logical_not(has_x))
    def _():
        last_x.wait_recv()

    @pl.when(jnp.logical_not(has_z))
    def _():
        last_z.wait_recv()
        last_y.wait_recv()

    scale = 1.0 / math.sqrt(3 * 64 * 2 * NY * tiles)
    odd = (z % 2) == 1
    final = jnp.concatenate([fy[...], fx[...], fz[...]], axis=1).astype(F32) * scale
    for g in range(GROUPS):
        f = final[:, D * g:D * g + D]
        top, bot = f[0:8], f[8:16]
        top_r, bot_r = pltpu.roll(top, 4, 0), pltpu.roll(bot, 4, 0)
        low = low4((8, D))
        first = jnp.where(odd, jnp.where(low, bot_r, top_r), top)
        rest = jnp.where(odd, top_r, bot)
        extra = jnp.where(odd, bot, bot_r)
        for s in range(3):
            lanes = slice(s * D + 128 * g, s * D + 128 * g + 128)
            gq_ref[0:8, lanes] = first[:, 128 * s:128 * s + 128]
            gq_ref[8:12, lanes] = rest[0:4, 128 * s:128 * s + 128]
        go_ref[4 * g:4 * g + 4, :] = extra[0:4]

    def sent_if(copies):
        for c, yes in copies:
            pl.when(yes)(c.wait_send)

    for c in sends:
        c.wait_send()
    sent_if(p1y + [p1y_last] + p1z + [p1z_last] + p2x)

    @pl.when(mid_y)
    def _():
        for c in p2y:
            c.wait_send()
        sent_if(p3y)

    @pl.when(has_x)
    def _():
        for c in y_copies(r3x, s3x, q3x):
            c.wait_send()
        last_x.wait_send()

    @pl.when(has_z)
    def _():
        for c in p2z + y_copies(r3z, s3z, q3z):
            c.wait_send()
        last_z.wait_send()
        last_y.wait_send()

    @pl.when(own_y)
    def _():
        for c in p4y:
            c.wait_send()


def hand_over(a, b, c, a_out, b_out, c_out, sems):
    copies = [
        pltpu.make_async_copy(src, dst, sems.at[i])
        for i, (src, dst) in enumerate(((a, a_out), (b, b_out), (c, c_out)))
    ]
    for c in copies:
        c.start()
    for c in copies:
        c.wait()


def body(tokens, grad_out, ocean_mask, w_qkv, w_out):
    any_spec = pl.BlockSpec(memory_space=pl.ANY)
    vmem_spec = pl.BlockSpec(memory_space=pltpu.VMEM)

    def buf(*shape, dtype=BF16):
        return pltpu.VMEM(shape, dtype)

    def sem(*shape):
        return pltpu.SemaphoreType.DMA(shape)

    column = [
        buf(D, 128), buf(D, 128), buf(D, 128), buf(128, 2 * D),
        buf(128, D, dtype=F32), buf(128, 128, dtype=F32), buf(128, D),
    ]
    results = pl.pallas_call(
        kernel,
        out_shape=(buf(16, 16, D), buf(12, 3 * D, dtype=F32), buf(12, D, dtype=F32)),
        in_specs=[any_spec] * 5,
        out_specs=(vmem_spec, vmem_spec, vmem_spec),
        scratch_shapes=[
            buf(16, 16, D), buf(16, 16, D), pltpu.SMEM((2, 2), jnp.int32),
            buf(D, 3 * D), buf(D, D),
            buf(2, 64, D), buf(2, 64, D), buf(64, D), buf(64, D),
            *column, *column, buf(128, D, dtype=F32),
            buf(3, NX, 8, 16, D), buf(3, NX, 4, 16, D),
            buf(NX, 4, 16, D), buf(NX, 4, 16, D), buf(NX, 4, 16, D),
            buf(NX, 16, D), buf(NX, 16, D),
            buf(NX - 1, 4, 16, D), buf(NY - 1, NX, 16, D), buf(NZ - 1, NX, 16, D),
            buf(4, 16, D), buf(NX, 16, D), buf(NX, 16, D),
            buf(NZ - 1, 16, D), buf(NX - 1, 16, D), buf(NX - 1, 16, D),
            buf(NY, 16, D), buf(16, D), buf(NZ - 1, 16, D), buf(NY, 16, D),
            buf(16, D), buf(16, D), buf(16, D),
            sem(5), sem(2), sem(2), sem(2),
            sem(3), sem(3), sem(NX - 1), sem(NX - 1),
            sem(NY - 1), sem(NY - 1), sem(NZ - 1), sem(NZ - 1),
            sem(NZ - 1), sem(NZ - 1), sem(NX - 1), sem(NX - 1), sem(NX - 1), sem(NX - 1),
            sem(NY - 1), sem(NY), sem(NZ - 1), sem(NZ - 1), sem(NY - 1), sem(NY),
            sem(NY - 1), pltpu.SemaphoreType.DMA, sem(3), sem(3),
        ],
        compiler_params=pltpu.CompilerParams(
            collective_id=0, has_side_effects=True, vmem_limit_bytes=56 * 1024 * 1024
        ),
        cost_estimate=pl.CostEstimate(
            flops=900_000_000, bytes_accessed=2_000_000, transcendentals=200_000
        ),
        name="window_grads",
    )(tokens, grad_out, ocean_mask, w_qkv, w_out)
    return pl.pallas_call(
        hand_over,
        out_shape=[jax.ShapeDtypeStruct(r.shape, r.dtype) for r in results],
        in_specs=[any_spec] * 3,
        out_specs=[any_spec] * 3,
        scratch_shapes=[sem(3)],
        compiler_params=pltpu.CompilerParams(vmem_limit_bytes=4 * 1024 * 1024),
        cost_estimate=pl.CostEstimate(flops=0, bytes_accessed=600_000, transcendentals=0),
        name="hand_over",
    )(*results)


def solution(mesh):
    return jax.shard_map(
        body,
        mesh=mesh,
        in_specs=(
            P("region", "tile", None),
            P("region", "tile", None),
            P("region", "tile"),
            P(),
            P(),
        ),
        out_specs=(P("region", "tile", None), P("tile", None), P("tile", None)),
        check_vma=False,
    )
```

```python
import math

import jax
import jax.numpy as jnp
from jax import lax
from jax.experimental import pallas as pl
from jax.experimental.pallas import tpu as pltpu
from jax.sharding import PartitionSpec as P

MESH = pl.DeviceIdType.MESH
F32 = jnp.float32
BF16 = jnp.bfloat16
D = 384
HD = 32
LOG2E = math.log2(math.e)
GROUPS = 3
NX, NZ, NY = 4, 8, 8
PY, PX, PZ = 0, 1, 2
AROUND = (3, 2, 6, 1, 7)
NT = (((1,), (1,)), ((), ()))


def dot(a, b, dims=(((1,), (0,)), ((), ()))):
    return lax.dot_general(a, b, dims, preferred_element_type=F32)


def roll4(a):
    n, _, width = a.shape
    return pltpu.roll(a.reshape(n * 8, width).reshape(n, 8, width), 4, 1)


def low4(shape):
    return lax.broadcasted_iota(jnp.int32, shape, len(shape) - 2) % 8 < 4


def part(array, a, first):
    return array[64 * a:64 * a + 64, first:first + 128]


def spread(array, a):
    lane_head = lax.broadcasted_iota(jnp.int32, (1, 128), 1) // HD
    order = (1, 0, 3, 2) if a else (0, 1, 2, 3)
    return jnp.concatenate(
        [array * (lane_head == h).astype(F32).astype(BF16) for h in order], axis=0
    )


def own(zero, one):
    first_half = lax.broadcasted_iota(jnp.int32, (1, 128), 1) < 64
    blocks = []
    for h in range(4):
        r, c = slice(32 * h, 32 * h + 32), slice(128 * (h // 2), 128 * (h // 2) + 128)
        if h % 2 == 0:
            blocks.append(jnp.where(first_half, zero[r, c], one[r, c]))
        else:
            blocks.append(pltpu.roll(jnp.where(first_half, one[r, c], zero[r, c]), 64, 1))
    return jnp.concatenate(blocks, axis=0).astype(BF16)


UNITS = [(a, g) for g in range(GROUPS) for a in range(2)]
ROOT = HD ** -0.5


def normalise(feats, normed_t, xhat, istd):
    center = jnp.mean(feats, axis=-1, keepdims=True)
    dev = feats - center
    inv = lax.rsqrt(jnp.mean(dev * dev, axis=-1, keepdims=True) + 1e-05)
    hat = dev * inv
    xhat[...] = hat
    istd[...] = jnp.broadcast_to(inv, (128, 128))
    nb = hat.astype(BF16)
    normed_t[...] = nb.T
    return nb


def scores(proj, ga):
    q = [spread(part(proj, a, 128 * g), a) for a, g in UNITS]
    o = [spread(part(ga, a, 128 * g), a) for a, g in UNITS]
    k = [part(proj, a, D + 128 * g) for a, g in UNITS]
    v = [part(proj, a, 2 * D + 128 * g) for a, g in UNITS]
    s = [dot(m, n, NT) for m, n in zip(k, q)]
    dp = [dot(m, n, NT) for m, n in zip(v, o)]
    return q, o, [m.T for m in k], [m.T for m in v], s, dp


def softmax_grads(s, dp):
    pb, ds = [], []
    for t, d in zip(s, dp):
        e = jnp.exp2((t - jnp.max(t, axis=0, keepdims=True)) * (ROOT * LOG2E))
        p = e * (1.0 / jnp.sum(e, axis=0, keepdims=True))
        row = jnp.sum(d * p, axis=0, keepdims=True)
        pb.append(p.astype(BF16))
        ds.append((p * ((d - row) * ROOT)).astype(BF16))
    return pb, ds


def products(q, o, kt, vt, pb, ds):
    qt = [dot(m, n) for m, n in zip(kt, ds)]
    dk = [dot(m, n) for m, n in zip(ds, q)]
    dv = [dot(m, n) for m, n in zip(pb, o)]
    ot = [dot(m, n) for m, n in zip(vt, pb)]
    return qt, dk, dv, ot


def keep_products(qt, dk, dv, ot, att_t, query_t, gp):
    for i, (a, g) in enumerate(UNITS):
        at_row = pl.ds(64 * a, 64)
        gp[at_row, 128 * g:128 * g + 128] = dk[i].astype(BF16)
        gp[at_row, D + 128 * g:D + 128 * g + 128] = dv[i].astype(BF16)
    for g in range(GROUPS):
        query_t[128 * g:128 * g + 128, :] = own(qt[2 * g], qt[2 * g + 1])
        att_t[128 * g:128 * g + 128, :] = own(ot[2 * g], ot[2 * g + 1])


def device():
    region, tile = lax.axis_index("region"), lax.axis_index("tile")
    tiles = NX * NZ
    west = {"region": region, "tile": (tile + tiles - 1) % tiles}
    east = {"region": region, "tile": (tile + 1) % tiles}
    return region, tile, west, east


def send(src, dst, ss, rs, dev):
    return pltpu.make_async_remote_copy(
        src_ref=src, dst_ref=dst, send_sem=ss, recv_sem=rs, device_id=dev, device_id_type=MESH,
    )


def greet(partners):
    barrier = pltpu.get_barrier_semaphore()
    for dev in partners:
        pl.semaphore_signal(barrier, inc=1, device_id=dev, device_id_type=MESH)
    return lambda: pl.semaphore_wait(barrier, len(partners))


def pairs(v):
    v = v.reshape(8, 2, 8, D)
    return v[:, 0], v[:, 1]


def kernel(
    x_hbm, dy_hbm, mask_hbm, wq_hbm, wo_hbm,
    out_ref, gq_ref, go_ref,
    xv, dyv, mask_ref, wq, wo,
    rim_out, rim_in, back_out, back_in,
    normed_t0, att_t0, query_t0, gp0, xhat0, istd0, masked0,
    normed_t1, att_t1, query_t1, gp1, xhat1, istd1, masked1, branch,
    grads, r0, hx, hy, hz, relay_y, relay_z, r1x, r1y, r1z, jx, jy, jz,
    r2x, r2y, r2z, r3x, ky, r3y, r3z, fx, fy, fz,
    in_sem, rim_send, rim_recv, back_sem,
    s0, q0, s1x, q1x, s1y, q1y, s1z, q1z, s2x, q2x, s2y, q2y, s2z, q2z,
    s3x, q3x, s3y, q3y, s3z, q3z, s4y, q4y, s5, q5,
):
    loads = [
        pltpu.make_async_copy(src, dst, in_sem.at[i])
        for i, (src, dst) in enumerate(
            ((x_hbm, xv), (dy_hbm, dyv), (wq_hbm, wq), (wo_hbm, wo), (mask_hbm, mask_ref))
        )
    ]
    for c in loads:
        c.start()
    region, tile, west, east = device()
    y, core = region // 2, region % 2
    x, z = tile // NZ, tile % NZ
    tiles = NX * NZ

    def at(ax, ay, az, ac):
        return {"region": ay * 2 + ac, "tile": ax * NZ + az}

    other = at(x, y, z, 1 - core)
    by_x = [at((x + k) % NX, y, z, core) for k in range(1, NX)]
    by_z = [at(x, y, (z + k) % NZ, core) for k in range(1, NZ)]
    by_y = [at(x, (y + k) % NY, z, core) for k in range(1, NY)]
    greeted = greet([west, east, other] + by_x + by_z + by_y)
    sub = low4((1, 8, D))

    def halves(ref):
        v = ref[...].astype(F32)
        return v[:, :8, :], v[:, 8:, :]

    def rim_of(lo):
        even, odd = pairs(lo)
        return jnp.where(sub, even, roll4(odd)).reshape(64, D).astype(BF16)

    rims = [
        send(rim_out.at[i], rim_in.at[i], rim_send.at[i], rim_recv.at[i], west) for i in range(2)
    ]
    loads[0].wait()
    x_lo, x_hi = halves(xv)
    rim_out[0] = rim_of(x_lo)
    greeted()
    rims[0].start()
    loads[1].wait()
    dy_lo, dy_hi = halves(dyv)
    rim_out[1] = rim_of(dy_lo)
    rims[1].start()

    for c in loads[2:]:
        c.wait()
    flag = [[mask_ref[a, b].astype(F32) for a in range(2)] for b in range(2)]

    def mask_of(dys, b):
        return jnp.concatenate([dys[:64] * flag[b][0], dys[64:] * flag[b][1]], axis=0).astype(BF16)

    nb = normalise(jnp.where(sub, x_hi, x_lo).reshape(128, D), normed_t0, xhat0, istd0)
    mk = mask_of(jnp.where(sub, dy_hi, dy_lo).reshape(128, D), 0)
    masked0[...] = mk
    ga = dot(mk, wo[...], NT).astype(BF16)
    proj = dot(nb, wq[...]).astype(BF16)
    q, o, kt, vt, sc, dp = scores(proj, ga)

    def joined(hi, far):
        even, odd = pairs(hi)
        loc = jnp.where(sub, roll4(even), odd).reshape(64, D)
        far = far.astype(F32)
        return jnp.concatenate([loc[:32], far[:32], loc[32:], far[32:]], axis=0)

    rims[0].wait()
    nb = normalise(joined(x_hi, rim_in[0]), normed_t1, xhat1, istd1)
    pb, ds = softmax_grads(sc, dp)
    proj = dot(nb, wq[...]).astype(BF16)
    first = products(q, o, kt, vt, pb, ds)
    rims[1].wait()
    mk = mask_of(joined(dy_hi, rim_in[1]), 1)
    masked1[...] = mk
    ga = dot(mk, wo[...], NT).astype(BF16)
    q, o, kt, vt, sc, dp = scores(proj, ga)
    keep_products(*first, att_t0, query_t0, gp0)
    pb, ds = softmax_grads(sc, dp)
    keep_products(*products(q, o, kt, vt, pb, ds), att_t1, query_t1, gp1)

    def both(a, b, axis):
        return jnp.concatenate([a, b], axis=axis)

    nt = both(normed_t0[...], normed_t1[...], 1)
    ga_full = dot(
        both(att_t0[...], att_t1[...], 1), both(masked0[...], masked1[...], 0)
    ).reshape(16, 3, 8, D)
    w0, w1, w2 = ga_full[:, 0], ga_full[:, 1], ga_full[:, 2]
    spare = [
        roll4(jnp.where(sub, w0, w1)),
        jnp.where(sub, w2, w0),
        roll4(jnp.where(sub, w1, w2)),
    ]
    sends = []

    def start(c):
        c.start()
        sends.append(c)
        return c

    keep = {PX: core, PY: 1 - core, PZ: 1 - core}
    core0 = []
    for g in range(GROUPS):
        at_g = slice(128 * g, 128 * g + 128)
        at_gv = slice(D + 128 * g, D + 128 * g + 128)
        gn = jnp.concatenate([
            dot(nt, both(query_t0[at_g, :], query_t1[at_g, :], 1), NT),
            dot(nt, both(gp0[:, at_g], gp1[:, at_g], 0)),
            dot(nt, both(gp0[:, at_gv], gp1[:, at_gv], 0)),
        ], axis=1).reshape(16, 3, 8, D)
        v0, v1, v2 = gn[:, 0], gn[:, 1], gn[:, 2]
        packed = jnp.stack(
            [v0, jnp.where(sub, v1, spare[g]), v2, jnp.where(sub, spare[g], v1)], axis=1
        ).reshape(NX, NZ, 16, D).astype(BF16)
        grads[g] = packed
        core0.append(start(send(
            grads.at[g, :, pl.ds((1 - keep[g]) * 4, 4)], r0.at[g], s0.at[g], q0.at[g], other,
        )))

    def start_if(copies):
        for c, yes in copies:
            pl.when(yes)(c.start)

    def combined(part):
        core0[part].wait_recv()
        mine = grads[part, :, pl.ds(keep[part] * 4, 4)].astype(F32)
        return (mine + r0[part].astype(F32)).astype(BF16)

    def around(buf, slots, relay, ss, qs, devs, place, half):
        def copy(k, slot, dev):
            to = (place + k) % 8
            c = send(buf.at[:, to % 4], slot, ss.at[k - 1], qs.at[k - 1], devs[dev - 1])
            return c, to // 4 == half

        return (
            [copy(4, relay, 7)] + [copy(k, slots.at[k - 1], k) for k in AROUND],
            copy(5, slots.at[4], 5),
        )

    def pass_on(buf, relay, first, last, place):
        arrived, (c, yes) = first[0][0], last
        at_chunk = (place + 5) % 4

        @pl.when(yes)
        def _():
            arrived.wait_recv()
            t = buf[:, at_chunk].astype(F32) + relay[...].astype(F32)
            buf[:, at_chunk] = t.astype(BF16)
            c.start()

    p1y, p1y_last = around(hy, r1y, relay_y, s1y, q1y, by_y, y, keep[PY])
    p1z, p1z_last = around(hz, r1z, relay_z, s1z, q1z, by_z, z, keep[PZ])
    hy[...] = combined(PY)
    start_if(p1y)
    hx[...] = combined(PX)
    p1x = [
        start(send(hx.at[(x + k) % NX], r1x.at[k - 1], s1x.at[k - 1], q1x.at[k - 1], by_x[k - 1]))
        for k in (2, 1, 3)
    ]
    hz[...] = combined(PZ)
    start_if(p1z)
    pass_on(hy, relay_y, p1y, p1y_last, y)
    pass_on(hz, relay_z, p1z, p1z_last, z)

    gn = dot(both(query_t0[...].T, query_t1[...].T, 0), wq[:, 0:D], NT)
    gn = gn + dot(both(gp0[...], gp1[...], 0), wq[:, D:3 * D], NT)
    hat = both(xhat0[...], xhat1[...], 0)
    inv = both(istd0[:, 0:1], istd1[:, 0:1], 0)
    m0 = jnp.mean(gn, axis=-1, keepdims=True)
    m1 = jnp.mean(gn * hat, axis=-1, keepdims=True)
    br = (inv * (gn - m0 - hat * m1)).astype(BF16)
    branch[...] = br[0:128].astype(F32)
    back_out[0:32, :] = br[160:192]
    back_out[32:64, :] = br[224:256]
    loc = jnp.concatenate([br[128:160], br[192:224]], axis=0).astype(F32).reshape(8, 8, D)

    has_x = z // 4 == core
    has_z = z // 4 != core
    mid_y = y // 4 != core

    def total(first, buf, slots):
        t = first.astype(F32)
        for i in slots:
            t = t + buf[i].astype(F32)
        return t.astype(BF16)

    def over_x(buf, slots, ss, qs):
        return [
            send(buf.at[(x + k) % NX], slots.at[k - 1], ss.at[k - 1], qs.at[k - 1], by_x[k - 1])
            for k in (2, 1, 3)
        ]

    def over_z(buf, slots, ss, qs):
        out = []
        for k in (4, 3, 5, 2, 6, 1, 7):
            to = (z + k) % NZ
            c = send(buf.at[to % 4], slots.at[k - 1], ss.at[k - 1], qs.at[k - 1], by_z[k - 1])
            out.append((c, to // 4 == core))
        return out

    p2y = over_x(jy, r2y, s2y, q2y)
    p2x = over_z(jx, r2x, s2x, q2x)
    p2z = over_x(jz, r2z, s2z, q2z)
    direct = tuple(k - 1 for k in AROUND)

    def arrived(first, last):
        for c, _ in first[1:]:
            c.wait_recv()
        last[0].wait_recv()

    @pl.when(mid_y)
    def _():
        arrived(p1y, p1y_last)
        jy[...] = total(hy[:, y % 4], r1y, direct + (4,))
        for c in p2y:
            c.start()

    for c in p1x:
        c.wait_recv()
    jx[...] = total(hx[x], r1x, range(NX - 1))
    start_if(p2x)

    @pl.when(has_z)
    def _():
        arrived(p1z, p1z_last)
        jz[...] = total(hz[:, z % 4], r1z, direct + (4,))
        for c in p2z:
            c.start()

    back = start(send(back_out, back_in, back_sem.at[0], back_sem.at[1], east))

    def y_copies(buf, ss, qs):
        return [
            send(buf.at[y], buf.at[y], ss.at[k - 1], qs.at[y], by_y[k - 1])
            for k in (4, 3, 5, 2, 6, 1, 7)
        ]

    def y_arrivals(buf, ss, qs):
        return [
            send(buf.at[y], buf.at[(y + k) % NY], ss.at[k - 1], qs.at[(y + k) % NY], by_y[k - 1])
            for k in range(1, NY)
        ]

    own_y = jnp.logical_and(has_z, y == z)
    p3y = [
        (send(ky, r3y.at[k - 1], s3y.at[k - 1], q3y.at[k - 1], by_z[k - 1]), (z + k) % NZ == y)
        for k in range(1, NZ)
    ]
    p4y = [send(fy, fy, s4y.at[k], q4y, dev) for k, dev in enumerate(by_y)]

    @pl.when(mid_y)
    def _():
        for c in p2y:
            c.wait_recv()
        ky[...] = total(jy[x], r2y, range(NX - 1))
        start_if(p3y)

    @pl.when(has_x)
    def _():
        for c, _ in p2x:
            c.wait_recv()
        r3x[y] = total(jx[z % 4], r2x, range(NZ - 1))
        for c in y_copies(r3x, s3x, q3x):
            c.start()

    @pl.when(has_z)
    def _():
        for c in p2z:
            c.wait_recv()
        r3z[y] = total(jz[x], r2z, range(NX - 1))
        for c in y_copies(r3z, s3z, q3z):
            c.start()

    @pl.when(own_y)
    def _():
        for c, _ in p3y:
            c.wait_recv()
        fy[...] = total(ky[...], r3y, range(NZ - 1))
        for c in p4y:
            c.start()

    back.wait_recv()
    far = back_in[...].astype(F32).reshape(8, 8, D)
    br0 = branch[...].reshape(16, 8, D)

    def unpaired(even, odd):
        return jnp.stack([even, odd], axis=1).reshape(16, 8, D)

    new_lo = dyv[:, :8, :].astype(F32) + jnp.where(sub, unpaired(far, roll4(far)), br0)
    new_hi = dyv[:, 8:, :].astype(F32) + jnp.where(sub, br0, unpaired(roll4(loc), loc))
    out_ref[...] = jnp.concatenate([new_lo, new_hi], axis=1).astype(BF16)

    last_x = send(fx, fx, s5.at[0], q5.at[0], other)
    last_y = send(fy, fy, s5.at[1], q5.at[1], other)
    last_z = send(fz, fz, s5.at[2], q5.at[2], other)

    def settle(buf, out, ss, qs, last):
        for c in y_arrivals(buf, ss, qs):
            c.wait_recv()
        out[...] = total(buf[0], buf, range(1, NY))
        last.start()

    @pl.when(has_x)
    def _():
        settle(r3x, fx, s3x, q3x, last_x)

    @pl.when(has_z)
    def _():
        settle(r3z, fz, s3z, q3z, last_z)
        pl.when(y != z)(p4y[0].wait_recv)
        last_y.start()

    @pl.when(jnp.logical_not(has_x))
    def _():
        last_x.wait_recv()

    @pl.when(jnp.logical_not(has_z))
    def _():
        last_z.wait_recv()
        last_y.wait_recv()

    scale = 1.0 / math.sqrt(3 * 64 * 2 * NY * tiles)
    odd = (z % 2) == 1
    final = jnp.concatenate([fy[...], fx[...], fz[...]], axis=1).astype(F32) * scale
    for g in range(GROUPS):
        f = final[:, D * g:D * g + D]
        top, bot = f[0:8], f[8:16]
        top_r, bot_r = pltpu.roll(top, 4, 0), pltpu.roll(bot, 4, 0)
        low = low4((8, D))
        first = jnp.where(odd, jnp.where(low, bot_r, top_r), top)
        rest = jnp.where(odd, top_r, bot)
        extra = jnp.where(odd, bot, bot_r)
        for s in range(3):
            lanes = slice(s * D + 128 * g, s * D + 128 * g + 128)
            gq_ref[0:8, lanes] = first[:, 128 * s:128 * s + 128]
            gq_ref[8:12, lanes] = rest[0:4, 128 * s:128 * s + 128]
        go_ref[4 * g:4 * g + 4, :] = extra[0:4]

    def sent_if(copies):
        for c, yes in copies:
            pl.when(yes)(c.wait_send)

    for c in sends:
        c.wait_send()
    sent_if(p1y + [p1y_last] + p1z + [p1z_last] + p2x)

    @pl.when(mid_y)
    def _():
        for c in p2y:
            c.wait_send()
        sent_if(p3y)

    @pl.when(has_x)
    def _():
        for c in y_copies(r3x, s3x, q3x):
            c.wait_send()
        last_x.wait_send()

    @pl.when(has_z)
    def _():
        for c in p2z + y_copies(r3z, s3z, q3z):
            c.wait_send()
        last_z.wait_send()
        last_y.wait_send()

    @pl.when(own_y)
    def _():
        for c in p4y:
            c.wait_send()


def hand_over(a, b, c, a_out, b_out, c_out, sems):
    copies = [
        pltpu.make_async_copy(src, dst, sems.at[i])
        for i, (src, dst) in enumerate(((a, a_out), (b, b_out), (c, c_out)))
    ]
    for c in copies:
        c.start()
    for c in copies:
        c.wait()


def body(tokens, grad_out, ocean_mask, w_qkv, w_out):
    any_spec = pl.BlockSpec(memory_space=pl.ANY)
    vmem_spec = pl.BlockSpec(memory_space=pltpu.VMEM)

    def buf(*shape, dtype=BF16):
        return pltpu.VMEM(shape, dtype)

    def sem(*shape):
        return pltpu.SemaphoreType.DMA(shape)

    column = [
        buf(D, 128), buf(D, 128), buf(D, 128), buf(128, 2 * D),
        buf(128, D, dtype=F32), buf(128, 128, dtype=F32), buf(128, D),
    ]
    results = pl.pallas_call(
        kernel,
        out_shape=(buf(16, 16, D), buf(12, 3 * D, dtype=F32), buf(12, D, dtype=F32)),
        in_specs=[any_spec] * 5,
        out_specs=(vmem_spec, vmem_spec, vmem_spec),
        scratch_shapes=[
            buf(16, 16, D), buf(16, 16, D), pltpu.SMEM((2, 2), jnp.int32),
            buf(D, 3 * D), buf(D, D),
            buf(2, 64, D), buf(2, 64, D), buf(64, D), buf(64, D),
            *column, *column, buf(128, D, dtype=F32),
            buf(3, NX, 8, 16, D), buf(3, NX, 4, 16, D),
            buf(NX, 4, 16, D), buf(NX, 4, 16, D), buf(NX, 4, 16, D),
            buf(NX, 16, D), buf(NX, 16, D),
            buf(NX - 1, 4, 16, D), buf(NY - 1, NX, 16, D), buf(NZ - 1, NX, 16, D),
            buf(4, 16, D), buf(NX, 16, D), buf(NX, 16, D),
            buf(NZ - 1, 16, D), buf(NX - 1, 16, D), buf(NX - 1, 16, D),
            buf(NY, 16, D), buf(16, D), buf(NZ - 1, 16, D), buf(NY, 16, D),
            buf(16, D), buf(16, D), buf(16, D),
            sem(5), sem(2), sem(2), sem(2),
            sem(3), sem(3), sem(NX - 1), sem(NX - 1),
            sem(NY - 1), sem(NY - 1), sem(NZ - 1), sem(NZ - 1),
            sem(NZ - 1), sem(NZ - 1), sem(NX - 1), sem(NX - 1), sem(NX - 1), sem(NX - 1),
            sem(NY - 1), sem(NY), sem(NZ - 1), sem(NZ - 1), sem(NY - 1), sem(NY),
            sem(NY - 1), pltpu.SemaphoreType.DMA, sem(3), sem(3),
        ],
        compiler_params=pltpu.CompilerParams(
            collective_id=0, has_side_effects=True, vmem_limit_bytes=56 * 1024 * 1024
        ),
        cost_estimate=pl.CostEstimate(
            flops=900_000_000, bytes_accessed=2_000_000, transcendentals=200_000
        ),
        name="window_grads",
    )(tokens, grad_out, ocean_mask, w_qkv, w_out)
    return pl.pallas_call(
        hand_over,
        out_shape=[jax.ShapeDtypeStruct(r.shape, r.dtype) for r in results],
        in_specs=[any_spec] * 3,
        out_specs=[any_spec] * 3,
        scratch_shapes=[sem(3)],
        compiler_params=pltpu.CompilerParams(vmem_limit_bytes=4 * 1024 * 1024),
        cost_estimate=pl.CostEstimate(flops=0, bytes_accessed=600_000, transcendentals=0),
        name="hand_over",
    )(*results)


def solution(mesh):
    return jax.shard_map(
        body,
        mesh=mesh,
        in_specs=(
            P("region", "tile", None),
            P("region", "tile", None),
            P("region", "tile"),
            P(),
            P(),
        ),
        out_specs=(P("region", "tile", None), P("tile", None), P("tile", None)),
        check_vma=False,
    )
```

```python
import math

import jax
import jax.numpy as jnp
from jax import lax
from jax.experimental import pallas as pl
from jax.experimental.pallas import tpu as pltpu
from jax.sharding import PartitionSpec as P

MESH = pl.DeviceIdType.MESH
F32 = jnp.float32
BF16 = jnp.bfloat16
D = 384
HD = 32
LOG2E = math.log2(math.e)
GROUPS = 3
NX, NZ, NY = 4, 8, 8
PY, PX, PZ = 0, 1, 2
FAR_FIRST = (4, 3, 5, 2, 6, 1, 7)
NT = (((1,), (1,)), ((), ()))


def dot(a, b, dims=(((1,), (0,)), ((), ()))):
    return lax.dot_general(a, b, dims, preferred_element_type=F32)


def roll4(a):
    n, _, width = a.shape
    return pltpu.roll(a.reshape(n * 8, width).reshape(n, 8, width), 4, 1)


def low4(shape):
    return lax.broadcasted_iota(jnp.int32, shape, len(shape) - 2) % 8 < 4


def part(array, a, first):
    return array[64 * a:64 * a + 64, first:first + 128]


def spread(array, a):
    lane_head = lax.broadcasted_iota(jnp.int32, (1, 128), 1) // HD
    order = (1, 0, 3, 2) if a else (0, 1, 2, 3)
    return jnp.concatenate(
        [array * (lane_head == h).astype(F32).astype(BF16) for h in order], axis=0
    )


def own(zero, one):
    first_half = lax.broadcasted_iota(jnp.int32, (1, 128), 1) < 64
    blocks = []
    for h in range(4):
        r, c = slice(32 * h, 32 * h + 32), slice(128 * (h // 2), 128 * (h // 2) + 128)
        if h % 2 == 0:
            blocks.append(jnp.where(first_half, zero[r, c], one[r, c]))
        else:
            blocks.append(pltpu.roll(jnp.where(first_half, one[r, c], zero[r, c]), 64, 1))
    return jnp.concatenate(blocks, axis=0).astype(BF16)


UNITS = [(a, g) for g in range(GROUPS) for a in range(2)]
ROOT = HD ** -0.5


def normalise(feats, normed_t, xhat, istd):
    center = jnp.mean(feats, axis=-1, keepdims=True)
    dev = feats - center
    inv = lax.rsqrt(jnp.mean(dev * dev, axis=-1, keepdims=True) + 1e-05)
    hat = dev * inv
    xhat[...] = hat
    istd[...] = jnp.broadcast_to(inv, (128, 128))
    nb = hat.astype(BF16)
    normed_t[...] = nb.T
    return nb


def scores(proj, ga):
    q = [spread(part(proj, a, 128 * g), a) for a, g in UNITS]
    o = [spread(part(ga, a, 128 * g), a) for a, g in UNITS]
    k = [part(proj, a, D + 128 * g) for a, g in UNITS]
    v = [part(proj, a, 2 * D + 128 * g) for a, g in UNITS]
    s = [dot(m, n, NT) for m, n in zip(k, q)]
    dp = [dot(m, n, NT) for m, n in zip(v, o)]
    return q, o, [m.T for m in k], [m.T for m in v], s, dp


def softmax_grads(s, dp):
    pb, ds = [], []
    for t, d in zip(s, dp):
        e = jnp.exp2((t - jnp.max(t, axis=0, keepdims=True)) * (ROOT * LOG2E))
        p = e * (1.0 / jnp.sum(e, axis=0, keepdims=True))
        row = jnp.sum(d * p, axis=0, keepdims=True)
        pb.append(p.astype(BF16))
        ds.append((p * ((d - row) * ROOT)).astype(BF16))
    return pb, ds


def products(q, o, kt, vt, pb, ds):
    qt = [dot(m, n) for m, n in zip(kt, ds)]
    dk = [dot(m, n) for m, n in zip(ds, q)]
    dv = [dot(m, n) for m, n in zip(pb, o)]
    ot = [dot(m, n) for m, n in zip(vt, pb)]
    return qt, dk, dv, ot


def keep_products(qt, dk, dv, ot, att_t, query_t, gp):
    for i, (a, g) in enumerate(UNITS):
        at_row = pl.ds(64 * a, 64)
        gp[at_row, 128 * g:128 * g + 128] = dk[i].astype(BF16)
        gp[at_row, D + 128 * g:D + 128 * g + 128] = dv[i].astype(BF16)
    for g in range(GROUPS):
        query_t[128 * g:128 * g + 128, :] = own(qt[2 * g], qt[2 * g + 1])
        att_t[128 * g:128 * g + 128, :] = own(ot[2 * g], ot[2 * g + 1])


def device():
    region, tile = lax.axis_index("region"), lax.axis_index("tile")
    tiles = NX * NZ
    west = {"region": region, "tile": (tile + tiles - 1) % tiles}
    east = {"region": region, "tile": (tile + 1) % tiles}
    return region, tile, west, east


def send(src, dst, ss, rs, dev):
    return pltpu.make_async_remote_copy(
        src_ref=src, dst_ref=dst, send_sem=ss, recv_sem=rs, device_id=dev, device_id_type=MESH,
    )


def greet(partners):
    barrier = pltpu.get_barrier_semaphore()
    for dev in partners:
        pl.semaphore_signal(barrier, inc=1, device_id=dev, device_id_type=MESH)
    return lambda: pl.semaphore_wait(barrier, len(partners))


def pairs(v):
    v = v.reshape(8, 2, 8, D)
    return v[:, 0], v[:, 1]


def kernel(
    x_hbm, dy_hbm, mask_hbm, wq_hbm, wo_hbm,
    out_ref, gq_ref, go_ref,
    xv, dyv, mask_ref, wq, wo,
    rim_out, rim_in, back_out, back_in,
    normed_t0, att_t0, query_t0, gp0, xhat0, istd0, masked0,
    normed_t1, att_t1, query_t1, gp1, xhat1, istd1, masked1, branch,
    grads, r0, hx, hy, hz, r1x, r1y, r1z, jx, jy, jz,
    r2x, r2y, r2z, r3x, ky, r3y, r3z, fx, fy, fz,
    in_sem, two_away, four_away, rim_send, rim_recv, back_sem,
    s0, q0, s1x, q1x, s1y, q1y, s1z, q1z, s2x, q2x, s2y, q2y, s2z, q2z,
    s3x, q3x, s3y, q3y, s3z, q3z, s4y, q4y, s5, q5,
):
    loads = [
        pltpu.make_async_copy(src, dst, in_sem.at[i])
        for i, (src, dst) in enumerate(
            ((x_hbm, xv), (dy_hbm, dyv), (wq_hbm, wq), (wo_hbm, wo), (mask_hbm, mask_ref))
        )
    ]
    for c in loads[:2]:
        c.start()
    region, tile, west, east = device()
    y, core = region // 2, region % 2
    x, z = tile // NZ, tile % NZ
    tiles = NX * NZ

    def at(ax, ay, az, ac):
        return {"region": ay * 2 + ac, "tile": ax * NZ + az}

    other = at(x, y, z, 1 - core)
    by_x = [at((x + k) % NX, y, z, core) for k in range(1, NX)]
    by_z = [at(x, y, (z + k) % NZ, core) for k in range(1, NZ)]
    by_y = [at(x, (y + k) % NY, z, core) for k in range(1, NY)]
    near = [by_x[0], by_x[2], by_y[0], by_y[6], by_z[0], by_z[6]]
    greeted = greet([west, east, other] + near)
    for c in loads[2:]:
        c.start()
    sub = low4((1, 8, D))

    def halves(ref):
        v = ref[...].astype(F32)
        return v[:, :8, :], v[:, 8:, :]

    def rim_of(lo):
        even, odd = pairs(lo)
        return jnp.where(sub, even, roll4(odd)).reshape(64, D).astype(BF16)

    rims = [
        send(rim_out.at[i], rim_in.at[i], rim_send.at[i], rim_recv.at[i], west) for i in range(2)
    ]
    loads[0].wait()
    x_lo, x_hi = halves(xv)
    rim_out[0] = rim_of(x_lo)
    greeted()
    rims[0].start()
    for dev in near:
        pl.semaphore_signal(two_away, inc=1, device_id=dev, device_id_type=MESH)
    loads[1].wait()
    dy_lo, dy_hi = halves(dyv)
    rim_out[1] = rim_of(dy_lo)
    rims[1].start()

    for c in loads[2:]:
        c.wait()
    flag = [[mask_ref[a, b].astype(F32) for a in range(2)] for b in range(2)]

    def mask_of(dys, b):
        return jnp.concatenate([dys[:64] * flag[b][0], dys[64:] * flag[b][1]], axis=0).astype(BF16)

    nb = normalise(jnp.where(sub, x_hi, x_lo).reshape(128, D), normed_t0, xhat0, istd0)
    mk = mask_of(jnp.where(sub, dy_hi, dy_lo).reshape(128, D), 0)
    masked0[...] = mk
    ga = dot(mk, wo[...], NT).astype(BF16)
    proj = dot(nb, wq[...]).astype(BF16)
    q, o, kt, vt, sc, dp = scores(proj, ga)
    pl.semaphore_wait(two_away, len(near))
    far = [by_y[1], by_y[5], by_z[1], by_z[5]]
    for dev in far:
        pl.semaphore_signal(four_away, inc=1, device_id=dev, device_id_type=MESH)

    def joined(hi, far):
        even, odd = pairs(hi)
        loc = jnp.where(sub, roll4(even), odd).reshape(64, D)
        far = far.astype(F32)
        return jnp.concatenate([loc[:32], far[:32], loc[32:], far[32:]], axis=0)

    rims[0].wait()
    nb = normalise(joined(x_hi, rim_in[0]), normed_t1, xhat1, istd1)
    pb, ds = softmax_grads(sc, dp)
    proj = dot(nb, wq[...]).astype(BF16)
    first = products(q, o, kt, vt, pb, ds)
    rims[1].wait()
    mk = mask_of(joined(dy_hi, rim_in[1]), 1)
    masked1[...] = mk
    ga = dot(mk, wo[...], NT).astype(BF16)
    q, o, kt, vt, sc, dp = scores(proj, ga)
    keep_products(*first, att_t0, query_t0, gp0)
    pb, ds = softmax_grads(sc, dp)
    keep_products(*products(q, o, kt, vt, pb, ds), att_t1, query_t1, gp1)

    def both(a, b, axis):
        return jnp.concatenate([a, b], axis=axis)

    nt = both(normed_t0[...], normed_t1[...], 1)
    ga_full = dot(
        both(att_t0[...], att_t1[...], 1), both(masked0[...], masked1[...], 0)
    ).reshape(16, 3, 8, D)
    w0, w1, w2 = ga_full[:, 0], ga_full[:, 1], ga_full[:, 2]
    spare = [
        roll4(jnp.where(sub, w0, w1)),
        jnp.where(sub, w2, w0),
        roll4(jnp.where(sub, w1, w2)),
    ]
    sends = []

    def start(c):
        c.start()
        sends.append(c)
        return c

    keep = {PX: core, PY: 1 - core, PZ: 1 - core}
    core0 = []
    for g in range(GROUPS):
        at_g = slice(128 * g, 128 * g + 128)
        at_gv = slice(D + 128 * g, D + 128 * g + 128)
        gn = jnp.concatenate([
            dot(nt, both(query_t0[at_g, :], query_t1[at_g, :], 1), NT),
            dot(nt, both(gp0[:, at_g], gp1[:, at_g], 0)),
            dot(nt, both(gp0[:, at_gv], gp1[:, at_gv], 0)),
        ], axis=1).reshape(16, 3, 8, D)
        v0, v1, v2 = gn[:, 0], gn[:, 1], gn[:, 2]
        packed = jnp.stack(
            [v0, jnp.where(sub, v1, spare[g]), v2, jnp.where(sub, spare[g], v1)], axis=1
        ).reshape(NX, NZ, 16, D).astype(BF16)
        grads[g] = packed
        core0.append(start(send(
            grads.at[g, :, pl.ds((1 - keep[g]) * 4, 4)], r0.at[g], s0.at[g], q0.at[g], other,
        )))

    def start_if(copies):
        for c, yes in copies:
            pl.when(yes)(c.start)

    def combined(part):
        core0[part].wait_recv()
        mine = grads[part, :, pl.ds(keep[part] * 4, 4)].astype(F32)
        return (mine + r0[part].astype(F32)).astype(BF16)

    def around(buf, slots, ss, qs, devs, place, half):
        out = []
        for k in FAR_FIRST:
            to = (place + k) % 8
            c = send(buf.at[:, to % 4], slots.at[k - 1], ss.at[k - 1], qs.at[k - 1], devs[k - 1])
            out.append((c, to // 4 == half))
        return out

    p1y = around(hy, r1y, s1y, q1y, by_y, y, keep[PY])
    p1z = around(hz, r1z, s1z, q1z, by_z, z, keep[PZ])
    hy[...] = combined(PY)
    pl.semaphore_wait(four_away, len(far))
    start_if(p1y)
    hx[...] = combined(PX)
    p1x = [
        start(send(hx.at[(x + k) % NX], r1x.at[k - 1], s1x.at[k - 1], q1x.at[k - 1], by_x[k - 1]))
        for k in (2, 1, 3)
    ]
    hz[...] = combined(PZ)
    start_if(p1z)

    gn = dot(both(query_t0[...].T, query_t1[...].T, 0), wq[:, 0:D], NT)
    gn = gn + dot(both(gp0[...], gp1[...], 0), wq[:, D:3 * D], NT)
    hat = both(xhat0[...], xhat1[...], 0)
    inv = both(istd0[:, 0:1], istd1[:, 0:1], 0)
    m0 = jnp.mean(gn, axis=-1, keepdims=True)
    m1 = jnp.mean(gn * hat, axis=-1, keepdims=True)
    br = (inv * (gn - m0 - hat * m1)).astype(BF16)
    branch[...] = br[0:128].astype(F32)
    back_out[0:32, :] = br[160:192]
    back_out[32:64, :] = br[224:256]
    loc = jnp.concatenate([br[128:160], br[192:224]], axis=0).astype(F32).reshape(8, 8, D)

    has_x = z // 4 == core
    has_z = z // 4 != core
    mid_y = y // 4 != core

    def total(first, buf, slots):
        t = first.astype(F32)
        for i in slots:
            t = t + buf[i].astype(F32)
        return t.astype(BF16)

    def over_x(buf, slots, ss, qs):
        return [
            send(buf.at[(x + k) % NX], slots.at[k - 1], ss.at[k - 1], qs.at[k - 1], by_x[k - 1])
            for k in (2, 1, 3)
        ]

    def over_z(buf, slots, ss, qs):
        out = []
        for k in FAR_FIRST:
            to = (z + k) % NZ
            c = send(buf.at[to % 4], slots.at[k - 1], ss.at[k - 1], qs.at[k - 1], by_z[k - 1])
            out.append((c, to // 4 == core))
        return out

    p2y = over_x(jy, r2y, s2y, q2y)
    p2x = over_z(jx, r2x, s2x, q2x)
    p2z = over_x(jz, r2z, s2z, q2z)
    @pl.when(mid_y)
    def _():
        for c, _ in p1y:
            c.wait_recv()
        jy[...] = total(hy[:, y % 4], r1y, range(NY - 1))
        for c in p2y:
            c.start()

    for c in p1x:
        c.wait_recv()
    jx[...] = total(hx[x], r1x, range(NX - 1))
    start_if(p2x)

    @pl.when(has_z)
    def _():
        for c, _ in p1z:
            c.wait_recv()
        jz[...] = total(hz[:, z % 4], r1z, range(NZ - 1))
        for c in p2z:
            c.start()

    back = start(send(back_out, back_in, back_sem.at[0], back_sem.at[1], east))

    def y_copies(buf, ss, qs):
        return [
            send(buf.at[y], buf.at[y], ss.at[k - 1], qs.at[y], by_y[k - 1])
            for k in FAR_FIRST
        ]

    def y_arrivals(buf, ss, qs):
        return [
            send(buf.at[y], buf.at[(y + k) % NY], ss.at[k - 1], qs.at[(y + k) % NY], by_y[k - 1])
            for k in range(1, NY)
        ]

    own_y = jnp.logical_and(has_z, y == z)
    p3y = [
        (send(ky, r3y.at[k - 1], s3y.at[k - 1], q3y.at[k - 1], by_z[k - 1]), (z + k) % NZ == y)
        for k in range(1, NZ)
    ]
    bands = 2 * NY
    p4y = [
        send(fy, fy, s4y.at[k - 1], q4y, {"region": (region + k) % bands, "tile": tile})
        for k in (8, 7, 9, 6, 10, 5, 11, 4, 12, 3, 13, 2, 14, 1, 15)
    ]

    @pl.when(mid_y)
    def _():
        for c in p2y:
            c.wait_recv()
        ky[...] = total(jy[x], r2y, range(NX - 1))
        start_if(p3y)

    @pl.when(has_x)
    def _():
        for c, _ in p2x:
            c.wait_recv()
        r3x[y] = total(jx[z % 4], r2x, range(NZ - 1))
        for c in y_copies(r3x, s3x, q3x):
            c.start()

    @pl.when(has_z)
    def _():
        for c in p2z:
            c.wait_recv()
        r3z[y] = total(jz[x], r2z, range(NX - 1))
        for c in y_copies(r3z, s3z, q3z):
            c.start()

    @pl.when(own_y)
    def _():
        for c, _ in p3y:
            c.wait_recv()
        fy[...] = total(ky[...], r3y, range(NZ - 1))
        for c in p4y:
            c.start()

    back.wait_recv()
    far = back_in[...].astype(F32).reshape(8, 8, D)
    br0 = branch[...].reshape(16, 8, D)

    def unpaired(even, odd):
        return jnp.stack([even, odd], axis=1).reshape(16, 8, D)

    new_lo = dyv[:, :8, :].astype(F32) + jnp.where(sub, unpaired(far, roll4(far)), br0)
    new_hi = dyv[:, 8:, :].astype(F32) + jnp.where(sub, br0, unpaired(roll4(loc), loc))
    out_ref[...] = jnp.concatenate([new_lo, new_hi], axis=1).astype(BF16)

    last_x = send(fx, fx, s5.at[0], q5.at[0], other)
    last_z = send(fz, fz, s5.at[1], q5.at[1], other)

    def settle(buf, out, ss, qs, last):
        for c in y_arrivals(buf, ss, qs):
            c.wait_recv()
        out[...] = total(buf[0], buf, range(1, NY))
        last.start()

    @pl.when(has_x)
    def _():
        settle(r3x, fx, s3x, q3x, last_x)

    @pl.when(has_z)
    def _():
        settle(r3z, fz, s3z, q3z, last_z)

    @pl.when(jnp.logical_not(has_x))
    def _():
        last_x.wait_recv()

    @pl.when(jnp.logical_not(has_z))
    def _():
        last_z.wait_recv()

    pl.when(jnp.logical_not(own_y))(p4y[0].wait_recv)

    scale = 1.0 / math.sqrt(3 * 64 * 2 * NY * tiles)
    odd = (z % 2) == 1
    final = jnp.concatenate([fy[...], fx[...], fz[...]], axis=1).astype(F32) * scale
    for g in range(GROUPS):
        f = final[:, D * g:D * g + D]
        top, bot = f[0:8], f[8:16]
        top_r, bot_r = pltpu.roll(top, 4, 0), pltpu.roll(bot, 4, 0)
        low = low4((8, D))
        first = jnp.where(odd, jnp.where(low, bot_r, top_r), top)
        rest = jnp.where(odd, top_r, bot)
        extra = jnp.where(odd, bot, bot_r)
        for s in range(3):
            lanes = slice(s * D + 128 * g, s * D + 128 * g + 128)
            gq_ref[0:8, lanes] = first[:, 128 * s:128 * s + 128]
            gq_ref[8:12, lanes] = rest[0:4, 128 * s:128 * s + 128]
        go_ref[4 * g:4 * g + 4, :] = extra[0:4]

    def sent_if(copies):
        for c, yes in copies:
            pl.when(yes)(c.wait_send)

    for c in sends:
        c.wait_send()
    sent_if(p1y + p1z + p2x)

    @pl.when(mid_y)
    def _():
        for c in p2y:
            c.wait_send()
        sent_if(p3y)

    @pl.when(has_x)
    def _():
        for c in y_copies(r3x, s3x, q3x):
            c.wait_send()
        last_x.wait_send()

    @pl.when(has_z)
    def _():
        for c in p2z + y_copies(r3z, s3z, q3z):
            c.wait_send()
        last_z.wait_send()

    @pl.when(own_y)
    def _():
        for c in p4y:
            c.wait_send()


def hand_over(a, b, c, a_out, b_out, c_out, sems):
    copies = [
        pltpu.make_async_copy(src, dst, sems.at[i])
        for i, (src, dst) in enumerate(((a, a_out), (b, b_out), (c, c_out)))
    ]
    for c in copies:
        c.start()
    for c in copies:
        c.wait()


def body(tokens, grad_out, ocean_mask, w_qkv, w_out):
    any_spec = pl.BlockSpec(memory_space=pl.ANY)
    vmem_spec = pl.BlockSpec(memory_space=pltpu.VMEM)

    def buf(*shape, dtype=BF16):
        return pltpu.VMEM(shape, dtype)

    def sem(*shape):
        return pltpu.SemaphoreType.DMA(shape)

    column = [
        buf(D, 128), buf(D, 128), buf(D, 128), buf(128, 2 * D),
        buf(128, D, dtype=F32), buf(128, 128, dtype=F32), buf(128, D),
    ]
    results = pl.pallas_call(
        kernel,
        out_shape=(buf(16, 16, D), buf(12, 3 * D, dtype=F32), buf(12, D, dtype=F32)),
        in_specs=[any_spec] * 5,
        out_specs=(vmem_spec, vmem_spec, vmem_spec),
        scratch_shapes=[
            buf(16, 16, D), buf(16, 16, D), pltpu.SMEM((2, 2), jnp.int32),
            buf(D, 3 * D), buf(D, D),
            buf(2, 64, D), buf(2, 64, D), buf(64, D), buf(64, D),
            *column, *column, buf(128, D, dtype=F32),
            buf(3, NX, 8, 16, D), buf(3, NX, 4, 16, D),
            buf(NX, 4, 16, D), buf(NX, 4, 16, D), buf(NX, 4, 16, D),
            buf(NX - 1, 4, 16, D), buf(NY - 1, NX, 16, D), buf(NZ - 1, NX, 16, D),
            buf(4, 16, D), buf(NX, 16, D), buf(NX, 16, D),
            buf(NZ - 1, 16, D), buf(NX - 1, 16, D), buf(NX - 1, 16, D),
            buf(NY, 16, D), buf(16, D), buf(NZ - 1, 16, D), buf(NY, 16, D),
            buf(16, D), buf(16, D), buf(16, D),
            sem(5), pltpu.SemaphoreType.REGULAR, pltpu.SemaphoreType.REGULAR, sem(2), sem(2), sem(2),
            sem(3), sem(3), sem(NX - 1), sem(NX - 1),
            sem(NY - 1), sem(NY - 1), sem(NZ - 1), sem(NZ - 1),
            sem(NZ - 1), sem(NZ - 1), sem(NX - 1), sem(NX - 1), sem(NX - 1), sem(NX - 1),
            sem(NY - 1), sem(NY), sem(NZ - 1), sem(NZ - 1), sem(NY - 1), sem(NY),
            sem(2 * NY - 1), pltpu.SemaphoreType.DMA, sem(2), sem(2),
        ],
        compiler_params=pltpu.CompilerParams(
            collective_id=0, has_side_effects=True, vmem_limit_bytes=56 * 1024 * 1024
        ),
        cost_estimate=pl.CostEstimate(
            flops=900_000_000, bytes_accessed=2_000_000, transcendentals=200_000
        ),
        name="window_grads",
    )(tokens, grad_out, ocean_mask, w_qkv, w_out)
    return pl.pallas_call(
        hand_over,
        out_shape=[jax.ShapeDtypeStruct(r.shape, r.dtype) for r in results],
        in_specs=[any_spec] * 3,
        out_specs=[any_spec] * 3,
        scratch_shapes=[sem(3)],
        compiler_params=pltpu.CompilerParams(vmem_limit_bytes=4 * 1024 * 1024),
        cost_estimate=pl.CostEstimate(flops=0, bytes_accessed=600_000, transcendentals=0),
        name="hand_over",
    )(*results)


def solution(mesh):
    return jax.shard_map(
        body,
        mesh=mesh,
        in_specs=(
            P("region", "tile", None),
            P("region", "tile", None),
            P("region", "tile"),
            P(),
            P(),
        ),
        out_specs=(P("region", "tile", None), P("tile", None), P("tile", None)),
        check_vma=False,
    )
```

```python
import math

import jax
import jax.numpy as jnp
from jax import lax
from jax.experimental import pallas as pl
from jax.experimental.pallas import tpu as pltpu
from jax.sharding import PartitionSpec as P

MESH = pl.DeviceIdType.MESH
F32 = jnp.float32
BF16 = jnp.bfloat16
D = 384
HD = 32
LOG2E = math.log2(math.e)
GROUPS = 3
NX, NZ, NY = 4, 8, 8
WY, WX, WZ = 256, 512, 384
CUT = (slice(0, WY), slice(WY, WY + WX), slice(WY + WX, 3 * D))
PY, PX, PZ = 0, 1, 2
FAR_FIRST = (4, 3, 5, 2, 6, 1, 7)
NT = (((1,), (1,)), ((), ()))


def dot(a, b, dims=(((1,), (0,)), ((), ()))):
    return lax.dot_general(a, b, dims, preferred_element_type=F32)


def roll4(a):
    n, _, width = a.shape
    return pltpu.roll(a.reshape(n * 8, width).reshape(n, 8, width), 4, 1)


def low4(shape):
    return lax.broadcasted_iota(jnp.int32, shape, len(shape) - 2) % 8 < 4


def part(array, a, first):
    return array[64 * a:64 * a + 64, first:first + 128]


def spread(array, a):
    lane_head = lax.broadcasted_iota(jnp.int32, (1, 128), 1) // HD
    order = (1, 0, 3, 2) if a else (0, 1, 2, 3)
    return jnp.concatenate(
        [array * (lane_head == h).astype(F32).astype(BF16) for h in order], axis=0
    )


def own(zero, one):
    first_half = lax.broadcasted_iota(jnp.int32, (1, 128), 1) < 64
    blocks = []
    for h in range(4):
        r, c = slice(32 * h, 32 * h + 32), slice(128 * (h // 2), 128 * (h // 2) + 128)
        if h % 2 == 0:
            blocks.append(jnp.where(first_half, zero[r, c], one[r, c]))
        else:
            blocks.append(pltpu.roll(jnp.where(first_half, one[r, c], zero[r, c]), 64, 1))
    return jnp.concatenate(blocks, axis=0).astype(BF16)


UNITS = [(a, g) for g in range(GROUPS) for a in range(2)]
ROOT = HD ** -0.5


def normalise(feats, normed_t, xhat, istd):
    center = jnp.mean(feats, axis=-1, keepdims=True)
    dev = feats - center
    inv = lax.rsqrt(jnp.mean(dev * dev, axis=-1, keepdims=True) + 1e-05)
    hat = dev * inv
    xhat[...] = hat
    istd[...] = jnp.broadcast_to(inv, (128, 128))
    nb = hat.astype(BF16)
    normed_t[...] = nb.T
    return nb


def scores(proj):
    q = [spread(part(proj, a, 128 * g), a) for a, g in UNITS]
    k = [part(proj, a, D + 128 * g) for a, g in UNITS]
    s = [dot(m, n, NT) for m, n in zip(k, q)]
    return q, [m.T for m in k], s


def softmax(s):
    p = []
    for t in s:
        e = jnp.exp2((t - jnp.max(t, axis=0, keepdims=True)) * (ROOT * LOG2E))
        p.append(e * (1.0 / jnp.sum(e, axis=0, keepdims=True)))
    return p


def grad_probs(proj, ga):
    o = [spread(part(ga, a, 128 * g), a) for a, g in UNITS]
    v = [part(proj, a, 2 * D + 128 * g) for a, g in UNITS]
    dp = [dot(m, n, NT) for m, n in zip(v, o)]
    return o, [m.T for m in v], dp


def grad_scores(p, dp):
    ds = []
    for t, d in zip(p, dp):
        row = jnp.sum(d * t, axis=0, keepdims=True)
        ds.append((t * ((d - row) * ROOT)).astype(BF16))
    return [t.astype(BF16) for t in p], ds


def products(q, o, kt, vt, pb, ds):
    qt = [dot(m, n) for m, n in zip(kt, ds)]
    dk = [dot(m, n) for m, n in zip(ds, q)]
    dv = [dot(m, n) for m, n in zip(pb, o)]
    ot = [dot(m, n) for m, n in zip(vt, pb)]
    return qt, dk, dv, ot


def keep_products(qt, dk, dv, ot, att_t, query_t, gp):
    for i, (a, g) in enumerate(UNITS):
        at_row = pl.ds(64 * a, 64)
        gp[at_row, 128 * g:128 * g + 128] = dk[i].astype(BF16)
        gp[at_row, D + 128 * g:D + 128 * g + 128] = dv[i].astype(BF16)
    for g in range(GROUPS):
        query_t[128 * g:128 * g + 128, :] = own(qt[2 * g], qt[2 * g + 1])
        att_t[128 * g:128 * g + 128, :] = own(ot[2 * g], ot[2 * g + 1])


def device():
    region, tile = lax.axis_index("region"), lax.axis_index("tile")
    tiles = NX * NZ
    west = {"region": region, "tile": (tile + tiles - 1) % tiles}
    east = {"region": region, "tile": (tile + 1) % tiles}
    return region, tile, west, east


def send(src, dst, ss, rs, dev):
    return pltpu.make_async_remote_copy(
        src_ref=src, dst_ref=dst, send_sem=ss, recv_sem=rs, device_id=dev, device_id_type=MESH,
    )


def greet(partners):
    barrier = pltpu.get_barrier_semaphore()
    for dev in partners:
        pl.semaphore_signal(barrier, inc=1, device_id=dev, device_id_type=MESH)
    return lambda: pl.semaphore_wait(barrier, len(partners))


def pairs(v):
    v = v.reshape(8, 2, 8, D)
    return v[:, 0], v[:, 1]


def kernel(
    x_hbm, dy_hbm, mask_hbm, wq_hbm, wo_hbm,
    out_ref, gq_ref, go_ref,
    xv, dyv, mask_ref, wq, wo,
    rim_out, rim_in, back_out, back_in,
    feats, normed_t, att_t, query_t, gp, xhat, istd, masked, branch, hi_out, spare,
    grads, r0, hx, hy, hz, r1x, r1y, r1z, jx, jy, jz,
    r2x, r2y, r2z, r3x, ky, r3y, r3z, fx, fy, fz,
    in_sem, two_away, four_away, rim_send, rim_recv, back_sem,
    s0, q0, s1x, q1x, s1y, q1y, s1z, q1z, s2x, q2x, s2y, q2y, s2z, q2z,
    s3x, q3x, s3y, q3y, s3z, q3z, s4y, q4y, s5, q5,
):
    loads = [
        pltpu.make_async_copy(src, dst, in_sem.at[i])
        for i, (src, dst) in enumerate(
            ((x_hbm, xv), (dy_hbm, dyv), (wq_hbm, wq), (wo_hbm, wo), (mask_hbm, mask_ref))
        )
    ]
    for c in loads[:2]:
        c.start()
    region, tile, west, east = device()
    y, core = region // 2, region % 2
    x, z = tile // NZ, tile % NZ
    tiles = NX * NZ

    def at(ax, ay, az, ac):
        return {"region": ay * 2 + ac, "tile": ax * NZ + az}

    other = at(x, y, z, 1 - core)
    by_x = [at((x + k) % NX, y, z, core) for k in range(1, NX)]
    by_z = [at(x, y, (z + k) % NZ, core) for k in range(1, NZ)]
    by_y = [at(x, (y + k) % NY, z, core) for k in range(1, NY)]
    near = [by_x[0], by_x[2], by_y[0], by_y[6], by_z[0], by_z[6]]
    greeted = greet([west, east, other] + near)
    for c in loads[2:]:
        c.start()
    sub = low4((1, 8, D))

    def halves(ref):
        v = ref[...].astype(F32)
        return v[:, :8, :], v[:, 8:, :]

    def rim_of(lo):
        even, odd = pairs(lo)
        return jnp.where(sub, even, roll4(odd)).reshape(64, D).astype(BF16)

    rims = [
        send(rim_out.at[i], rim_in.at[i], rim_send.at[i], rim_recv.at[i], west) for i in range(2)
    ]
    loads[0].wait()
    x_lo, x_hi = halves(xv)
    rim_out[0] = rim_of(x_lo)
    greeted()
    rims[0].start()
    for dev in near:
        pl.semaphore_signal(two_away, inc=1, device_id=dev, device_id_type=MESH)
    loads[1].wait()
    dy_lo, dy_hi = halves(dyv)
    rim_out[1] = rim_of(dy_lo)
    rims[1].start()

    for c in loads[2:]:
        c.wait()

    def mask_of(dys, b):
        flag = [mask_ref[a, b].astype(F32) for a in range(2)]
        return jnp.concatenate([dys[:64] * flag[0], dys[64:] * flag[1]], axis=0).astype(BF16)

    def joined(hi, far):
        even, odd = pairs(hi.astype(F32))
        loc = jnp.where(sub, roll4(even), odd).reshape(64, D)
        far = far.astype(F32)
        return jnp.concatenate([loc[:32], far[:32], loc[32:], far[32:]], axis=0)

    feats[0] = jnp.where(sub, x_hi, x_lo).reshape(128, D)
    masked[0] = mask_of(jnp.where(sub, dy_hi, dy_lo).reshape(128, D), 0)
    far = [by_y[1], by_y[5], by_z[1], by_z[5]]

    def column(b, _):
        @pl.when(b == 1)
        def _():
            pl.semaphore_wait(two_away, len(near))
            for dev in far:
                pl.semaphore_signal(four_away, inc=1, device_id=dev, device_id_type=MESH)
            rims[0].wait()
            feats[1] = joined(xv[:, 8:, :], rim_in[0])

        nb = normalise(feats[b], normed_t.at[b], xhat.at[b], istd.at[b])
        proj = dot(nb, wq[...]).astype(BF16)
        q, kt, sc = scores(proj)
        p = softmax(sc)

        @pl.when(b == 1)
        def _():
            rims[1].wait()
            masked[1] = mask_of(joined(dyv[:, 8:, :], rim_in[1]), 1)

        ga = dot(masked[b], wo[...], NT).astype(BF16)
        o, vt, dp = grad_probs(proj, ga)
        pb, ds = grad_scores(p, dp)
        keep_products(
            *products(q, o, kt, vt, pb, ds), att_t.at[b], query_t.at[b], gp.at[b]
        )
        return 0

    lax.fori_loop(0, 2, column, 0)

    def both(a, b, axis):
        return jnp.concatenate([a, b], axis=axis)

    nt = both(normed_t[0], normed_t[1], 1)
    ga_full = dot(both(att_t[0], att_t[1], 1), both(masked[0], masked[1], 0)).reshape(16, 3, 8, D)
    w0, w1, w2 = ga_full[:, 0], ga_full[:, 1], ga_full[:, 2]
    spare[0] = roll4(jnp.where(sub, w0, w1))
    spare[1] = jnp.where(sub, w2, w0)
    spare[2] = roll4(jnp.where(sub, w1, w2))
    sends = []

    def start(c):
        c.start()
        sends.append(c)
        return c

    keep = {PX: core, PY: 1 - core, PZ: 1 - core}
    pl.semaphore_wait(four_away, len(far))

    def swap(i):
        cut = CUT[i]
        return start(send(
            grads.at[:, pl.ds((1 - keep[i]) * 4, 4), :, cut], r0.at[:, :, :, cut],
            s0.at[i], q0.at[i], other,
        ))

    core0 = []
    for g in range(GROUPS):
        at_g = slice(128 * g, 128 * g + 128)
        at_gv = slice(D + 128 * g, D + 128 * g + 128)
        gn = jnp.concatenate([
            dot(nt, both(query_t[0, at_g, :], query_t[1, at_g, :], 1), NT),
            dot(nt, both(gp[0, :, at_g], gp[1, :, at_g], 0)),
            dot(nt, both(gp[0, :, at_gv], gp[1, :, at_gv], 0)),
        ], axis=1).reshape(16, 3, 8, D)
        v0, v1, v2, extra = gn[:, 0], gn[:, 1], gn[:, 2], spare[g]
        packed = jnp.stack(
            [v0, jnp.where(sub, v1, extra), v2, jnp.where(sub, extra, v1)], axis=1
        ).reshape(NX, NZ, 16, D).astype(BF16)
        grads[:, :, :, D * g:D * g + D] = packed
        core0.append(swap(g))

    def start_if(copies):
        for c, yes in copies:
            pl.when(yes)(c.start)

    def combined(i):
        core0[i].wait_recv()
        mine = grads[:, pl.ds(keep[i] * 4, 4), :, CUT[i]].astype(F32)
        return (mine + r0[:, :, :, CUT[i]].astype(F32)).astype(BF16)

    def around(buf, slots, ss, qs, devs, place, half):
        out = []
        for k in FAR_FIRST:
            to = (place + k) % 8
            c = send(buf.at[:, to % 4], slots.at[k - 1], ss.at[k - 1], qs.at[k - 1], devs[k - 1])
            out.append((c, to // 4 == half))
        return out

    p1y = around(hy, r1y, s1y, q1y, by_y, y, keep[PY])
    p1z = around(hz, r1z, s1z, q1z, by_z, z, keep[PZ])
    hy[...] = combined(PY)
    start_if(p1y)
    hx[...] = combined(PX)
    p1x = [
        start(send(hx.at[(x + k) % NX], r1x.at[k - 1], s1x.at[k - 1], q1x.at[k - 1], by_x[k - 1]))
        for k in (2, 1, 3)
    ]
    hz[...] = combined(PZ)
    start_if(p1z)

    def branch_of(b, _):
        gn = dot(query_t[b].T, wq[:, 0:D], NT) + dot(gp[b], wq[:, D:3 * D], NT)
        hat = xhat[b]
        m0 = jnp.mean(gn, axis=-1, keepdims=True)
        m1 = jnp.mean(gn * hat, axis=-1, keepdims=True)
        branch[b] = (istd[b][:, 0:1] * (gn - m0 - hat * m1)).astype(BF16)
        return 0

    lax.fori_loop(0, 2, branch_of, 0)
    back_out[0:32, :] = branch[1, 32:64, :]
    back_out[32:64, :] = branch[1, 96:128, :]
    loc = both(branch[1, 0:32, :], branch[1, 64:96, :], 0).astype(F32).reshape(8, 8, D)

    def unpaired(even, odd):
        return jnp.stack([even, odd], axis=1).reshape(16, 8, D)

    br0 = branch[0].astype(F32).reshape(16, 8, D)
    hi_out[...] = dyv[:, 8:, :].astype(F32) + jnp.where(sub, br0, unpaired(roll4(loc), loc))

    has_x = z // 4 == core
    has_z = z // 4 != core
    mid_y = y // 4 != core

    def total(first, buf, slots):
        t = first.astype(F32)
        for i in slots:
            t = t + buf[i].astype(F32)
        return t.astype(BF16)

    def over_x(buf, slots, ss, qs):
        return [
            send(buf.at[(x + k) % NX], slots.at[k - 1], ss.at[k - 1], qs.at[k - 1], by_x[k - 1])
            for k in (2, 1, 3)
        ]

    def over_z(buf, slots, ss, qs):
        out = []
        for k in FAR_FIRST:
            to = (z + k) % NZ
            c = send(buf.at[to % 4], slots.at[k - 1], ss.at[k - 1], qs.at[k - 1], by_z[k - 1])
            out.append((c, to // 4 == core))
        return out

    p2y = over_x(jy, r2y, s2y, q2y)
    p2x = over_z(jx, r2x, s2x, q2x)
    p2z = over_x(jz, r2z, s2z, q2z)
    for c in p1x:
        c.wait_recv()
    jx[...] = total(hx[x], r1x, range(NX - 1))
    start_if(p2x)

    @pl.when(has_z)
    def _():
        for c, _ in p1z:
            c.wait_recv()
        jz[...] = total(hz[:, z % 4], r1z, range(NZ - 1))
        for c in p2z:
            c.start()

    @pl.when(mid_y)
    def _():
        for c, _ in p1y:
            c.wait_recv()
        jy[...] = total(hy[:, y % 4], r1y, range(NY - 1))
        for c in p2y:
            c.start()

    back = start(send(back_out, back_in, back_sem.at[0], back_sem.at[1], east))

    def y_copies(buf, ss, qs):
        return [
            send(buf.at[y], buf.at[y], ss.at[k - 1], qs.at[y], by_y[k - 1])
            for k in FAR_FIRST
        ]

    def y_arrivals(buf, ss, qs):
        return [
            send(buf.at[y], buf.at[(y + k) % NY], ss.at[k - 1], qs.at[(y + k) % NY], by_y[k - 1])
            for k in range(1, NY)
        ]

    own_y = jnp.logical_and(has_z, y == z)
    p3y = [
        (send(ky, r3y.at[k - 1], s3y.at[k - 1], q3y.at[k - 1], by_z[k - 1]), (z + k) % NZ == y)
        for k in range(1, NZ)
    ]
    bands = 2 * NY
    p4y = [
        send(fy, fy, s4y.at[k - 1], q4y, {"region": (region + k) % bands, "tile": tile})
        for k in (8, 7, 9, 6, 10, 5, 11, 4, 12, 3, 13, 2, 14, 1, 15)
    ]

    @pl.when(has_x)
    def _():
        for c, _ in p2x:
            c.wait_recv()
        r3x[y] = total(jx[z % 4], r2x, range(NZ - 1))
        for c in y_copies(r3x, s3x, q3x):
            c.start()

    @pl.when(has_z)
    def _():
        for c in p2z:
            c.wait_recv()
        r3z[y] = total(jz[x], r2z, range(NX - 1))
        for c in y_copies(r3z, s3z, q3z):
            c.start()

    @pl.when(mid_y)
    def _():
        for c in p2y:
            c.wait_recv()
        ky[...] = total(jy[x], r2y, range(NX - 1))
        start_if(p3y)

    @pl.when(own_y)
    def _():
        for c, _ in p3y:
            c.wait_recv()
        fy[...] = total(ky[...], r3y, range(NZ - 1))
        for c in p4y:
            c.start()

    def sent_if(copies):
        for c, yes in copies:
            pl.when(yes)(c.wait_send)

    for c in sends:
        c.wait_send()
    sent_if(p1y + p1z + p2x)

    @pl.when(mid_y)
    def _():
        for c in p2y:
            c.wait_send()
        sent_if(p3y)

    @pl.when(has_z)
    def _():
        for c in p2z:
            c.wait_send()

    back.wait_recv()
    far = back_in[...].astype(F32).reshape(8, 8, D)
    br0 = branch[0].astype(F32).reshape(16, 8, D)
    new_lo = dyv[:, :8, :].astype(F32) + jnp.where(sub, unpaired(far, roll4(far)), br0)
    out_ref[...] = jnp.concatenate([new_lo, hi_out[...]], axis=1).astype(BF16)

    @pl.when(has_x)
    def _():
        for c in y_copies(r3x, s3x, q3x):
            c.wait_send()

    @pl.when(has_z)
    def _():
        for c in y_copies(r3z, s3z, q3z):
            c.wait_send()

    last_x = send(fx, fx, s5.at[0], q5.at[0], other)
    last_z = send(fz, fz, s5.at[1], q5.at[1], other)

    def settle(buf, out, ss, qs, last):
        for c in y_arrivals(buf, ss, qs):
            c.wait_recv()
        out[...] = total(buf[0], buf, range(1, NY))
        last.start()

    @pl.when(has_x)
    def _():
        settle(r3x, fx, s3x, q3x, last_x)

    @pl.when(has_z)
    def _():
        settle(r3z, fz, s3z, q3z, last_z)

    @pl.when(jnp.logical_not(has_x))
    def _():
        last_x.wait_recv()

    @pl.when(jnp.logical_not(has_z))
    def _():
        last_z.wait_recv()

    pl.when(jnp.logical_not(own_y))(p4y[0].wait_recv)

    scale = 1.0 / math.sqrt(3 * 64 * 2 * NY * tiles)
    odd = (z % 2) == 1
    final = jnp.concatenate([fy[...], fx[...], fz[...]], axis=1).astype(F32) * scale
    for g in range(GROUPS):
        f = final[:, D * g:D * g + D]
        top, bot = f[0:8], f[8:16]
        top_r, bot_r = pltpu.roll(top, 4, 0), pltpu.roll(bot, 4, 0)
        low = low4((8, D))
        first = jnp.where(odd, jnp.where(low, bot_r, top_r), top)
        rest = jnp.where(odd, top_r, bot)
        extra = jnp.where(odd, bot, bot_r)
        for s in range(3):
            lanes = slice(s * D + 128 * g, s * D + 128 * g + 128)
            gq_ref[0:8, lanes] = first[:, 128 * s:128 * s + 128]
            gq_ref[8:12, lanes] = rest[0:4, 128 * s:128 * s + 128]
        go_ref[4 * g:4 * g + 4, :] = extra[0:4]

    @pl.when(own_y)
    def _():
        for c in p4y:
            c.wait_send()

    pl.when(has_x)(last_x.wait_send)
    pl.when(has_z)(last_z.wait_send)


def hand_over(a, b, c, a_out, b_out, c_out, sems):
    copies = [
        pltpu.make_async_copy(src, dst, sems.at[i])
        for i, (src, dst) in enumerate(((a, a_out), (b, b_out), (c, c_out)))
    ]
    for c in copies:
        c.start()
    for c in copies:
        c.wait()


def body(tokens, grad_out, ocean_mask, w_qkv, w_out):
    any_spec = pl.BlockSpec(memory_space=pl.ANY)
    vmem_spec = pl.BlockSpec(memory_space=pltpu.VMEM)

    def buf(*shape, dtype=BF16):
        return pltpu.VMEM(shape, dtype)

    def sem(*shape):
        return pltpu.SemaphoreType.DMA(shape)

    results = pl.pallas_call(
        kernel,
        out_shape=(buf(16, 16, D), buf(12, 3 * D, dtype=F32), buf(12, D, dtype=F32)),
        in_specs=[any_spec] * 5,
        out_specs=(vmem_spec, vmem_spec, vmem_spec),
        scratch_shapes=[
            buf(16, 16, D), buf(16, 16, D), pltpu.SMEM((2, 2), jnp.int32),
            buf(D, 3 * D), buf(D, D),
            buf(2, 64, D), buf(2, 64, D), buf(64, D), buf(64, D),
            buf(2, 128, D, dtype=F32), buf(2, D, 128), buf(2, D, 128), buf(2, D, 128),
            buf(2, 128, 2 * D), buf(2, 128, D, dtype=F32), buf(2, 128, 128, dtype=F32),
            buf(2, 128, D), buf(2, 128, D), buf(16, 8, D, dtype=F32),
            buf(GROUPS, 16, 8, D, dtype=F32),
            buf(NX, 8, 16, 3 * D), buf(NX, 4, 16, 3 * D),
            buf(NX, 4, 16, WX), buf(NX, 4, 16, WY), buf(NX, 4, 16, WZ),
            buf(NX - 1, 4, 16, WX), buf(NY - 1, NX, 16, WY), buf(NZ - 1, NX, 16, WZ),
            buf(4, 16, WX), buf(NX, 16, WY), buf(NX, 16, WZ),
            buf(NZ - 1, 16, WX), buf(NX - 1, 16, WY), buf(NX - 1, 16, WZ),
            buf(NY, 16, WX), buf(16, WY), buf(NZ - 1, 16, WY), buf(NY, 16, WZ),
            buf(16, WX), buf(16, WY), buf(16, WZ),
            sem(5), pltpu.SemaphoreType.REGULAR, pltpu.SemaphoreType.REGULAR, sem(2), sem(2), sem(2),
            sem(3), sem(3), sem(NX - 1), sem(NX - 1),
            sem(NY - 1), sem(NY - 1), sem(NZ - 1), sem(NZ - 1),
            sem(NZ - 1), sem(NZ - 1), sem(NX - 1), sem(NX - 1), sem(NX - 1), sem(NX - 1),
            sem(NY - 1), sem(NY), sem(NZ - 1), sem(NZ - 1), sem(NY - 1), sem(NY),
            sem(2 * NY - 1), pltpu.SemaphoreType.DMA, sem(2), sem(2),
        ],
        compiler_params=pltpu.CompilerParams(
            collective_id=0, has_side_effects=True, vmem_limit_bytes=56 * 1024 * 1024
        ),
        cost_estimate=pl.CostEstimate(
            flops=900_000_000, bytes_accessed=2_000_000, transcendentals=200_000
        ),
        name="window_grads",
    )(tokens, grad_out, ocean_mask, w_qkv, w_out)
    return pl.pallas_call(
        hand_over,
        out_shape=[jax.ShapeDtypeStruct(r.shape, r.dtype) for r in results],
        in_specs=[any_spec] * 3,
        out_specs=[any_spec] * 3,
        scratch_shapes=[sem(3)],
        compiler_params=pltpu.CompilerParams(vmem_limit_bytes=4 * 1024 * 1024),
        cost_estimate=pl.CostEstimate(flops=0, bytes_accessed=600_000, transcendentals=0),
        name="hand_over",
    )(*results)


def solution(mesh):
    return jax.shard_map(
        body,
        mesh=mesh,
        in_specs=(
            P("region", "tile", None),
            P("region", "tile", None),
            P("region", "tile"),
            P(),
            P(),
        ),
        out_specs=(P("region", "tile", None), P("tile", None), P("tile", None)),
        check_vma=False,
    )
```

```python
import math

import jax
import jax.numpy as jnp
from jax import lax
from jax.experimental import pallas as pl
from jax.experimental.pallas import tpu as pltpu
from jax.sharding import PartitionSpec as P

MESH = pl.DeviceIdType.MESH
F32 = jnp.float32
BF16 = jnp.bfloat16
D = 384
HD = 32
LOG2E = math.log2(math.e)
GROUPS = 3
NX, NZ, NY = 4, 8, 8
WY, WX, WZ = 384, 512, 256
CUT = (slice(0, WY), slice(WY, WY + WX), slice(WY + WX, 3 * D))
PY, PX, PZ = 0, 1, 2
PIECES = ((PY, CUT[PY], 0), (PX, slice(WY, 2 * D), 1), (PX, slice(2 * D, WY + WX), 2), (PZ, CUT[PZ], 2))
FAR_FIRST = (4, 3, 5, 2, 6, 1, 7)
NT = (((1,), (1,)), ((), ()))


def dot(a, b, dims=(((1,), (0,)), ((), ()))):
    return lax.dot_general(a, b, dims, preferred_element_type=F32)


def roll4(a):
    n, _, width = a.shape
    return pltpu.roll(a.reshape(n * 8, width).reshape(n, 8, width), 4, 1)


def low4(shape):
    return lax.broadcasted_iota(jnp.int32, shape, len(shape) - 2) % 8 < 4


def part(array, a, first):
    return array[64 * a:64 * a + 64, first:first + 128]


def spread(array, a):
    lane_head = lax.broadcasted_iota(jnp.int32, (1, 128), 1) // HD
    order = (1, 0, 3, 2) if a else (0, 1, 2, 3)
    return jnp.concatenate(
        [array * (lane_head == h).astype(F32).astype(BF16) for h in order], axis=0
    )


def own(zero, one):
    first_half = lax.broadcasted_iota(jnp.int32, (1, 128), 1) < 64
    blocks = []
    for h in range(4):
        r, c = slice(32 * h, 32 * h + 32), slice(128 * (h // 2), 128 * (h // 2) + 128)
        if h % 2 == 0:
            blocks.append(jnp.where(first_half, zero[r, c], one[r, c]))
        else:
            blocks.append(pltpu.roll(jnp.where(first_half, one[r, c], zero[r, c]), 64, 1))
    return jnp.concatenate(blocks, axis=0).astype(BF16)


UNITS = [(a, g) for g in range(GROUPS) for a in range(2)]
ROOT = HD ** -0.5


def normalise(feats, normed_t, xhat, istd):
    center = jnp.mean(feats, axis=-1, keepdims=True)
    dev = feats - center
    inv = lax.rsqrt(jnp.mean(dev * dev, axis=-1, keepdims=True) + 1e-05)
    hat = dev * inv
    xhat[...] = hat
    istd[...] = jnp.broadcast_to(inv, (128, 128))
    nb = hat.astype(BF16)
    normed_t[...] = nb.T
    return nb


def scores(proj):
    q = [spread(part(proj, a, 128 * g), a) for a, g in UNITS]
    k = [part(proj, a, D + 128 * g) for a, g in UNITS]
    s = [dot(m, n, NT) for m, n in zip(k, q)]
    return q, [m.T for m in k], s


def softmax(s):
    p = []
    for t in s:
        e = jnp.exp2((t - jnp.max(t, axis=0, keepdims=True)) * (ROOT * LOG2E))
        p.append(e * (1.0 / jnp.sum(e, axis=0, keepdims=True)))
    return p


def grad_probs(proj, ga):
    o = [spread(part(ga, a, 128 * g), a) for a, g in UNITS]
    v = [part(proj, a, 2 * D + 128 * g) for a, g in UNITS]
    dp = [dot(m, n, NT) for m, n in zip(v, o)]
    return o, [m.T for m in v], dp


def grad_scores(p, dp):
    ds = []
    for t, d in zip(p, dp):
        row = jnp.sum(d * t, axis=0, keepdims=True)
        ds.append((t * ((d - row) * ROOT)).astype(BF16))
    return [t.astype(BF16) for t in p], ds


def products(q, o, kt, vt, pb, ds):
    qt = [dot(m, n) for m, n in zip(kt, ds)]
    dk = [dot(m, n) for m, n in zip(ds, q)]
    dv = [dot(m, n) for m, n in zip(pb, o)]
    ot = [dot(m, n) for m, n in zip(vt, pb)]
    return qt, dk, dv, ot


def keep_products(qt, dk, dv, ot, att_t, query_t, gp):
    for i, (a, g) in enumerate(UNITS):
        at_row = pl.ds(64 * a, 64)
        gp[at_row, 128 * g:128 * g + 128] = dk[i].astype(BF16)
        gp[at_row, D + 128 * g:D + 128 * g + 128] = dv[i].astype(BF16)
    for g in range(GROUPS):
        query_t[128 * g:128 * g + 128, :] = own(qt[2 * g], qt[2 * g + 1])
        att_t[128 * g:128 * g + 128, :] = own(ot[2 * g], ot[2 * g + 1])


def device():
    region, tile = lax.axis_index("region"), lax.axis_index("tile")
    tiles = NX * NZ
    west = {"region": region, "tile": (tile + tiles - 1) % tiles}
    east = {"region": region, "tile": (tile + 1) % tiles}
    return region, tile, west, east


def send(src, dst, ss, rs, dev):
    return pltpu.make_async_remote_copy(
        src_ref=src, dst_ref=dst, send_sem=ss, recv_sem=rs, device_id=dev, device_id_type=MESH,
    )


def greet(partners):
    barrier = pltpu.get_barrier_semaphore()
    for dev in partners:
        pl.semaphore_signal(barrier, inc=1, device_id=dev, device_id_type=MESH)
    return lambda: pl.semaphore_wait(barrier, len(partners))


def pairs(v):
    v = v.reshape(8, 2, 8, D)
    return v[:, 0], v[:, 1]


def kernel(
    x_hbm, dy_hbm, mask_hbm, wq_hbm, wo_hbm,
    out_ref, gq_ref, go_ref,
    xv, dyv, mask_ref, wq, wo,
    rim_out, rim_in, back_out, back_in,
    feats, normed_t, att_t, query_t, gp, xhat, istd, masked, branch, hi_out, spare,
    grads, r0, hx, hy, hz, r1x, r1y, r1z, jx, jy, jz,
    r2x, r2y, r2z, r3x, ky, r3y, r3z, fx, fy, fz,
    in_sem, two_away, four_away, rim_send, rim_recv, back_sem,
    s0, q0, s1x, q1x, s1y, q1y, s1z, q1z, s2x, q2x, s2y, q2y, s2z, q2z,
    s3x, q3x, s3y, q3y, s3z, q3z, s4y, q4y, s5, q5,
):
    loads = [
        pltpu.make_async_copy(src, dst, in_sem.at[i])
        for i, (src, dst) in enumerate(
            ((x_hbm, xv), (dy_hbm, dyv), (wq_hbm, wq), (wo_hbm, wo), (mask_hbm, mask_ref))
        )
    ]
    for c in loads[:2]:
        c.start()
    region, tile, west, east = device()
    y, core = region // 2, region % 2
    x, z = tile // NZ, tile % NZ
    tiles = NX * NZ

    def at(ax, ay, az, ac):
        return {"region": ay * 2 + ac, "tile": ax * NZ + az}

    other = at(x, y, z, 1 - core)
    by_x = [at((x + k) % NX, y, z, core) for k in range(1, NX)]
    by_z = [at(x, y, (z + k) % NZ, core) for k in range(1, NZ)]
    by_y = [at(x, (y + k) % NY, z, core) for k in range(1, NY)]
    near = [by_x[0], by_x[2], by_y[0], by_y[6], by_z[0], by_z[6]]
    greeted = greet([west, east, other] + near)
    for c in loads[2:]:
        c.start()
    sub = low4((1, 8, D))

    def halves(ref):
        v = ref[...].astype(F32)
        return v[:, :8, :], v[:, 8:, :]

    def rim_of(lo):
        even, odd = pairs(lo)
        return jnp.where(sub, even, roll4(odd)).reshape(64, D).astype(BF16)

    rims = [
        send(rim_out.at[i], rim_in.at[i], rim_send.at[i], rim_recv.at[i], west) for i in range(2)
    ]
    loads[0].wait()
    x_lo, x_hi = halves(xv)
    rim_out[0] = rim_of(x_lo)
    greeted()
    rims[0].start()
    for dev in near:
        pl.semaphore_signal(two_away, inc=1, device_id=dev, device_id_type=MESH)
    loads[1].wait()
    dy_lo, dy_hi = halves(dyv)
    rim_out[1] = rim_of(dy_lo)
    rims[1].start()

    for c in loads[2:]:
        c.wait()

    def mask_of(dys, b):
        flag = [mask_ref[a, b].astype(F32) for a in range(2)]
        return jnp.concatenate([dys[:64] * flag[0], dys[64:] * flag[1]], axis=0).astype(BF16)

    def joined(hi, far):
        even, odd = pairs(hi.astype(F32))
        loc = jnp.where(sub, roll4(even), odd).reshape(64, D)
        far = far.astype(F32)
        return jnp.concatenate([loc[:32], far[:32], loc[32:], far[32:]], axis=0)

    feats[0] = jnp.where(sub, x_hi, x_lo).reshape(128, D)
    masked[0] = mask_of(jnp.where(sub, dy_hi, dy_lo).reshape(128, D), 0)
    far = [by_y[1], by_y[5], by_z[1], by_z[5]]

    def column(b, _):
        @pl.when(b == 1)
        def _():
            pl.semaphore_wait(two_away, len(near))
            for dev in far:
                pl.semaphore_signal(four_away, inc=1, device_id=dev, device_id_type=MESH)
            rims[0].wait()
            feats[1] = joined(xv[:, 8:, :], rim_in[0])

        nb = normalise(feats[b], normed_t.at[b], xhat.at[b], istd.at[b])
        proj = dot(nb, wq[...]).astype(BF16)
        q, kt, sc = scores(proj)
        p = softmax(sc)

        @pl.when(b == 1)
        def _():
            rims[1].wait()
            masked[1] = mask_of(joined(dyv[:, 8:, :], rim_in[1]), 1)

        ga = dot(masked[b], wo[...], NT).astype(BF16)
        o, vt, dp = grad_probs(proj, ga)
        pb, ds = grad_scores(p, dp)
        keep_products(
            *products(q, o, kt, vt, pb, ds), att_t.at[b], query_t.at[b], gp.at[b]
        )
        return 0

    lax.fori_loop(0, 2, column, 0)

    def both(a, b, axis):
        return jnp.concatenate([a, b], axis=axis)

    nt = both(normed_t[0], normed_t[1], 1)
    ga_full = dot(both(att_t[0], att_t[1], 1), both(masked[0], masked[1], 0)).reshape(16, 3, 8, D)
    w0, w1, w2 = ga_full[:, 0], ga_full[:, 1], ga_full[:, 2]
    spare[0] = roll4(jnp.where(sub, w0, w1))
    spare[1] = jnp.where(sub, w2, w0)
    spare[2] = roll4(jnp.where(sub, w1, w2))
    sends = []

    def start(c):
        c.start()
        sends.append(c)
        return c

    keep = {PX: core, PY: 1 - core, PZ: 1 - core}
    pl.semaphore_wait(four_away, len(far))

    def swap(i):
        part, cut, _ = PIECES[i]
        return start(send(
            grads.at[:, pl.ds((1 - keep[part]) * 4, 4), :, cut], r0.at[:, :, :, cut],
            s0.at[i], q0.at[i], other,
        ))

    core0 = []
    for g in range(GROUPS):
        at_g = slice(128 * g, 128 * g + 128)
        at_gv = slice(D + 128 * g, D + 128 * g + 128)
        gn = jnp.concatenate([
            dot(nt, both(query_t[0, at_g, :], query_t[1, at_g, :], 1), NT),
            dot(nt, both(gp[0, :, at_g], gp[1, :, at_g], 0)),
            dot(nt, both(gp[0, :, at_gv], gp[1, :, at_gv], 0)),
        ], axis=1).reshape(16, 3, 8, D)
        v0, v1, v2, extra = gn[:, 0], gn[:, 1], gn[:, 2], spare[g]
        packed = jnp.stack(
            [v0, jnp.where(sub, v1, extra), v2, jnp.where(sub, extra, v1)], axis=1
        ).reshape(NX, NZ, 16, D).astype(BF16)
        grads[:, :, :, D * g:D * g + D] = packed
        core0 += [swap(i) for i, piece in enumerate(PIECES) if piece[2] == g]

    def start_if(copies):
        for c, yes in copies:
            pl.when(yes)(c.start)

    def combined(i):
        for c, piece in zip(core0, PIECES):
            if piece[0] == i:
                c.wait_recv()
        mine = grads[:, pl.ds(keep[i] * 4, 4), :, CUT[i]].astype(F32)
        return (mine + r0[:, :, :, CUT[i]].astype(F32)).astype(BF16)

    def around(buf, slots, ss, qs, devs, place, half):
        out = []
        for k in FAR_FIRST:
            to = (place + k) % 8
            c = send(buf.at[:, to % 4], slots.at[k - 1], ss.at[k - 1], qs.at[k - 1], devs[k - 1])
            out.append((c, to // 4 == half))
        return out

    p1y = around(hy, r1y, s1y, q1y, by_y, y, keep[PY])
    p1z = around(hz, r1z, s1z, q1z, by_z, z, keep[PZ])
    hy[...] = combined(PY)
    start_if(p1y)
    hx[...] = combined(PX)
    p1x = [
        start(send(hx.at[(x + k) % NX], r1x.at[k - 1], s1x.at[k - 1], q1x.at[k - 1], by_x[k - 1]))
        for k in (2, 1, 3)
    ]
    hz[...] = combined(PZ)
    start_if(p1z)

    def branch_of(b, _):
        gn = dot(query_t[b].T, wq[:, 0:D], NT) + dot(gp[b], wq[:, D:3 * D], NT)
        hat = xhat[b]
        m0 = jnp.mean(gn, axis=-1, keepdims=True)
        m1 = jnp.mean(gn * hat, axis=-1, keepdims=True)
        branch[b] = (istd[b][:, 0:1] * (gn - m0 - hat * m1)).astype(BF16)
        return 0

    lax.fori_loop(0, 2, branch_of, 0)
    back_out[0:32, :] = branch[1, 32:64, :]
    back_out[32:64, :] = branch[1, 96:128, :]
    loc = both(branch[1, 0:32, :], branch[1, 64:96, :], 0).astype(F32).reshape(8, 8, D)

    def unpaired(even, odd):
        return jnp.stack([even, odd], axis=1).reshape(16, 8, D)

    br0 = branch[0].astype(F32).reshape(16, 8, D)
    hi_out[...] = dyv[:, 8:, :].astype(F32) + jnp.where(sub, br0, unpaired(roll4(loc), loc))

    has_x = z // 4 == core
    has_z = z // 4 != core
    mid_y = y // 4 != core

    def total(first, buf, slots):
        t = first.astype(F32)
        for i in slots:
            t = t + buf[i].astype(F32)
        return t.astype(BF16)

    def over_x(buf, slots, ss, qs):
        return [
            send(buf.at[(x + k) % NX], slots.at[k - 1], ss.at[k - 1], qs.at[k - 1], by_x[k - 1])
            for k in (2, 1, 3)
        ]

    def over_z(buf, slots, ss, qs):
        out = []
        for k in FAR_FIRST:
            to = (z + k) % NZ
            c = send(buf.at[to % 4], slots.at[k - 1], ss.at[k - 1], qs.at[k - 1], by_z[k - 1])
            out.append((c, to // 4 == core))
        return out

    p2y = over_x(jy, r2y, s2y, q2y)
    p2x = over_z(jx, r2x, s2x, q2x)
    p2z = over_x(jz, r2z, s2z, q2z)
    for c in p1x:
        c.wait_recv()
    jx[...] = total(hx[x], r1x, range(NX - 1))
    start_if(p2x)

    @pl.when(has_z)
    def _():
        for c, _ in p1z:
            c.wait_recv()
        jz[...] = total(hz[:, z % 4], r1z, range(NZ - 1))
        for c in p2z:
            c.start()

    @pl.when(mid_y)
    def _():
        for c, _ in p1y:
            c.wait_recv()
        jy[...] = total(hy[:, y % 4], r1y, range(NY - 1))
        for c in p2y:
            c.start()

    back = start(send(back_out, back_in, back_sem.at[0], back_sem.at[1], east))

    def y_copies(buf, ss, qs):
        return [
            send(buf.at[y], buf.at[y], ss.at[k - 1], qs.at[y], by_y[k - 1])
            for k in FAR_FIRST
        ]

    def y_arrivals(buf, ss, qs):
        return [
            send(buf.at[y], buf.at[(y + k) % NY], ss.at[k - 1], qs.at[(y + k) % NY], by_y[k - 1])
            for k in range(1, NY)
        ]

    own_y = jnp.logical_and(has_z, y == z)
    p3y = [
        (send(ky, r3y.at[k - 1], s3y.at[k - 1], q3y.at[k - 1], by_z[k - 1]), (z + k) % NZ == y)
        for k in range(1, NZ)
    ]
    bands = 2 * NY
    p4y = [
        send(fy, fy, s4y.at[k - 1], q4y, {"region": (region + k) % bands, "tile": tile})
        for k in (8, 7, 9, 6, 10, 5, 11, 4, 12, 3, 13, 2, 14, 1, 15)
    ]

    @pl.when(has_x)
    def _():
        for c, _ in p2x:
            c.wait_recv()
        r3x[y] = total(jx[z % 4], r2x, range(NZ - 1))
        for c in y_copies(r3x, s3x, q3x):
            c.start()

    @pl.when(has_z)
    def _():
        for c in p2z:
            c.wait_recv()
        r3z[y] = total(jz[x], r2z, range(NX - 1))
        for c in y_copies(r3z, s3z, q3z):
            c.start()

    @pl.when(mid_y)
    def _():
        for c in p2y:
            c.wait_recv()
        ky[...] = total(jy[x], r2y, range(NX - 1))
        start_if(p3y)

    @pl.when(own_y)
    def _():
        for c, _ in p3y:
            c.wait_recv()
        fy[...] = total(ky[...], r3y, range(NZ - 1))
        for c in p4y:
            c.start()

    def sent_if(copies):
        for c, yes in copies:
            pl.when(yes)(c.wait_send)

    for c in sends:
        c.wait_send()
    sent_if(p1y + p1z + p2x)

    @pl.when(mid_y)
    def _():
        for c in p2y:
            c.wait_send()
        sent_if(p3y)

    @pl.when(has_z)
    def _():
        for c in p2z:
            c.wait_send()

    back.wait_recv()
    far = back_in[...].astype(F32).reshape(8, 8, D)
    br0 = branch[0].astype(F32).reshape(16, 8, D)
    new_lo = dyv[:, :8, :].astype(F32) + jnp.where(sub, unpaired(far, roll4(far)), br0)
    out_ref[...] = jnp.concatenate([new_lo, hi_out[...]], axis=1).astype(BF16)

    @pl.when(has_x)
    def _():
        for c in y_copies(r3x, s3x, q3x):
            c.wait_send()

    @pl.when(has_z)
    def _():
        for c in y_copies(r3z, s3z, q3z):
            c.wait_send()

    last_x = send(fx, fx, s5.at[0], q5.at[0], other)
    last_z = send(fz, fz, s5.at[1], q5.at[1], other)

    def settle(buf, out, ss, qs, last):
        for c in y_arrivals(buf, ss, qs):
            c.wait_recv()
        out[...] = total(buf[0], buf, range(1, NY))
        last.start()

    @pl.when(has_x)
    def _():
        settle(r3x, fx, s3x, q3x, last_x)

    @pl.when(has_z)
    def _():
        settle(r3z, fz, s3z, q3z, last_z)

    @pl.when(jnp.logical_not(has_x))
    def _():
        last_x.wait_recv()

    @pl.when(jnp.logical_not(has_z))
    def _():
        last_z.wait_recv()

    pl.when(jnp.logical_not(own_y))(p4y[0].wait_recv)

    scale = 1.0 / math.sqrt(3 * 64 * 2 * NY * tiles)
    odd = (z % 2) == 1
    final = jnp.concatenate([fy[...], fx[...], fz[...]], axis=1).astype(F32) * scale
    for g in range(GROUPS):
        f = final[:, D * g:D * g + D]
        top, bot = f[0:8], f[8:16]
        top_r, bot_r = pltpu.roll(top, 4, 0), pltpu.roll(bot, 4, 0)
        low = low4((8, D))
        first = jnp.where(odd, jnp.where(low, bot_r, top_r), top)
        rest = jnp.where(odd, top_r, bot)
        extra = jnp.where(odd, bot, bot_r)
        for s in range(3):
            lanes = slice(s * D + 128 * g, s * D + 128 * g + 128)
            gq_ref[0:8, lanes] = first[:, 128 * s:128 * s + 128]
            gq_ref[8:12, lanes] = rest[0:4, 128 * s:128 * s + 128]
        go_ref[4 * g:4 * g + 4, :] = extra[0:4]

    @pl.when(own_y)
    def _():
        for c in p4y:
            c.wait_send()

    pl.when(has_x)(last_x.wait_send)
    pl.when(has_z)(last_z.wait_send)


def hand_over(a, b, c, a_out, b_out, c_out, sems):
    copies = [
        pltpu.make_async_copy(src, dst, sems.at[i])
        for i, (src, dst) in enumerate(((a, a_out), (b, b_out), (c, c_out)))
    ]
    for c in copies:
        c.start()
    for c in copies:
        c.wait()


def body(tokens, grad_out, ocean_mask, w_qkv, w_out):
    any_spec = pl.BlockSpec(memory_space=pl.ANY)
    vmem_spec = pl.BlockSpec(memory_space=pltpu.VMEM)

    def buf(*shape, dtype=BF16):
        return pltpu.VMEM(shape, dtype)

    def sem(*shape):
        return pltpu.SemaphoreType.DMA(shape)

    results = pl.pallas_call(
        kernel,
        out_shape=(buf(16, 16, D), buf(12, 3 * D, dtype=F32), buf(12, D, dtype=F32)),
        in_specs=[any_spec] * 5,
        out_specs=(vmem_spec, vmem_spec, vmem_spec),
        scratch_shapes=[
            buf(16, 16, D), buf(16, 16, D), pltpu.SMEM((2, 2), jnp.int32),
            buf(D, 3 * D), buf(D, D),
            buf(2, 64, D), buf(2, 64, D), buf(64, D), buf(64, D),
            buf(2, 128, D, dtype=F32), buf(2, D, 128), buf(2, D, 128), buf(2, D, 128),
            buf(2, 128, 2 * D), buf(2, 128, D, dtype=F32), buf(2, 128, 128, dtype=F32),
            buf(2, 128, D), buf(2, 128, D), buf(16, 8, D, dtype=F32),
            buf(GROUPS, 16, 8, D, dtype=F32),
            buf(NX, 8, 16, 3 * D), buf(NX, 4, 16, 3 * D),
            buf(NX, 4, 16, WX), buf(NX, 4, 16, WY), buf(NX, 4, 16, WZ),
            buf(NX - 1, 4, 16, WX), buf(NY - 1, NX, 16, WY), buf(NZ - 1, NX, 16, WZ),
            buf(4, 16, WX), buf(NX, 16, WY), buf(NX, 16, WZ),
            buf(NZ - 1, 16, WX), buf(NX - 1, 16, WY), buf(NX - 1, 16, WZ),
            buf(NY, 16, WX), buf(16, WY), buf(NZ - 1, 16, WY), buf(NY, 16, WZ),
            buf(16, WX), buf(16, WY), buf(16, WZ),
            sem(5), pltpu.SemaphoreType.REGULAR, pltpu.SemaphoreType.REGULAR, sem(2), sem(2), sem(2),
            sem(4), sem(4), sem(NX - 1), sem(NX - 1),
            sem(NY - 1), sem(NY - 1), sem(NZ - 1), sem(NZ - 1),
            sem(NZ - 1), sem(NZ - 1), sem(NX - 1), sem(NX - 1), sem(NX - 1), sem(NX - 1),
            sem(NY - 1), sem(NY), sem(NZ - 1), sem(NZ - 1), sem(NY - 1), sem(NY),
            sem(2 * NY - 1), pltpu.SemaphoreType.DMA, sem(2), sem(2),
        ],
        compiler_params=pltpu.CompilerParams(
            collective_id=0, has_side_effects=True, vmem_limit_bytes=56 * 1024 * 1024
        ),
        cost_estimate=pl.CostEstimate(
            flops=900_000_000, bytes_accessed=2_000_000, transcendentals=200_000
        ),
        name="window_grads",
    )(tokens, grad_out, ocean_mask, w_qkv, w_out)
    return pl.pallas_call(
        hand_over,
        out_shape=[jax.ShapeDtypeStruct(r.shape, r.dtype) for r in results],
        in_specs=[any_spec] * 3,
        out_specs=[any_spec] * 3,
        scratch_shapes=[sem(3)],
        compiler_params=pltpu.CompilerParams(vmem_limit_bytes=4 * 1024 * 1024),
        cost_estimate=pl.CostEstimate(flops=0, bytes_accessed=600_000, transcendentals=0),
        name="hand_over",
    )(*results)


def solution(mesh):
    return jax.shard_map(
        body,
        mesh=mesh,
        in_specs=(
            P("region", "tile", None),
            P("region", "tile", None),
            P("region", "tile"),
            P(),
            P(),
        ),
        out_specs=(P("region", "tile", None), P("tile", None), P("tile", None)),
        check_vma=False,
    )
```

```python
import math

import jax
import jax.numpy as jnp
from jax import lax
from jax.experimental import pallas as pl
from jax.experimental.pallas import tpu as pltpu
from jax.sharding import PartitionSpec as P

MESH = pl.DeviceIdType.MESH
F32 = jnp.float32
BF16 = jnp.bfloat16
D = 384
HD = 32
LOG2E = math.log2(math.e)
GROUPS = 3
NX, NZ, NY = 4, 8, 8
PX, PY, PZ = 0, 1, 2
FAR_FIRST = (4, 3, 5, 2, 6, 1, 7)
UP_FIRST = (1, 2, 3, 4, 7, 6, 5)
NT = (((1,), (1,)), ((), ()))


def dot(a, b, dims=(((1,), (0,)), ((), ()))):
    return lax.dot_general(a, b, dims, preferred_element_type=F32)


def roll4(a):
    n, _, width = a.shape
    return pltpu.roll(a.reshape(n * 8, width).reshape(n, 8, width), 4, 1)


def low4(shape):
    return lax.broadcasted_iota(jnp.int32, shape, len(shape) - 2) % 8 < 4


def part(array, a, first):
    return array[64 * a:64 * a + 64, first:first + 128]


def spread(array, a):
    lane_head = lax.broadcasted_iota(jnp.int32, (1, 128), 1) // HD
    order = (1, 0, 3, 2) if a else (0, 1, 2, 3)
    return jnp.concatenate(
        [array * (lane_head == h).astype(F32).astype(BF16) for h in order], axis=0
    )


def own(zero, one):
    first_half = lax.broadcasted_iota(jnp.int32, (1, 128), 1) < 64
    blocks = []
    for h in range(4):
        r, c = slice(32 * h, 32 * h + 32), slice(128 * (h // 2), 128 * (h // 2) + 128)
        if h % 2 == 0:
            blocks.append(jnp.where(first_half, zero[r, c], one[r, c]))
        else:
            blocks.append(pltpu.roll(jnp.where(first_half, one[r, c], zero[r, c]), 64, 1))
    return jnp.concatenate(blocks, axis=0).astype(BF16)


UNITS = [(a, g) for g in range(GROUPS) for a in range(2)]
ROOT = HD ** -0.5


def normalise(feats, normed_t, xhat, istd):
    center = jnp.mean(feats, axis=-1, keepdims=True)
    dev = feats - center
    inv = lax.rsqrt(jnp.mean(dev * dev, axis=-1, keepdims=True) + 1e-05)
    hat = dev * inv
    xhat[...] = hat
    istd[...] = jnp.broadcast_to(inv, (128, 128))
    nb = hat.astype(BF16)
    normed_t[...] = nb.T
    return nb


def scores(proj):
    q = [spread(part(proj, a, 128 * g), a) for a, g in UNITS]
    k = [part(proj, a, D + 128 * g) for a, g in UNITS]
    s = [dot(m, n, NT) for m, n in zip(k, q)]
    return q, [m.T for m in k], s


def softmax(s):
    p = []
    for t in s:
        e = jnp.exp2((t - jnp.max(t, axis=0, keepdims=True)) * (ROOT * LOG2E))
        p.append(e * (1.0 / jnp.sum(e, axis=0, keepdims=True)))
    return p


def grad_probs(proj, ga):
    o = [spread(part(ga, a, 128 * g), a) for a, g in UNITS]
    v = [part(proj, a, 2 * D + 128 * g) for a, g in UNITS]
    dp = [dot(m, n, NT) for m, n in zip(v, o)]
    return o, [m.T for m in v], dp


def grad_scores(p, dp):
    ds = []
    for t, d in zip(p, dp):
        row = jnp.sum(d * t, axis=0, keepdims=True)
        ds.append((t * ((d - row) * ROOT)).astype(BF16))
    return [t.astype(BF16) for t in p], ds


def products(q, o, kt, vt, pb, ds):
    qt = [dot(m, n) for m, n in zip(kt, ds)]
    dk = [dot(m, n) for m, n in zip(ds, q)]
    dv = [dot(m, n) for m, n in zip(pb, o)]
    ot = [dot(m, n) for m, n in zip(vt, pb)]
    return qt, dk, dv, ot


def keep_products(qt, dk, dv, ot, att_t, query_t, gp):
    for i, (a, g) in enumerate(UNITS):
        at_row = pl.ds(64 * a, 64)
        gp[at_row, 128 * g:128 * g + 128] = dk[i].astype(BF16)
        gp[at_row, D + 128 * g:D + 128 * g + 128] = dv[i].astype(BF16)
    for g in range(GROUPS):
        query_t[128 * g:128 * g + 128, :] = own(qt[2 * g], qt[2 * g + 1])
        att_t[128 * g:128 * g + 128, :] = own(ot[2 * g], ot[2 * g + 1])


def device():
    region, tile = lax.axis_index("region"), lax.axis_index("tile")
    tiles = NX * NZ
    west = {"region": region, "tile": (tile + tiles - 1) % tiles}
    east = {"region": region, "tile": (tile + 1) % tiles}
    return region, tile, west, east


def send(src, dst, ss, rs, dev):
    return pltpu.make_async_remote_copy(
        src_ref=src, dst_ref=dst, send_sem=ss, recv_sem=rs, device_id=dev, device_id_type=MESH,
    )


def greet(partners):
    barrier = pltpu.get_barrier_semaphore()
    for dev in partners:
        pl.semaphore_signal(barrier, inc=1, device_id=dev, device_id_type=MESH)
    return lambda: pl.semaphore_wait(barrier, len(partners))


def pairs(v):
    v = v.reshape(8, 2, 8, D)
    return v[:, 0], v[:, 1]


def kernel(
    x_hbm, dy_hbm, mask_hbm, wq_hbm, wo_hbm,
    out_ref, gq_ref, go_ref,
    xv, dyv, mask_ref, wq, wo,
    rim_out, rim_in, back_out, back_in,
    feats, normed_t, att_t, query_t, gp, xhat, istd, masked, branch, hi_out, spare,
    grads, r0, hx, hy, hz, r1x, r1y, r1z, jx, jy, jz,
    r2x, r2y, r2z, r3x, ky, r3y, r3z, fy,
    in_sem, two_away, four_away, rim_send, rim_recv, back_sem,
    s0, q0, s1x, q1x, s1y, q1y, s1z, q1z, s2x, q2x, s2y, q2y, s2z, q2z,
    s3x, q3x, s3y, q3y, s3z, q3z, s4y, q4y,
):
    loads = [
        pltpu.make_async_copy(src, dst, in_sem.at[i])
        for i, (src, dst) in enumerate(
            ((x_hbm, xv), (dy_hbm, dyv), (wq_hbm, wq), (wo_hbm, wo), (mask_hbm, mask_ref))
        )
    ]
    for c in loads[:2]:
        c.start()
    region, tile, west, east = device()
    y, core = region // 2, region % 2
    x, z = tile // NZ, tile % NZ
    tiles = NX * NZ

    def at(ax, ay, az, ac):
        return {"region": ay * 2 + ac, "tile": ax * NZ + az}

    other = at(x, y, z, 1 - core)
    by_x = [at((x + k) % NX, y, z, core) for k in range(1, NX)]
    by_z = [at(x, y, (z + k) % NZ, core) for k in range(1, NZ)]
    by_y = [at(x, (y + k) % NY, z, core) for k in range(1, NY)]
    near = [by_x[0], by_x[2], by_y[0], by_y[6], by_z[0], by_z[6]]
    greeted = greet([west, east, other] + near)
    for c in loads[2:]:
        c.start()
    sub = low4((1, 8, D))

    def halves(ref):
        v = ref[...].astype(F32)
        return v[:, :8, :], v[:, 8:, :]

    def rim_of(lo):
        even, odd = pairs(lo)
        return jnp.where(sub, even, roll4(odd)).reshape(64, D).astype(BF16)

    rims = [
        send(rim_out.at[i], rim_in.at[i], rim_send.at[i], rim_recv.at[i], west) for i in range(2)
    ]
    loads[0].wait()
    x_lo, x_hi = halves(xv)
    rim_out[0] = rim_of(x_lo)
    greeted()
    rims[0].start()
    for dev in near:
        pl.semaphore_signal(two_away, inc=1, device_id=dev, device_id_type=MESH)
    loads[1].wait()
    dy_lo, dy_hi = halves(dyv)
    rim_out[1] = rim_of(dy_lo)
    rims[1].start()

    for c in loads[2:]:
        c.wait()

    def mask_of(dys, b):
        flag = [mask_ref[a, b].astype(F32) for a in range(2)]
        return jnp.concatenate([dys[:64] * flag[0], dys[64:] * flag[1]], axis=0).astype(BF16)

    def joined(hi, far):
        even, odd = pairs(hi.astype(F32))
        loc = jnp.where(sub, roll4(even), odd).reshape(64, D)
        far = far.astype(F32)
        return jnp.concatenate([loc[:32], far[:32], loc[32:], far[32:]], axis=0)

    feats[0] = jnp.where(sub, x_hi, x_lo).reshape(128, D)
    masked[0] = mask_of(jnp.where(sub, dy_hi, dy_lo).reshape(128, D), 0)
    far = [by_y[1], by_y[5], by_z[1], by_z[5]]

    def column(b, _):
        @pl.when(b == 1)
        def _():
            pl.semaphore_wait(two_away, len(near))
            for dev in far:
                pl.semaphore_signal(four_away, inc=1, device_id=dev, device_id_type=MESH)
            rims[0].wait()
            feats[1] = joined(xv[:, 8:, :], rim_in[0])

        nb = normalise(feats[b], normed_t.at[b], xhat.at[b], istd.at[b])
        proj = dot(nb, wq[...]).astype(BF16)
        q, kt, sc = scores(proj)
        p = softmax(sc)

        @pl.when(b == 1)
        def _():
            rims[1].wait()
            masked[1] = mask_of(joined(dyv[:, 8:, :], rim_in[1]), 1)

        ga = dot(masked[b], wo[...], NT).astype(BF16)
        o, vt, dp = grad_probs(proj, ga)
        pb, ds = grad_scores(p, dp)
        keep_products(
            *products(q, o, kt, vt, pb, ds), att_t.at[b], query_t.at[b], gp.at[b]
        )
        return 0

    lax.fori_loop(0, 2, column, 0)

    def both(a, b, axis):
        return jnp.concatenate([a, b], axis=axis)

    nt = both(normed_t[0], normed_t[1], 1)
    ga_full = dot(both(att_t[0], att_t[1], 1), both(masked[0], masked[1], 0)).reshape(16, 3, 8, D)
    w0, w1, w2 = ga_full[:, 0], ga_full[:, 1], ga_full[:, 2]
    spare[0] = roll4(jnp.where(sub, w0, w1))
    spare[1] = jnp.where(sub, w2, w0)
    spare[2] = roll4(jnp.where(sub, w1, w2))
    sends = []

    def start(c):
        c.start()
        sends.append(c)
        return c

    keep = {PX: core, PY: 1 - core, PZ: 1 - core}
    pl.semaphore_wait(four_away, len(far))

    def swap(g, half):
        return send(grads.at[g, :, pl.ds(half * 4, 4)], r0.at[g], s0.at[g], q0.at[g], other)

    def gradients(g, _):
        at_g = pl.ds(pl.multiple_of(128 * g, 128), 128)
        at_gv = pl.ds(pl.multiple_of(D + 128 * g, 128), 128)
        gn = jnp.concatenate([
            dot(nt, both(query_t[0, at_g, :], query_t[1, at_g, :], 1), NT),
            dot(nt, both(gp[0, :, at_g], gp[1, :, at_g], 0)),
            dot(nt, both(gp[0, :, at_gv], gp[1, :, at_gv], 0)),
        ], axis=1).reshape(16, 3, 8, D)
        v0, v1, v2, extra = gn[:, 0], gn[:, 1], gn[:, 2], spare[g]
        packed = jnp.stack(
            [v0, jnp.where(sub, v1, extra), v2, jnp.where(sub, extra, v1)], axis=1
        ).reshape(NX, NZ, 16, D).astype(BF16)
        grads[g] = packed
        swap(g, jnp.where(g == PX, 1 - core, core)).start()
        return 0

    lax.fori_loop(0, GROUPS, gradients, 0)
    core0 = [swap(g, 1 - keep[g]) for g in range(GROUPS)]
    sends += core0

    def start_if(copies):
        for c, yes in copies:
            pl.when(yes)(c.start)

    def combined(part):
        core0[part].wait_recv()
        mine = grads[part, :, pl.ds(keep[part] * 4, 4)].astype(F32)
        return (mine + r0[part].astype(F32)).astype(BF16)

    def around(order, buf, slots, ss, qs, devs, place, half):
        out = []
        for k in order:
            to = (place + k) % 8
            c = send(buf.at[:, to % 4], slots.at[k - 1], ss.at[k - 1], qs.at[k - 1], devs[k - 1])
            out.append((c, to // 4 == half))
        return out

    row = (y + 4) % NY
    p1y = around(FAR_FIRST, hy, r1y, s1y, q1y, by_y, row, keep[PY])
    p1z = around(UP_FIRST, hz, r1z, s1z, q1z, by_z, z, keep[PZ])
    hx[...] = combined(PX)
    p1x = [
        start(send(hx.at[(x + k) % NX], r1x.at[k - 1], s1x.at[k - 1], q1x.at[k - 1], by_x[k - 1]))
        for k in (2, 1, 3)
    ]
    hy[...] = combined(PY)
    start_if(p1y)
    hz[...] = combined(PZ)
    start_if(p1z)

    def branch_of(b, _):
        gn = dot(query_t[b].T, wq[:, 0:D], NT) + dot(gp[b], wq[:, D:3 * D], NT)
        hat = xhat[b]
        m0 = jnp.mean(gn, axis=-1, keepdims=True)
        m1 = jnp.mean(gn * hat, axis=-1, keepdims=True)
        branch[b] = (istd[b][:, 0:1] * (gn - m0 - hat * m1)).astype(BF16)
        return 0

    lax.fori_loop(0, 2, branch_of, 0)
    back_out[0:32, :] = branch[1, 32:64, :]
    back_out[32:64, :] = branch[1, 96:128, :]
    loc = both(branch[1, 0:32, :], branch[1, 64:96, :], 0).astype(F32).reshape(8, 8, D)

    def unpaired(even, odd):
        return jnp.stack([even, odd], axis=1).reshape(16, 8, D)

    br0 = branch[0].astype(F32).reshape(16, 8, D)
    hi_out[...] = dyv[:, 8:, :].astype(F32) + jnp.where(sub, br0, unpaired(roll4(loc), loc))

    has_x = z // 4 == core
    has_z = z // 4 != core
    mid_y = row // 4 != core

    def total(first, buf, slots):
        t = first.astype(F32)
        for i in slots:
            t = t + buf[i].astype(F32)
        return t.astype(BF16)

    def over_x(buf, slots, ss, qs):
        return [
            send(buf.at[(x + k) % NX], slots.at[k - 1], ss.at[k - 1], qs.at[k - 1], by_x[k - 1])
            for k in (2, 1, 3)
        ]

    def over_z(buf, slots, ss, qs):
        out = []
        for k in UP_FIRST:
            to = (z + k) % NZ
            c = send(buf.at[to % 4], slots.at[k - 1], ss.at[k - 1], qs.at[k - 1], by_z[k - 1])
            out.append((c, to // 4 == core))
        return out

    p2y = over_x(jy, r2y, s2y, q2y)
    p2x = over_z(jx, r2x, s2x, q2x)
    p2z = over_x(jz, r2z, s2z, q2z)
    for c in p1x:
        c.wait_recv()
    jx[...] = total(hx[x], r1x, range(NX - 1))
    start_if(p2x)

    @pl.when(has_z)
    def _():
        for c, _ in p1z:
            c.wait_recv()
        jz[...] = total(hz[:, z % 4], r1z, range(NZ - 1))
        for c in p2z:
            c.start()

    @pl.when(mid_y)
    def _():
        for c, _ in p1y:
            c.wait_recv()
        jy[...] = total(hy[:, row % 4], r1y, range(NY - 1))
        for c in p2y:
            c.start()

    back = start(send(back_out, back_in, back_sem.at[0], back_sem.at[1], east))

    bands = 2 * NY
    by_region = [
        {"region": (region + k) % bands, "tile": tile}
        for k in (8, 7, 9, 6, 10, 5, 11, 4, 12, 3, 13, 2, 14, 1, 15)
    ]

    def y_copies(buf, ss, qs):
        return [
            send(buf.at[y], buf.at[y], ss.at[k], qs.at[y], dev) for k, dev in enumerate(by_region)
        ]

    def y_arrivals(buf, ss, qs, holder):
        out = []
        for k in range(NY):
            place = (y + k) % NY
            c = send(buf.at[y], buf.at[place], ss.at[0], qs.at[place], by_region[0])
            out.append((c, jnp.logical_not(holder) if k == 0 else None))
        return out

    own_y = jnp.logical_and(has_z, row == z)
    p3y = [
        (send(ky, r3y.at[k - 1], s3y.at[k - 1], q3y.at[k - 1], by_z[k - 1]), (z + k) % NZ == row)
        for k in range(1, NZ)
    ]
    p4y = [send(fy, fy, s4y.at[k], q4y, dev) for k, dev in enumerate(by_region)]

    @pl.when(has_x)
    def _():
        for c, _ in p2x:
            c.wait_recv()
        r3x[y] = total(jx[z % 4], r2x, range(NZ - 1))
        for c in y_copies(r3x, s3x, q3x):
            c.start()

    @pl.when(has_z)
    def _():
        for c in p2z:
            c.wait_recv()
        r3z[y] = total(jz[x], r2z, range(NX - 1))
        for c in y_copies(r3z, s3z, q3z):
            c.start()

    @pl.when(mid_y)
    def _():
        for c in p2y:
            c.wait_recv()
        ky[...] = total(jy[x], r2y, range(NX - 1))
        start_if(p3y)

    @pl.when(own_y)
    def _():
        for c, _ in p3y:
            c.wait_recv()
        fy[...] = total(ky[...], r3y, range(NZ - 1))
        for c in p4y:
            c.start()

    def sent_if(copies):
        for c, yes in copies:
            pl.when(yes)(c.wait_send)

    for c in sends:
        c.wait_send()
    sent_if(p1y + p1z + p2x)

    @pl.when(mid_y)
    def _():
        for c in p2y:
            c.wait_send()
        sent_if(p3y)

    @pl.when(has_z)
    def _():
        for c in p2z:
            c.wait_send()

    back.wait_recv()
    far = back_in[...].astype(F32).reshape(8, 8, D)
    br0 = branch[0].astype(F32).reshape(16, 8, D)
    new_lo = dyv[:, :8, :].astype(F32) + jnp.where(sub, unpaired(far, roll4(far)), br0)
    out_ref[...] = jnp.concatenate([new_lo, hi_out[...]], axis=1).astype(BF16)

    @pl.when(has_x)
    def _():
        for c in y_copies(r3x, s3x, q3x):
            c.wait_send()

    @pl.when(has_z)
    def _():
        for c in y_copies(r3z, s3z, q3z):
            c.wait_send()

    def settled(buf, ss, qs, holder):
        for c, other_core in y_arrivals(buf, ss, qs, holder):
            if other_core is None:
                c.wait_recv()
            else:
                pl.when(other_core)(c.wait_recv)
        t = buf[0].astype(F32)
        for i in range(1, NY):
            t = t + buf[i].astype(F32)
        return t

    pl.when(jnp.logical_not(own_y))(p4y[0].wait_recv)
    sum_x = settled(r3x, s3x, q3x, has_x)
    sum_z = settled(r3z, s3z, q3z, has_z)

    scale = 1.0 / math.sqrt(3 * 64 * 2 * NY * tiles)
    odd = (z % 2) == 1
    final = jnp.concatenate([sum_x, fy[...].astype(F32), sum_z], axis=1) * scale
    for g in range(GROUPS):
        f = final[:, D * g:D * g + D]
        top, bot = f[0:8], f[8:16]
        top_r, bot_r = pltpu.roll(top, 4, 0), pltpu.roll(bot, 4, 0)
        low = low4((8, D))
        first = jnp.where(odd, jnp.where(low, bot_r, top_r), top)
        rest = jnp.where(odd, top_r, bot)
        extra = jnp.where(odd, bot, bot_r)
        for s in range(3):
            lanes = slice(s * D + 128 * g, s * D + 128 * g + 128)
            gq_ref[0:8, lanes] = first[:, 128 * s:128 * s + 128]
            gq_ref[8:12, lanes] = rest[0:4, 128 * s:128 * s + 128]
        go_ref[4 * g:4 * g + 4, :] = extra[0:4]

    @pl.when(own_y)
    def _():
        for c in p4y:
            c.wait_send()


def hand_over(a, b, c, a_out, b_out, c_out, sems):
    copies = [
        pltpu.make_async_copy(src, dst, sems.at[i])
        for i, (src, dst) in enumerate(((a, a_out), (b, b_out), (c, c_out)))
    ]
    for c in copies:
        c.start()
    for c in copies:
        c.wait()


def body(tokens, grad_out, ocean_mask, w_qkv, w_out):
    any_spec = pl.BlockSpec(memory_space=pl.ANY)
    vmem_spec = pl.BlockSpec(memory_space=pltpu.VMEM)

    def buf(*shape, dtype=BF16):
        return pltpu.VMEM(shape, dtype)

    def sem(*shape):
        return pltpu.SemaphoreType.DMA(shape)

    results = pl.pallas_call(
        kernel,
        out_shape=(buf(16, 16, D), buf(12, 3 * D, dtype=F32), buf(12, D, dtype=F32)),
        in_specs=[any_spec] * 5,
        out_specs=(vmem_spec, vmem_spec, vmem_spec),
        scratch_shapes=[
            buf(16, 16, D), buf(16, 16, D), pltpu.SMEM((2, 2), jnp.int32),
            buf(D, 3 * D), buf(D, D),
            buf(2, 64, D), buf(2, 64, D), buf(64, D), buf(64, D),
            buf(2, 128, D, dtype=F32), buf(2, D, 128), buf(2, D, 128), buf(2, D, 128),
            buf(2, 128, 2 * D), buf(2, 128, D, dtype=F32), buf(2, 128, 128, dtype=F32),
            buf(2, 128, D), buf(2, 128, D), buf(16, 8, D, dtype=F32),
            buf(GROUPS, 16, 8, D, dtype=F32),
            buf(3, NX, 8, 16, D), buf(3, NX, 4, 16, D),
            buf(NX, 4, 16, D), buf(NX, 4, 16, D), buf(NX, 4, 16, D),
            buf(NX - 1, 4, 16, D), buf(NY - 1, NX, 16, D), buf(NZ - 1, NX, 16, D),
            buf(4, 16, D), buf(NX, 16, D), buf(NX, 16, D),
            buf(NZ - 1, 16, D), buf(NX - 1, 16, D), buf(NX - 1, 16, D),
            buf(NY, 16, D), buf(16, D), buf(NZ - 1, 16, D), buf(NY, 16, D),
            buf(16, D),
            sem(5), pltpu.SemaphoreType.REGULAR, pltpu.SemaphoreType.REGULAR, sem(2), sem(2), sem(2),
            sem(3), sem(3), sem(NX - 1), sem(NX - 1),
            sem(NY - 1), sem(NY - 1), sem(NZ - 1), sem(NZ - 1),
            sem(NZ - 1), sem(NZ - 1), sem(NX - 1), sem(NX - 1), sem(NX - 1), sem(NX - 1),
            sem(2 * NY - 1), sem(NY), sem(NZ - 1), sem(NZ - 1), sem(2 * NY - 1), sem(NY),
            sem(2 * NY - 1), pltpu.SemaphoreType.DMA,
        ],
        compiler_params=pltpu.CompilerParams(
            collective_id=0, has_side_effects=True, vmem_limit_bytes=56 * 1024 * 1024
        ),
        cost_estimate=pl.CostEstimate(
            flops=900_000_000, bytes_accessed=2_000_000, transcendentals=200_000
        ),
        name="window_grads",
    )(tokens, grad_out, ocean_mask, w_qkv, w_out)
    return pl.pallas_call(
        hand_over,
        out_shape=[jax.ShapeDtypeStruct(r.shape, r.dtype) for r in results],
        in_specs=[any_spec] * 3,
        out_specs=[any_spec] * 3,
        scratch_shapes=[sem(3)],
        compiler_params=pltpu.CompilerParams(vmem_limit_bytes=4 * 1024 * 1024),
        cost_estimate=pl.CostEstimate(flops=0, bytes_accessed=600_000, transcendentals=0),
        name="hand_over",
    )(*results)


def solution(mesh):
    return jax.shard_map(
        body,
        mesh=mesh,
        in_specs=(
            P("region", "tile", None),
            P("region", "tile", None),
            P("region", "tile"),
            P(),
            P(),
        ),
        out_specs=(P("region", "tile", None), P("tile", None), P("tile", None)),
        check_vma=False,
    )
```

```python
import math

import jax
import jax.numpy as jnp
from jax import lax
from jax.experimental import pallas as pl
from jax.experimental.pallas import tpu as pltpu
from jax.sharding import PartitionSpec as P

MESH = pl.DeviceIdType.MESH
F32 = jnp.float32
BF16 = jnp.bfloat16
D = 384
HD = 32
LOG2E = math.log2(math.e)
GROUPS = 3
NX, NZ, NY = 4, 8, 8
PX, PY, PZ = 0, 1, 2
FAR_FIRST = (4, 3, 5, 2, 6, 1, 7)
UP_FIRST = (1, 2, 3, 4, 7, 6, 5)
NT = (((1,), (1,)), ((), ()))


def dot(a, b, dims=(((1,), (0,)), ((), ()))):
    return lax.dot_general(a, b, dims, preferred_element_type=F32)


def roll4(a):
    n, _, width = a.shape
    return pltpu.roll(a.reshape(n * 8, width).reshape(n, 8, width), 4, 1)


def low4(shape):
    return lax.broadcasted_iota(jnp.int32, shape, len(shape) - 2) % 8 < 4


def part(array, a, first):
    return array[64 * a:64 * a + 64, first:first + 128]


def spread(array, a):
    lane_head = lax.broadcasted_iota(jnp.int32, (1, 128), 1) // HD
    order = (1, 0, 3, 2) if a else (0, 1, 2, 3)
    return jnp.concatenate(
        [array * (lane_head == h).astype(F32).astype(BF16) for h in order], axis=0
    )


def own(zero, one):
    first_half = lax.broadcasted_iota(jnp.int32, (1, 128), 1) < 64
    blocks = []
    for h in range(4):
        r, c = slice(32 * h, 32 * h + 32), slice(128 * (h // 2), 128 * (h // 2) + 128)
        if h % 2 == 0:
            blocks.append(jnp.where(first_half, zero[r, c], one[r, c]))
        else:
            blocks.append(pltpu.roll(jnp.where(first_half, one[r, c], zero[r, c]), 64, 1))
    return jnp.concatenate(blocks, axis=0).astype(BF16)


UNITS = [(a, g) for g in range(GROUPS) for a in range(2)]
ROOT = HD ** -0.5


def normalise(feats, normed_t, xhat, istd):
    center = jnp.mean(feats, axis=-1, keepdims=True)
    dev = feats - center
    inv = lax.rsqrt(jnp.mean(dev * dev, axis=-1, keepdims=True) + 1e-05)
    hat = dev * inv
    xhat[...] = hat
    istd[...] = jnp.broadcast_to(inv, (128, 128))
    nb = hat.astype(BF16)
    normed_t[...] = nb.T
    return nb


def scores(proj):
    q = [spread(part(proj, a, 128 * g), a) for a, g in UNITS]
    k = [part(proj, a, D + 128 * g) for a, g in UNITS]
    s = [dot(m, n, NT) for m, n in zip(k, q)]
    return q, [m.T for m in k], s


def softmax(s):
    p = []
    for t in s:
        e = jnp.exp2((t - jnp.max(t, axis=0, keepdims=True)) * (ROOT * LOG2E))
        p.append(e * (1.0 / jnp.sum(e, axis=0, keepdims=True)))
    return p


def grad_probs(proj, ga):
    o = [spread(part(ga, a, 128 * g), a) for a, g in UNITS]
    v = [part(proj, a, 2 * D + 128 * g) for a, g in UNITS]
    dp = [dot(m, n, NT) for m, n in zip(v, o)]
    return o, [m.T for m in v], dp


def grad_scores(p, dp):
    ds = []
    for t, d in zip(p, dp):
        row = jnp.sum(d * t, axis=0, keepdims=True)
        ds.append((t * ((d - row) * ROOT)).astype(BF16))
    return [t.astype(BF16) for t in p], ds


def products(q, o, kt, vt, pb, ds):
    qt = [dot(m, n) for m, n in zip(kt, ds)]
    dk = [dot(m, n) for m, n in zip(ds, q)]
    dv = [dot(m, n) for m, n in zip(pb, o)]
    ot = [dot(m, n) for m, n in zip(vt, pb)]
    return qt, dk, dv, ot


def keep_products(qt, dk, dv, ot, att_t, query_t, gp):
    for i, (a, g) in enumerate(UNITS):
        at_row = pl.ds(64 * a, 64)
        gp[at_row, 128 * g:128 * g + 128] = dk[i].astype(BF16)
        gp[at_row, D + 128 * g:D + 128 * g + 128] = dv[i].astype(BF16)
    for g in range(GROUPS):
        query_t[128 * g:128 * g + 128, :] = own(qt[2 * g], qt[2 * g + 1])
        att_t[128 * g:128 * g + 128, :] = own(ot[2 * g], ot[2 * g + 1])


def device():
    region, tile = lax.axis_index("region"), lax.axis_index("tile")
    tiles = NX * NZ
    west = {"region": region, "tile": (tile + tiles - 1) % tiles}
    east = {"region": region, "tile": (tile + 1) % tiles}
    return region, tile, west, east


def send(src, dst, ss, rs, dev):
    return pltpu.make_async_remote_copy(
        src_ref=src, dst_ref=dst, send_sem=ss, recv_sem=rs, device_id=dev, device_id_type=MESH,
    )


def greet(partners):
    barrier = pltpu.get_barrier_semaphore()
    for dev in partners:
        pl.semaphore_signal(barrier, inc=1, device_id=dev, device_id_type=MESH)
    return lambda: pl.semaphore_wait(barrier, len(partners))


def pairs(v):
    v = v.reshape(8, 2, 8, D)
    return v[:, 0], v[:, 1]


def kernel(
    x_hbm, dy_hbm, mask_hbm, wq_hbm, wo_hbm,
    out_ref, gq_ref, go_ref,
    xv, dyv, mask_ref, wq, wo,
    rim_out, rim_in, back_out, back_in,
    feats, normed_t, att_t, query_t, gp, xhat, istd, masked, branch, hi_out, spare,
    grads, r0, hx, hy, hz, r1x, r1y, r1z, jx, jy, jz,
    r2x, r2y, r2z, r3x, ky, r3y, r3z, fy,
    in_sem, two_away, four_away, rim_send, rim_recv, back_sem,
    s0, q0, s1x, q1x, s1y, q1y, s1z, q1z, s2x, q2x, s2y, q2y, s2z, q2z,
    s3x, q3x, s3y, q3y, s3z, q3z, s4y, q4y,
):
    loads = [
        pltpu.make_async_copy(src, dst, in_sem.at[i])
        for i, (src, dst) in enumerate(
            ((x_hbm, xv), (dy_hbm, dyv), (wq_hbm, wq), (wo_hbm, wo), (mask_hbm, mask_ref))
        )
    ]
    for c in loads[:2]:
        c.start()
    region, tile, west, east = device()
    y, core = region // 2, region % 2
    x, z = tile // NZ, tile % NZ
    tiles = NX * NZ

    def at(ax, ay, az, ac):
        return {"region": ay * 2 + ac, "tile": ax * NZ + az}

    other = at(x, y, z, 1 - core)
    by_x = [at((x + k) % NX, y, z, core) for k in range(1, NX)]
    by_z = [at(x, y, (z + k) % NZ, core) for k in range(1, NZ)]
    by_y = [at(x, (y + k) % NY, z, core) for k in range(1, NY)]
    near = [by_x[0], by_x[2], by_y[0], by_y[6], by_z[0], by_z[6]]
    greeted = greet([west, east, other] + near)
    for c in loads[2:]:
        c.start()
    sub = low4((1, 8, D))

    def halves(ref):
        v = ref[...].astype(F32)
        return v[:, :8, :], v[:, 8:, :]

    def rim_of(lo):
        even, odd = pairs(lo)
        return jnp.where(sub, even, roll4(odd)).reshape(64, D).astype(BF16)

    rims = [
        send(rim_out.at[i], rim_in.at[i], rim_send.at[i], rim_recv.at[i], west) for i in range(2)
    ]
    loads[0].wait()
    x_lo, x_hi = halves(xv)
    rim_out[0] = rim_of(x_lo)
    greeted()
    rims[0].start()
    for dev in near:
        pl.semaphore_signal(two_away, inc=1, device_id=dev, device_id_type=MESH)
    loads[1].wait()
    dy_lo, dy_hi = halves(dyv)
    rim_out[1] = rim_of(dy_lo)
    rims[1].start()

    for c in loads[2:]:
        c.wait()

    def mask_of(dys, b):
        flag = [mask_ref[a, b].astype(F32) for a in range(2)]
        return jnp.concatenate([dys[:64] * flag[0], dys[64:] * flag[1]], axis=0).astype(BF16)

    def joined(hi, far):
        even, odd = pairs(hi.astype(F32))
        loc = jnp.where(sub, roll4(even), odd).reshape(64, D)
        far = far.astype(F32)
        return jnp.concatenate([loc[:32], far[:32], loc[32:], far[32:]], axis=0)

    feats[0] = jnp.where(sub, x_hi, x_lo).reshape(128, D)
    masked[0] = mask_of(jnp.where(sub, dy_hi, dy_lo).reshape(128, D), 0)
    far = [by_y[1], by_y[5], by_z[1], by_z[5]]

    def column(b, _):
        @pl.when(b == 1)
        def _():
            pl.semaphore_wait(two_away, len(near))
            for dev in far:
                pl.semaphore_signal(four_away, inc=1, device_id=dev, device_id_type=MESH)
            rims[0].wait()
            feats[1] = joined(xv[:, 8:, :], rim_in[0])

        nb = normalise(feats[b], normed_t.at[b], xhat.at[b], istd.at[b])
        proj = dot(nb, wq[...]).astype(BF16)
        q, kt, sc = scores(proj)
        p = softmax(sc)

        @pl.when(b == 1)
        def _():
            rims[1].wait()
            masked[1] = mask_of(joined(dyv[:, 8:, :], rim_in[1]), 1)

        ga = dot(masked[b], wo[...], NT).astype(BF16)
        o, vt, dp = grad_probs(proj, ga)
        pb, ds = grad_scores(p, dp)
        keep_products(
            *products(q, o, kt, vt, pb, ds), att_t.at[b], query_t.at[b], gp.at[b]
        )
        return 0

    lax.fori_loop(0, 2, column, 0)

    def both(a, b, axis):
        return jnp.concatenate([a, b], axis=axis)

    nt = both(normed_t[0], normed_t[1], 1)
    ga_full = dot(both(att_t[0], att_t[1], 1), both(masked[0], masked[1], 0)).reshape(16, 3, 8, D)
    w0, w1, w2 = ga_full[:, 0], ga_full[:, 1], ga_full[:, 2]
    spare[0] = roll4(jnp.where(sub, w0, w1))
    spare[1] = jnp.where(sub, w2, w0)
    spare[2] = roll4(jnp.where(sub, w1, w2))
    sends = []

    def start(c):
        c.start()
        sends.append(c)
        return c

    keep = {PX: core, PY: 1 - core, PZ: 1 - core}
    pl.semaphore_wait(four_away, len(far))

    def swap(g, half):
        return send(grads.at[g, :, pl.ds(half * 4, 4)], r0.at[g], s0.at[g], q0.at[g], other)

    def gradients(g, _):
        at_g = pl.ds(pl.multiple_of(128 * g, 128), 128)
        at_gv = pl.ds(pl.multiple_of(D + 128 * g, 128), 128)
        gn = jnp.concatenate([
            dot(nt, both(query_t[0, at_g, :], query_t[1, at_g, :], 1), NT),
            dot(nt, both(gp[0, :, at_g], gp[1, :, at_g], 0)),
            dot(nt, both(gp[0, :, at_gv], gp[1, :, at_gv], 0)),
        ], axis=1).reshape(16, 3, 8, D)
        v0, v1, v2, extra = gn[:, 0], gn[:, 1], gn[:, 2], spare[g]
        packed = jnp.stack(
            [v0, jnp.where(sub, v1, extra), v2, jnp.where(sub, extra, v1)], axis=1
        ).reshape(NX, NZ, 16, D).astype(BF16)
        grads[g] = packed
        swap(g, jnp.where(g == PX, 1 - core, core)).start()
        return 0

    lax.fori_loop(0, GROUPS, gradients, 0)
    core0 = [swap(g, 1 - keep[g]) for g in range(GROUPS)]
    sends += core0

    def start_if(copies):
        for c, yes in copies:
            pl.when(yes)(c.start)

    def combined(part):
        core0[part].wait_recv()
        mine = grads[part, :, pl.ds(keep[part] * 4, 4)].astype(F32)
        return (mine + r0[part].astype(F32)).astype(BF16)

    def around(order, buf, slots, ss, qs, devs, place, half):
        out = []
        for k in order:
            to = (place + k) % 8
            c = send(buf.at[:, to % 4], slots.at[k - 1], ss.at[k - 1], qs.at[k - 1], devs[k - 1])
            out.append((c, to // 4 == half))
        return out

    p1y = around(FAR_FIRST, hy, r1y, s1y, q1y, by_y, y, keep[PY])
    p1z = around(UP_FIRST, hz, r1z, s1z, q1z, by_z, z, keep[PZ])
    hx[...] = combined(PX)
    p1x = [
        start(send(hx.at[(x + k) % NX], r1x.at[k - 1], s1x.at[k - 1], q1x.at[k - 1], by_x[k - 1]))
        for k in (2, 1, 3)
    ]
    hy[...] = combined(PY)
    start_if(p1y)
    hz[...] = combined(PZ)
    start_if(p1z)

    def branch_of(b, _):
        gn = dot(query_t[b].T, wq[:, 0:D], NT) + dot(gp[b], wq[:, D:3 * D], NT)
        hat = xhat[b]
        m0 = jnp.mean(gn, axis=-1, keepdims=True)
        m1 = jnp.mean(gn * hat, axis=-1, keepdims=True)
        branch[b] = (istd[b][:, 0:1] * (gn - m0 - hat * m1)).astype(BF16)
        return 0

    lax.fori_loop(0, 2, branch_of, 0)
    back_out[0:32, :] = branch[1, 32:64, :]
    back_out[32:64, :] = branch[1, 96:128, :]
    back = start(send(back_out, back_in, back_sem.at[0], back_sem.at[1], east))
    loc = both(branch[1, 0:32, :], branch[1, 64:96, :], 0).astype(F32).reshape(8, 8, D)

    def unpaired(even, odd):
        return jnp.stack([even, odd], axis=1).reshape(16, 8, D)

    br0 = branch[0].astype(F32).reshape(16, 8, D)
    hi_out[...] = dyv[:, 8:, :].astype(F32) + jnp.where(sub, br0, unpaired(roll4(loc), loc))

    has_x = z // 4 == core
    has_z = z // 4 != core
    mid_y = y // 4 != core

    def total(first, buf, slots):
        t = first.astype(F32)
        for i in slots:
            t = t + buf[i].astype(F32)
        return t.astype(BF16)

    def over_x(buf, slots, ss, qs):
        return [
            send(buf.at[(x + k) % NX], slots.at[k - 1], ss.at[k - 1], qs.at[k - 1], by_x[k - 1])
            for k in (2, 1, 3)
        ]

    def over_z(buf, slots, ss, qs):
        out = []
        for k in UP_FIRST:
            to = (z + k) % NZ
            c = send(buf.at[to % 4], slots.at[k - 1], ss.at[k - 1], qs.at[k - 1], by_z[k - 1])
            out.append((c, to // 4 == core))
        return out

    p2y = over_x(jy, r2y, s2y, q2y)
    p2x = over_z(jx, r2x, s2x, q2x)
    p2z = over_x(jz, r2z, s2z, q2z)
    for c in p1x:
        c.wait_recv()
    jx[...] = total(hx[x], r1x, range(NX - 1))
    start_if(p2x)

    @pl.when(has_z)
    def _():
        for c, _ in p1z:
            c.wait_recv()
        jz[...] = total(hz[:, z % 4], r1z, range(NZ - 1))
        for c in p2z:
            c.start()

    @pl.when(mid_y)
    def _():
        for c, _ in p1y:
            c.wait_recv()
        jy[...] = total(hy[:, y % 4], r1y, range(NY - 1))
        for c in p2y:
            c.start()

    bands = 2 * NY
    by_region = [
        {"region": (region + k) % bands, "tile": tile}
        for k in (8, 7, 9, 6, 10, 5, 11, 4, 12, 3, 13, 2, 14, 1, 15)
    ]

    def y_copies(buf, ss, qs):
        return [
            send(buf.at[y], buf.at[y], ss.at[k], qs.at[y], dev) for k, dev in enumerate(by_region)
        ]

    def y_arrivals(buf, ss, qs, holder):
        out = []
        for k in range(NY):
            row = (y + k) % NY
            c = send(buf.at[y], buf.at[row], ss.at[0], qs.at[row], by_region[0])
            out.append((c, jnp.logical_not(holder) if k == 0 else None))
        return out

    own_y = jnp.logical_and(has_z, y == z)
    p3y = [
        (send(ky, r3y.at[k - 1], s3y.at[k - 1], q3y.at[k - 1], by_z[k - 1]), (z + k) % NZ == y)
        for k in range(1, NZ)
    ]
    p4y = [send(fy, fy, s4y.at[k], q4y, dev) for k, dev in enumerate(by_region)]

    @pl.when(has_x)
    def _():
        for c, _ in p2x:
            c.wait_recv()
        r3x[y] = total(jx[z % 4], r2x, range(NZ - 1))
        for c in y_copies(r3x, s3x, q3x):
            c.start()

    @pl.when(mid_y)
    def _():
        for c in p2y:
            c.wait_recv()
        ky[...] = total(jy[x], r2y, range(NX - 1))
        start_if(p3y)

    @pl.when(has_z)
    def _():
        for c in p2z:
            c.wait_recv()
        r3z[y] = total(jz[x], r2z, range(NX - 1))
        for c in y_copies(r3z, s3z, q3z):
            c.start()

    @pl.when(own_y)
    def _():
        for c, _ in p3y:
            c.wait_recv()
        fy[...] = total(ky[...], r3y, range(NZ - 1))
        for c in p4y:
            c.start()

    def sent_if(copies):
        for c, yes in copies:
            pl.when(yes)(c.wait_send)

    for c in sends:
        c.wait_send()
    sent_if(p1y + p1z + p2x)

    @pl.when(mid_y)
    def _():
        for c in p2y:
            c.wait_send()
        sent_if(p3y)

    @pl.when(has_z)
    def _():
        for c in p2z:
            c.wait_send()

    back.wait_recv()
    far = back_in[...].astype(F32).reshape(8, 8, D)
    br0 = branch[0].astype(F32).reshape(16, 8, D)
    new_lo = dyv[:, :8, :].astype(F32) + jnp.where(sub, unpaired(far, roll4(far)), br0)
    out_ref[...] = jnp.concatenate([new_lo, hi_out[...]], axis=1).astype(BF16)

    @pl.when(has_x)
    def _():
        for c in y_copies(r3x, s3x, q3x):
            c.wait_send()

    @pl.when(has_z)
    def _():
        for c in y_copies(r3z, s3z, q3z):
            c.wait_send()

    def settled(buf, ss, qs, holder):
        for c, other_core in y_arrivals(buf, ss, qs, holder):
            if other_core is None:
                c.wait_recv()
            else:
                pl.when(other_core)(c.wait_recv)
        t = buf[0].astype(F32)
        for i in range(1, NY):
            t = t + buf[i].astype(F32)
        return t

    pl.when(jnp.logical_not(own_y))(p4y[0].wait_recv)
    sum_x = settled(r3x, s3x, q3x, has_x)
    sum_z = settled(r3z, s3z, q3z, has_z)

    scale = 1.0 / math.sqrt(3 * 64 * 2 * NY * tiles)
    odd = (z % 2) == 1
    final = jnp.concatenate([sum_x, fy[...].astype(F32), sum_z], axis=1) * scale
    for g in range(GROUPS):
        f = final[:, D * g:D * g + D]
        top, bot = f[0:8], f[8:16]
        top_r, bot_r = pltpu.roll(top, 4, 0), pltpu.roll(bot, 4, 0)
        low = low4((8, D))
        first = jnp.where(odd, jnp.where(low, bot_r, top_r), top)
        rest = jnp.where(odd, top_r, bot)
        extra = jnp.where(odd, bot, bot_r)
        for s in range(3):
            lanes = slice(s * D + 128 * g, s * D + 128 * g + 128)
            gq_ref[0:8, lanes] = first[:, 128 * s:128 * s + 128]
            gq_ref[8:12, lanes] = rest[0:4, 128 * s:128 * s + 128]
        go_ref[4 * g:4 * g + 4, :] = extra[0:4]

    @pl.when(own_y)
    def _():
        for c in p4y:
            c.wait_send()


def hand_over(a, b, c, a_out, b_out, c_out, sems):
    copies = [
        pltpu.make_async_copy(src, dst, sems.at[i])
        for i, (src, dst) in enumerate(((a, a_out), (b, b_out), (c, c_out)))
    ]
    for c in copies:
        c.start()
    for c in copies:
        c.wait()


def body(tokens, grad_out, ocean_mask, w_qkv, w_out):
    any_spec = pl.BlockSpec(memory_space=pl.ANY)
    vmem_spec = pl.BlockSpec(memory_space=pltpu.VMEM)

    def buf(*shape, dtype=BF16):
        return pltpu.VMEM(shape, dtype)

    def sem(*shape):
        return pltpu.SemaphoreType.DMA(shape)

    results = pl.pallas_call(
        kernel,
        out_shape=(buf(16, 16, D), buf(12, 3 * D, dtype=F32), buf(12, D, dtype=F32)),
        in_specs=[any_spec] * 5,
        out_specs=(vmem_spec, vmem_spec, vmem_spec),
        scratch_shapes=[
            buf(16, 16, D), buf(16, 16, D), pltpu.SMEM((2, 2), jnp.int32),
            buf(D, 3 * D), buf(D, D),
            buf(2, 64, D), buf(2, 64, D), buf(64, D), buf(64, D),
            buf(2, 128, D, dtype=F32), buf(2, D, 128), buf(2, D, 128), buf(2, D, 128),
            buf(2, 128, 2 * D), buf(2, 128, D, dtype=F32), buf(2, 128, 128, dtype=F32),
            buf(2, 128, D), buf(2, 128, D), buf(16, 8, D, dtype=F32),
            buf(GROUPS, 16, 8, D, dtype=F32),
            buf(3, NX, 8, 16, D), buf(3, NX, 4, 16, D),
            buf(NX, 4, 16, D), buf(NX, 4, 16, D), buf(NX, 4, 16, D),
            buf(NX - 1, 4, 16, D), buf(NY - 1, NX, 16, D), buf(NZ - 1, NX, 16, D),
            buf(4, 16, D), buf(NX, 16, D), buf(NX, 16, D),
            buf(NZ - 1, 16, D), buf(NX - 1, 16, D), buf(NX - 1, 16, D),
            buf(NY, 16, D), buf(16, D), buf(NZ - 1, 16, D), buf(NY, 16, D),
            buf(16, D),
            sem(5), pltpu.SemaphoreType.REGULAR, pltpu.SemaphoreType.REGULAR, sem(2), sem(2), sem(2),
            sem(3), sem(3), sem(NX - 1), sem(NX - 1),
            sem(NY - 1), sem(NY - 1), sem(NZ - 1), sem(NZ - 1),
            sem(NZ - 1), sem(NZ - 1), sem(NX - 1), sem(NX - 1), sem(NX - 1), sem(NX - 1),
            sem(2 * NY - 1), sem(NY), sem(NZ - 1), sem(NZ - 1), sem(2 * NY - 1), sem(NY),
            sem(2 * NY - 1), pltpu.SemaphoreType.DMA,
        ],
        compiler_params=pltpu.CompilerParams(
            collective_id=0, has_side_effects=True, vmem_limit_bytes=56 * 1024 * 1024
        ),
        cost_estimate=pl.CostEstimate(
            flops=900_000_000, bytes_accessed=2_000_000, transcendentals=200_000
        ),
        name="window_grads",
    )(tokens, grad_out, ocean_mask, w_qkv, w_out)
    return pl.pallas_call(
        hand_over,
        out_shape=[jax.ShapeDtypeStruct(r.shape, r.dtype) for r in results],
        in_specs=[any_spec] * 3,
        out_specs=[any_spec] * 3,
        scratch_shapes=[sem(3)],
        compiler_params=pltpu.CompilerParams(vmem_limit_bytes=4 * 1024 * 1024),
        cost_estimate=pl.CostEstimate(flops=0, bytes_accessed=600_000, transcendentals=0),
        name="hand_over",
    )(*results)


def solution(mesh):
    return jax.shard_map(
        body,
        mesh=mesh,
        in_specs=(
            P("region", "tile", None),
            P("region", "tile", None),
            P("region", "tile"),
            P(),
            P(),
        ),
        out_specs=(P("region", "tile", None), P("tile", None), P("tile", None)),
        check_vma=False,
    )
```

```python
import math

import jax
import jax.numpy as jnp
from jax import lax
from jax.experimental import pallas as pl
from jax.experimental.pallas import tpu as pltpu
from jax.sharding import PartitionSpec as P

MESH = pl.DeviceIdType.MESH
F32 = jnp.float32
BF16 = jnp.bfloat16
D = 384
HD = 32
LOG2E = math.log2(math.e)
GROUPS = 3
NX, NZ, NY = 4, 8, 8
PY, PX, PZ = 0, 1, 2
FAR_FIRST = (4, 3, 5, 2, 6, 1, 7)
NT = (((1,), (1,)), ((), ()))


def dot(a, b, dims=(((1,), (0,)), ((), ()))):
    return lax.dot_general(a, b, dims, preferred_element_type=F32)


def roll4(a):
    n, _, width = a.shape
    return pltpu.roll(a.reshape(n * 8, width).reshape(n, 8, width), 4, 1)


def low4(shape):
    return lax.broadcasted_iota(jnp.int32, shape, len(shape) - 2) % 8 < 4


def part(array, a, first):
    return array[64 * a:64 * a + 64, first:first + 128]


def spread(array, a):
    lane_head = lax.broadcasted_iota(jnp.int32, (1, 128), 1) // HD
    order = (1, 0, 3, 2) if a else (0, 1, 2, 3)
    return jnp.concatenate(
        [array * (lane_head == h).astype(F32).astype(BF16) for h in order], axis=0
    )


def own(zero, one):
    first_half = lax.broadcasted_iota(jnp.int32, (1, 128), 1) < 64
    blocks = []
    for h in range(4):
        r, c = slice(32 * h, 32 * h + 32), slice(128 * (h // 2), 128 * (h // 2) + 128)
        if h % 2 == 0:
            blocks.append(jnp.where(first_half, zero[r, c], one[r, c]))
        else:
            blocks.append(pltpu.roll(jnp.where(first_half, one[r, c], zero[r, c]), 64, 1))
    return jnp.concatenate(blocks, axis=0).astype(BF16)


UNITS = [(a, g) for g in range(GROUPS) for a in range(2)]
ROOT = HD ** -0.5


def normalise(feats, normed_t, xhat, istd):
    center = jnp.mean(feats, axis=-1, keepdims=True)
    dev = feats - center
    inv = lax.rsqrt(jnp.mean(dev * dev, axis=-1, keepdims=True) + 1e-05)
    hat = dev * inv
    xhat[...] = hat
    istd[...] = jnp.broadcast_to(inv, (128, 128))
    nb = hat.astype(BF16)
    normed_t[...] = nb.T
    return nb


def scores(proj):
    q = [spread(part(proj, a, 128 * g), a) for a, g in UNITS]
    k = [part(proj, a, D + 128 * g) for a, g in UNITS]
    s = [dot(m, n, NT) for m, n in zip(k, q)]
    return q, [m.T for m in k], s


def softmax(s):
    p = []
    for t in s:
        e = jnp.exp2((t - jnp.max(t, axis=0, keepdims=True)) * (ROOT * LOG2E))
        p.append(e * (1.0 / jnp.sum(e, axis=0, keepdims=True)))
    return p


def grad_probs(proj, ga):
    o = [spread(part(ga, a, 128 * g), a) for a, g in UNITS]
    v = [part(proj, a, 2 * D + 128 * g) for a, g in UNITS]
    dp = [dot(m, n, NT) for m, n in zip(v, o)]
    return o, [m.T for m in v], dp


def grad_scores(p, dp):
    ds = []
    for t, d in zip(p, dp):
        row = jnp.sum(d * t, axis=0, keepdims=True)
        ds.append((t * ((d - row) * ROOT)).astype(BF16))
    return [t.astype(BF16) for t in p], ds


def products(q, o, kt, vt, pb, ds):
    qt = [dot(m, n) for m, n in zip(kt, ds)]
    dk = [dot(m, n) for m, n in zip(ds, q)]
    dv = [dot(m, n) for m, n in zip(pb, o)]
    ot = [dot(m, n) for m, n in zip(vt, pb)]
    return qt, dk, dv, ot


def keep_products(qt, dk, dv, ot, att_t, query_t, gp):
    for i, (a, g) in enumerate(UNITS):
        at_row = pl.ds(64 * a, 64)
        gp[at_row, 128 * g:128 * g + 128] = dk[i].astype(BF16)
        gp[at_row, D + 128 * g:D + 128 * g + 128] = dv[i].astype(BF16)
    for g in range(GROUPS):
        query_t[128 * g:128 * g + 128, :] = own(qt[2 * g], qt[2 * g + 1])
        att_t[128 * g:128 * g + 128, :] = own(ot[2 * g], ot[2 * g + 1])


def device():
    region, tile = lax.axis_index("region"), lax.axis_index("tile")
    tiles = NX * NZ
    west = {"region": region, "tile": (tile + tiles - 1) % tiles}
    east = {"region": region, "tile": (tile + 1) % tiles}
    return region, tile, west, east


def send(src, dst, ss, rs, dev):
    return pltpu.make_async_remote_copy(
        src_ref=src, dst_ref=dst, send_sem=ss, recv_sem=rs, device_id=dev, device_id_type=MESH,
    )


def greet(partners):
    barrier = pltpu.get_barrier_semaphore()
    for dev in partners:
        pl.semaphore_signal(barrier, inc=1, device_id=dev, device_id_type=MESH)
    return lambda: pl.semaphore_wait(barrier, len(partners))


def pairs(v):
    v = v.reshape(8, 2, 8, D)
    return v[:, 0], v[:, 1]


def kernel(
    x_hbm, dy_hbm, mask_hbm, wq_hbm, wo_hbm,
    out_ref, gq_ref, go_ref,
    xv, dyv, mask_ref, wq, wo,
    rim_out, rim_in, back_out, back_in,
    feats, normed_t, att_t, query_t, gp, xhat, istd, masked, branch, hi_out, spare,
    grads, r0, hx, hy, hz, r1x, r1y, r1z, jx, jy, jz,
    r2x, r2y, r2z, r3x, ky, r3y, r3z, fx, fy, fz,
    in_sem, two_away, four_away, rim_send, rim_recv, back_sem,
    s0, q0, s1x, q1x, s1y, q1y, s1z, q1z, s2x, q2x, s2y, q2y, s2z, q2z,
    s3x, q3x, s3y, q3y, s3z, q3z, s4y, q4y, s5, q5,
):
    loads = [
        pltpu.make_async_copy(src, dst, in_sem.at[i])
        for i, (src, dst) in enumerate(
            ((x_hbm, xv), (dy_hbm, dyv), (wq_hbm, wq), (wo_hbm, wo), (mask_hbm, mask_ref))
        )
    ]
    for c in loads[:2]:
        c.start()
    region, tile, west, east = device()
    y, core = region // 2, region % 2
    x, z = tile // NZ, tile % NZ
    tiles = NX * NZ

    def at(ax, ay, az, ac):
        return {"region": ay * 2 + ac, "tile": ax * NZ + az}

    other = at(x, y, z, 1 - core)
    by_x = [at((x + k) % NX, y, z, core) for k in range(1, NX)]
    by_z = [at(x, y, (z + k) % NZ, core) for k in range(1, NZ)]
    by_y = [at(x, (y + k) % NY, z, core) for k in range(1, NY)]
    near = [by_x[0], by_x[2], by_y[0], by_y[6], by_z[0], by_z[6]]
    greeted = greet([west, east, other] + near)
    for c in loads[2:]:
        c.start()
    sub = low4((1, 8, D))

    def halves(ref):
        v = ref[...].astype(F32)
        return v[:, :8, :], v[:, 8:, :]

    def rim_of(lo):
        even, odd = pairs(lo)
        return jnp.where(sub, even, roll4(odd)).reshape(64, D).astype(BF16)

    rims = [
        send(rim_out.at[i], rim_in.at[i], rim_send.at[i], rim_recv.at[i], west) for i in range(2)
    ]
    loads[0].wait()
    x_lo, x_hi = halves(xv)
    rim_out[0] = rim_of(x_lo)
    greeted()
    rims[0].start()
    for dev in near:
        pl.semaphore_signal(two_away, inc=1, device_id=dev, device_id_type=MESH)
    loads[1].wait()
    dy_lo, dy_hi = halves(dyv)
    rim_out[1] = rim_of(dy_lo)
    rims[1].start()

    for c in loads[2:]:
        c.wait()

    def mask_of(dys, b):
        flag = [mask_ref[a, b].astype(F32) for a in range(2)]
        return jnp.concatenate([dys[:64] * flag[0], dys[64:] * flag[1]], axis=0).astype(BF16)

    def joined(hi, far):
        even, odd = pairs(hi.astype(F32))
        loc = jnp.where(sub, roll4(even), odd).reshape(64, D)
        far = far.astype(F32)
        return jnp.concatenate([loc[:32], far[:32], loc[32:], far[32:]], axis=0)

    feats[0] = jnp.where(sub, x_hi, x_lo).reshape(128, D)
    masked[0] = mask_of(jnp.where(sub, dy_hi, dy_lo).reshape(128, D), 0)
    far = [by_y[1], by_y[5], by_z[1], by_z[5]]

    def column(b, _):
        @pl.when(b == 1)
        def _():
            pl.semaphore_wait(two_away, len(near))
            for dev in far:
                pl.semaphore_signal(four_away, inc=1, device_id=dev, device_id_type=MESH)
            rims[0].wait()
            feats[1] = joined(xv[:, 8:, :], rim_in[0])

        nb = normalise(feats[b], normed_t.at[b], xhat.at[b], istd.at[b])
        proj = dot(nb, wq[...]).astype(BF16)
        q, kt, sc = scores(proj)
        p = softmax(sc)

        @pl.when(b == 1)
        def _():
            rims[1].wait()
            masked[1] = mask_of(joined(dyv[:, 8:, :], rim_in[1]), 1)

        ga = dot(masked[b], wo[...], NT).astype(BF16)
        o, vt, dp = grad_probs(proj, ga)
        pb, ds = grad_scores(p, dp)
        keep_products(
            *products(q, o, kt, vt, pb, ds), att_t.at[b], query_t.at[b], gp.at[b]
        )
        return 0

    lax.fori_loop(0, 2, column, 0)

    def both(a, b, axis):
        return jnp.concatenate([a, b], axis=axis)

    nt = both(normed_t[0], normed_t[1], 1)
    ga_full = dot(both(att_t[0], att_t[1], 1), both(masked[0], masked[1], 0)).reshape(16, 3, 8, D)
    w0, w1, w2 = ga_full[:, 0], ga_full[:, 1], ga_full[:, 2]
    spare[0] = roll4(jnp.where(sub, w0, w1))
    spare[1] = jnp.where(sub, w2, w0)
    spare[2] = roll4(jnp.where(sub, w1, w2))
    sends = []

    def start(c):
        c.start()
        sends.append(c)
        return c

    keep = {PX: core, PY: 1 - core, PZ: 1 - core}
    pl.semaphore_wait(four_away, len(far))

    def swap(g, half):
        return send(grads.at[g, :, pl.ds(half * 4, 4)], r0.at[g], s0.at[g], q0.at[g], other)

    def gradients(g, _):
        at_g = pl.ds(pl.multiple_of(128 * g, 128), 128)
        at_gv = pl.ds(pl.multiple_of(D + 128 * g, 128), 128)
        gn = jnp.concatenate([
            dot(nt, both(query_t[0, at_g, :], query_t[1, at_g, :], 1), NT),
            dot(nt, both(gp[0, :, at_g], gp[1, :, at_g], 0)),
            dot(nt, both(gp[0, :, at_gv], gp[1, :, at_gv], 0)),
        ], axis=1).reshape(16, 3, 8, D)
        v0, v1, v2, extra = gn[:, 0], gn[:, 1], gn[:, 2], spare[g]
        packed = jnp.stack(
            [v0, jnp.where(sub, v1, extra), v2, jnp.where(sub, extra, v1)], axis=1
        ).reshape(NX, NZ, 16, D).astype(BF16)
        grads[g] = packed
        swap(g, jnp.where(g == PX, 1 - core, core)).start()
        return 0

    lax.fori_loop(0, GROUPS, gradients, 0)
    core0 = [swap(g, 1 - keep[g]) for g in range(GROUPS)]
    sends += core0

    def start_if(copies):
        for c, yes in copies:
            pl.when(yes)(c.start)

    def combined(part):
        core0[part].wait_recv()
        mine = grads[part, :, pl.ds(keep[part] * 4, 4)].astype(F32)
        return (mine + r0[part].astype(F32)).astype(BF16)

    def around(buf, slots, ss, qs, devs, place, half):
        out = []
        for k in FAR_FIRST:
            to = (place + k) % 8
            c = send(buf.at[:, to % 4], slots.at[k - 1], ss.at[k - 1], qs.at[k - 1], devs[k - 1])
            out.append((c, to // 4 == half))
        return out

    p1y = around(hy, r1y, s1y, q1y, by_y, y, keep[PY])
    p1z = around(hz, r1z, s1z, q1z, by_z, z, keep[PZ])
    hy[...] = combined(PY)
    start_if(p1y)
    hx[...] = combined(PX)
    p1x = [
        start(send(hx.at[(x + k) % NX], r1x.at[k - 1], s1x.at[k - 1], q1x.at[k - 1], by_x[k - 1]))
        for k in (2, 1, 3)
    ]
    hz[...] = combined(PZ)
    start_if(p1z)

    def branch_of(b, _):
        gn = dot(query_t[b].T, wq[:, 0:D], NT) + dot(gp[b], wq[:, D:3 * D], NT)
        hat = xhat[b]
        m0 = jnp.mean(gn, axis=-1, keepdims=True)
        m1 = jnp.mean(gn * hat, axis=-1, keepdims=True)
        branch[b] = (istd[b][:, 0:1] * (gn - m0 - hat * m1)).astype(BF16)
        return 0

    lax.fori_loop(0, 2, branch_of, 0)
    back_out[0:32, :] = branch[1, 32:64, :]
    back_out[32:64, :] = branch[1, 96:128, :]
    loc = both(branch[1, 0:32, :], branch[1, 64:96, :], 0).astype(F32).reshape(8, 8, D)

    def unpaired(even, odd):
        return jnp.stack([even, odd], axis=1).reshape(16, 8, D)

    br0 = branch[0].astype(F32).reshape(16, 8, D)
    hi_out[...] = dyv[:, 8:, :].astype(F32) + jnp.where(sub, br0, unpaired(roll4(loc), loc))

    has_x = z // 4 == core
    has_z = z // 4 != core
    mid_y = y // 4 != core

    def total(first, buf, slots):
        t = first.astype(F32)
        for i in slots:
            t = t + buf[i].astype(F32)
        return t.astype(BF16)

    def over_x(buf, slots, ss, qs):
        return [
            send(buf.at[(x + k) % NX], slots.at[k - 1], ss.at[k - 1], qs.at[k - 1], by_x[k - 1])
            for k in (2, 1, 3)
        ]

    def over_z(buf, slots, ss, qs):
        out = []
        for k in FAR_FIRST:
            to = (z + k) % NZ
            c = send(buf.at[to % 4], slots.at[k - 1], ss.at[k - 1], qs.at[k - 1], by_z[k - 1])
            out.append((c, to // 4 == core))
        return out

    p2y = over_x(jy, r2y, s2y, q2y)
    p2x = over_z(jx, r2x, s2x, q2x)
    p2z = over_x(jz, r2z, s2z, q2z)
    for c in p1x:
        c.wait_recv()
    jx[...] = total(hx[x], r1x, range(NX - 1))
    start_if(p2x)

    @pl.when(has_z)
    def _():
        for c, _ in p1z:
            c.wait_recv()
        jz[...] = total(hz[:, z % 4], r1z, range(NZ - 1))
        for c in p2z:
            c.start()

    @pl.when(mid_y)
    def _():
        for c, _ in p1y:
            c.wait_recv()
        jy[...] = total(hy[:, y % 4], r1y, range(NY - 1))
        for c in p2y:
            c.start()

    back = start(send(back_out, back_in, back_sem.at[0], back_sem.at[1], east))

    def y_copies(buf, ss, qs):
        return [
            send(buf.at[y], buf.at[y], ss.at[k - 1], qs.at[y], by_y[k - 1])
            for k in FAR_FIRST
        ]

    def y_arrivals(buf, ss, qs):
        return [
            send(buf.at[y], buf.at[(y + k) % NY], ss.at[k - 1], qs.at[(y + k) % NY], by_y[k - 1])
            for k in range(1, NY)
        ]

    own_y = jnp.logical_and(has_z, y == z)
    p3y = [
        (send(ky, r3y.at[k - 1], s3y.at[k - 1], q3y.at[k - 1], by_z[k - 1]), (z + k) % NZ == y)
        for k in range(1, NZ)
    ]
    bands = 2 * NY
    p4y = [
        send(fy, fy, s4y.at[k - 1], q4y, {"region": (region + k) % bands, "tile": tile})
        for k in (8, 7, 9, 6, 10, 5, 11, 4, 12, 3, 13, 2, 14, 1, 15)
    ]

    @pl.when(has_x)
    def _():
        for c, _ in p2x:
            c.wait_recv()
        r3x[y] = total(jx[z % 4], r2x, range(NZ - 1))
        for c in y_copies(r3x, s3x, q3x):
            c.start()

    @pl.when(has_z)
    def _():
        for c in p2z:
            c.wait_recv()
        r3z[y] = total(jz[x], r2z, range(NX - 1))
        for c in y_copies(r3z, s3z, q3z):
            c.start()

    @pl.when(mid_y)
    def _():
        for c in p2y:
            c.wait_recv()
        ky[...] = total(jy[x], r2y, range(NX - 1))
        start_if(p3y)

    @pl.when(own_y)
    def _():
        for c, _ in p3y:
            c.wait_recv()
        fy[...] = total(ky[...], r3y, range(NZ - 1))
        for c in p4y:
            c.start()

    def sent_if(copies):
        for c, yes in copies:
            pl.when(yes)(c.wait_send)

    for c in sends:
        c.wait_send()
    sent_if(p1y + p1z + p2x)

    @pl.when(mid_y)
    def _():
        for c in p2y:
            c.wait_send()
        sent_if(p3y)

    @pl.when(has_z)
    def _():
        for c in p2z:
            c.wait_send()

    back.wait_recv()
    far = back_in[...].astype(F32).reshape(8, 8, D)
    br0 = branch[0].astype(F32).reshape(16, 8, D)
    new_lo = dyv[:, :8, :].astype(F32) + jnp.where(sub, unpaired(far, roll4(far)), br0)
    out_ref[...] = jnp.concatenate([new_lo, hi_out[...]], axis=1).astype(BF16)

    @pl.when(has_x)
    def _():
        for c in y_copies(r3x, s3x, q3x):
            c.wait_send()

    @pl.when(has_z)
    def _():
        for c in y_copies(r3z, s3z, q3z):
            c.wait_send()

    last_x = send(fx, fx, s5.at[0], q5.at[0], other)
    last_z = send(fz, fz, s5.at[1], q5.at[1], other)

    def settle(buf, out, ss, qs, last):
        for c in y_arrivals(buf, ss, qs):
            c.wait_recv()
        out[...] = total(buf[0], buf, range(1, NY))
        last.start()

    @pl.when(has_x)
    def _():
        settle(r3x, fx, s3x, q3x, last_x)

    @pl.when(has_z)
    def _():
        settle(r3z, fz, s3z, q3z, last_z)

    @pl.when(jnp.logical_not(has_x))
    def _():
        last_x.wait_recv()

    @pl.when(jnp.logical_not(has_z))
    def _():
        last_z.wait_recv()

    pl.when(jnp.logical_not(own_y))(p4y[0].wait_recv)

    scale = 1.0 / math.sqrt(3 * 64 * 2 * NY * tiles)
    odd = (z % 2) == 1
    final = jnp.concatenate([fy[...], fx[...], fz[...]], axis=1).astype(F32) * scale
    for g in range(GROUPS):
        f = final[:, D * g:D * g + D]
        top, bot = f[0:8], f[8:16]
        top_r, bot_r = pltpu.roll(top, 4, 0), pltpu.roll(bot, 4, 0)
        low = low4((8, D))
        first = jnp.where(odd, jnp.where(low, bot_r, top_r), top)
        rest = jnp.where(odd, top_r, bot)
        extra = jnp.where(odd, bot, bot_r)
        for s in range(3):
            lanes = slice(s * D + 128 * g, s * D + 128 * g + 128)
            gq_ref[0:8, lanes] = first[:, 128 * s:128 * s + 128]
            gq_ref[8:12, lanes] = rest[0:4, 128 * s:128 * s + 128]
        go_ref[4 * g:4 * g + 4, :] = extra[0:4]

    @pl.when(own_y)
    def _():
        for c in p4y:
            c.wait_send()

    pl.when(has_x)(last_x.wait_send)
    pl.when(has_z)(last_z.wait_send)


def hand_over(a, b, c, a_out, b_out, c_out, sems):
    copies = [
        pltpu.make_async_copy(src, dst, sems.at[i])
        for i, (src, dst) in enumerate(((a, a_out), (b, b_out), (c, c_out)))
    ]
    for c in copies:
        c.start()
    for c in copies:
        c.wait()


def body(tokens, grad_out, ocean_mask, w_qkv, w_out):
    any_spec = pl.BlockSpec(memory_space=pl.ANY)
    vmem_spec = pl.BlockSpec(memory_space=pltpu.VMEM)

    def buf(*shape, dtype=BF16):
        return pltpu.VMEM(shape, dtype)

    def sem(*shape):
        return pltpu.SemaphoreType.DMA(shape)

    results = pl.pallas_call(
        kernel,
        out_shape=(buf(16, 16, D), buf(12, 3 * D, dtype=F32), buf(12, D, dtype=F32)),
        in_specs=[any_spec] * 5,
        out_specs=(vmem_spec, vmem_spec, vmem_spec),
        scratch_shapes=[
            buf(16, 16, D), buf(16, 16, D), pltpu.SMEM((2, 2), jnp.int32),
            buf(D, 3 * D), buf(D, D),
            buf(2, 64, D), buf(2, 64, D), buf(64, D), buf(64, D),
            buf(2, 128, D, dtype=F32), buf(2, D, 128), buf(2, D, 128), buf(2, D, 128),
            buf(2, 128, 2 * D), buf(2, 128, D, dtype=F32), buf(2, 128, 128, dtype=F32),
            buf(2, 128, D), buf(2, 128, D), buf(16, 8, D, dtype=F32),
            buf(GROUPS, 16, 8, D, dtype=F32),
            buf(3, NX, 8, 16, D), buf(3, NX, 4, 16, D),
            buf(NX, 4, 16, D), buf(NX, 4, 16, D), buf(NX, 4, 16, D),
            buf(NX - 1, 4, 16, D), buf(NY - 1, NX, 16, D), buf(NZ - 1, NX, 16, D),
            buf(4, 16, D), buf(NX, 16, D), buf(NX, 16, D),
            buf(NZ - 1, 16, D), buf(NX - 1, 16, D), buf(NX - 1, 16, D),
            buf(NY, 16, D), buf(16, D), buf(NZ - 1, 16, D), buf(NY, 16, D),
            buf(16, D), buf(16, D), buf(16, D),
            sem(5), pltpu.SemaphoreType.REGULAR, pltpu.SemaphoreType.REGULAR, sem(2), sem(2), sem(2),
            sem(3), sem(3), sem(NX - 1), sem(NX - 1),
            sem(NY - 1), sem(NY - 1), sem(NZ - 1), sem(NZ - 1),
            sem(NZ - 1), sem(NZ - 1), sem(NX - 1), sem(NX - 1), sem(NX - 1), sem(NX - 1),
            sem(NY - 1), sem(NY), sem(NZ - 1), sem(NZ - 1), sem(NY - 1), sem(NY),
            sem(2 * NY - 1), pltpu.SemaphoreType.DMA, sem(2), sem(2),
        ],
        compiler_params=pltpu.CompilerParams(
            collective_id=0, has_side_effects=True, vmem_limit_bytes=56 * 1024 * 1024
        ),
        cost_estimate=pl.CostEstimate(
            flops=900_000_000, bytes_accessed=2_000_000, transcendentals=200_000
        ),
        name="window_grads",
    )(tokens, grad_out, ocean_mask, w_qkv, w_out)
    return pl.pallas_call(
        hand_over,
        out_shape=[jax.ShapeDtypeStruct(r.shape, r.dtype) for r in results],
        in_specs=[any_spec] * 3,
        out_specs=[any_spec] * 3,
        scratch_shapes=[sem(3)],
        compiler_params=pltpu.CompilerParams(vmem_limit_bytes=4 * 1024 * 1024),
        cost_estimate=pl.CostEstimate(flops=0, bytes_accessed=600_000, transcendentals=0),
        name="hand_over",
    )(*results)


def solution(mesh):
    return jax.shard_map(
        body,
        mesh=mesh,
        in_specs=(
            P("region", "tile", None),
            P("region", "tile", None),
            P("region", "tile"),
            P(),
            P(),
        ),
        out_specs=(P("region", "tile", None), P("tile", None), P("tile", None)),
        check_vma=False,
    )
```
